256 devices in a mesh: sect: 2 (over y_hi), gx: 16 (over x, y_lo, core), yz: 8 (over z).
Axes of the slice: x: 4, y: 4 (y_hi: 2, y_lo: 2; y = y_hi * 2 + y_lo), z: 8, core: 2. Of those that a mesh axis runs over, the one named last changes fastest.
Arguments:
- fields: float32 [2, 5, 128, 32768], P('sect', None, 'gx', 'yz'), may hold values from -6 to 6
- jacobians: float32 [3, 5, 5], replicated, may hold values from -2.5 to 2.5
- inflow_map: int32 [128], P('yz'), may hold values from 0 to 127
- donor_tiles: int32 [2, 16, 8, 64, 3], P('sect', 'gx', 'yz'), may hold values from 0 to 247, as said below
- receptor_tiles: int32 [2, 16, 8, 64], P('sect', 'gx', 'yz'), may hold values from 0 to 64, as said below
Outputs:
- segment_fields: float32 [2, 5, 128, 32768], P('sect', None, 'gx', 'yz')
The draws below stay inside these ranges and needn't reach their ends.
Inputs may be any that keep to these rules, and one draw needn't show every extreme that they name: `donor_tiles`: each row holds a tile index along x below 1, a tile index along y below 2, and a first z cell. `receptor_tiles`: entry s * 4 + m names the tile of the receiving block that takes slot m from block s along gx; 64 marks an empty slot. In every group along gx some block has all slots live.
All inputs are finite; a program needn't handle non-finite values.
Results may differ from the reference program's by a relative error of at most 0.0003.
Values sent between devices are 32-bit elements; how exact they have to be, the bound alone decides.
A program may use at most 128 MiB of HBM per device.

```python
import jax
import jax.numpy as jnp
import numpy as np
from jax import lax

CX = 8
CY = 16
CZ = 256
CAP = 4
SLOTS = 64
TILES = 64
NX = 128
NY = 128
NYZ = 32768
N_GX = 16
N_YZ = 8


def draw_donor_tiles(key, part):
    key = jax.random.fold_in(key, 11)
    upper = jnp.array([CX // 8, CY // 8, CZ - 8], jnp.int32)
    picks = jax.random.randint(key, (2, N_GX, N_YZ, SLOTS, 3), 0, upper)
    picks = picks.at[0, 0, 0, 0, 2].set(CZ - 9)
    picks = picks.at[0, 0, 0, 1, 2].set(0)
    return picks.astype(jnp.int32)


def draw_receptor_tiles(key, part):
    key = jax.random.fold_in(key, 23)
    key_dest, key_rank, key_fill, key_full = jax.random.split(key, 4)
    shape = (2, N_GX, N_YZ, SLOTS)
    destinations = jax.random.randint(key_dest, shape, 0, TILES)
    destinations = destinations.at[0, 0, 0, 0].set(0)
    scores = jax.random.randint(key_rank, shape, 0, 2 ** 20) * SLOTS + jnp.arange(SLOTS, dtype=jnp.int32)
    scores = scores.at[0, 0, 0, 0].set(-1)
    ranks = jnp.argsort(jnp.argsort(scores, axis=-1), axis=-1)
    live_count = jax.random.randint(key_fill, (2, N_GX, N_YZ, 1), SLOTS // 8, SLOTS // 2)
    full_index = jax.random.randint(key_full, (2, 1, N_YZ, 1), 0, N_GX)
    is_full = jnp.arange(N_GX, dtype=jnp.int32)[None, :, None, None] == full_index
    live_count = jnp.where(is_full, SLOTS, live_count)
    return jnp.where(ranks < live_count, destinations, TILES).astype(jnp.int32)


def set_ends(values, rng, least, high):
    longest = values.shape.index(max(values.shape))
    spots = []
    for shift in (0, 1):
        where = [jax.random.randint(jax.random.fold_in(rng, axis), (), 0, length) for axis, length in enumerate(values.shape)]
        where[longest] = (where[longest] + shift) % values.shape[longest]
        spots.append(tuple(where))
    return values.at[spots[0]].set(least).at[spots[1]].set(high)


def shard_levels(key, extent, cuts, low, largest):
    factor_of = 1.0
    for dim, shards_of in cuts:
        draws = jax.random.uniform(jax.random.fold_in(jax.random.fold_in(key, 6), dim), (shards_of,), jnp.float32, low / len(cuts), largest / len(cuts))
        factor_of = factor_of * jnp.repeat(jnp.exp(draws), extent[dim] // shards_of).reshape((-1,) + (1,) * (len(extent) - 1 - dim))
    return factor_of


def noise(key, shape, width, limit, cuts=(), kind=jnp.bfloat16):
    entries = width * jax.random.normal(key, shape, jnp.float32)
    if cuts:
        entries = entries * shard_levels(key, shape, cuts, -0.22, 0.18)
    return jnp.clip(entries, -limit, limit).astype(kind)


def setup_inputs(seed: int = 0) -> dict:
    splits = jax.random.split(jax.random.key(seed), 6)
    fields = noise(splits[0], (2, 5, NX, NYZ), 1.0, 6.0, ((0, 2), (2, 16), (3, 8)), jnp.float32)
    jacobians = noise(splits[1], (3, 5, 5), 5 ** -0.5, 2.5, (), jnp.float32)
    inflow_map = set_ends(jax.random.randint(splits[2], (NY,), 0, NY), jax.random.fold_in(splits[2], 1), 0, NY - 1).astype(jnp.int32)
    donor_tiles = draw_donor_tiles(jax.random.fold_in(splits[5], 71), 0)
    receptor_tiles = draw_receptor_tiles(jax.random.fold_in(splits[5], 71), 0)
    return dict(fields=fields, jacobians=jacobians, inflow_map=inflow_map, donor_tiles=donor_tiles, receptor_tiles=receptor_tiles)


SEGMENT_STEP = 0.25
SIDE_DERIV = 1.0 / 3.0
SIDE_FILTER = 0.49
HIGHEST = lax.Precision.HIGHEST


def eliminate(left_side, right_side):
    matrix = left_side.copy()
    result = right_side.copy()
    length = matrix.shape[0]
    for pivot_row in range(length):
        pivot = matrix[pivot_row, pivot_row]
        matrix[pivot_row] = matrix[pivot_row] / pivot
        result[pivot_row] = result[pivot_row] / pivot
        factors = matrix[:, pivot_row].copy()
        factors[pivot_row] = 0.0
        matrix = matrix - np.outer(factors, matrix[pivot_row])
        result = result - np.outer(factors, result[pivot_row])
    return result


def band_table(length, periodic, stencil, side_weight):
    left_side = np.eye(length)
    right_side = np.zeros((length, length))
    for row_index in range(length):
        for offset in (-1, 1):
            col_index = row_index + offset
            if periodic:
                left_side[row_index, col_index % length] += side_weight
            elif 0 <= col_index < length:
                left_side[row_index, col_index] += side_weight
        for offset, factor in stencil:
            col_index = row_index + offset
            if periodic:
                right_side[row_index, col_index % length] += factor
            elif 0 <= col_index < length:
                right_side[row_index, col_index] += factor
    return eliminate(left_side, right_side).astype(np.float32)


def derivative_table(length, periodic):
    stencil = ((1, 7.0 / 9.0), (-1, -7.0 / 9.0), (2, 1.0 / 36.0), (-2, -1.0 / 36.0))
    return band_table(length, periodic, stencil, SIDE_DERIV)


def filter_table(length, periodic):
    side = SIDE_FILTER
    coeffs = [(193 + 126 * side) / 256, (105 + 302 * side) / 256, 15 * (-1 + 2 * side) / 64,
              45 * (1 - 2 * side) / 512, 5 * (-1 + 2 * side) / 256, (1 - 2 * side) / 512]
    stencil = [(0, coeffs[0])]
    for reach in range(1, 6):
        stencil.append((reach, coeffs[reach] / 2))
        stencil.append((-reach, coeffs[reach] / 2))
    return band_table(length, periodic, stencil, side)


def extract_tiles(cube, donors):
    def extract(donor_entry):
        window = lax.dynamic_slice(cube, (jnp.int32(0), donor_entry[0] * 8, donor_entry[1] * 8, donor_entry[2]), (5, 8, 8, 9))
        return (0.5 * (window[..., :-1] + window[..., 1:])).reshape(5 * 512)
    return jax.vmap(extract)(donors)


def place_tiles(cube, received, targets):
    cells_x, cells_y, depth = cube.shape[1], cube.shape[2], cube.shape[3]
    tile_count = (cells_x // 8) * (cells_y // 8) * (depth // 8)
    tiles_flat = cube.reshape(5, cells_x // 8, 8, cells_y // 8, 8, depth // 8, 8).transpose(1, 3, 5, 0, 2, 4, 6).reshape(tile_count, 5 * 512)
    onehot = (targets[:, None] == jnp.arange(tile_count, dtype=jnp.int32)[None, :]).astype(jnp.float32)
    totals = jnp.dot(onehot.T, received, precision=HIGHEST)
    hits = jnp.sum(onehot, axis=0)[:, None]
    replaced = jnp.where(hits > 0, totals / jnp.maximum(hits, 1.0), tiles_flat)
    return replaced.reshape(cells_x // 8, cells_y // 8, depth // 8, 5, 8, 8, 8).transpose(3, 0, 4, 1, 5, 2, 6).reshape(5, cells_x, cells_y, depth)


def reference(fields, jacobians, inflow_map, donor_tiles, receptor_tiles):
    outlet = fields[0, :, CX - 1, :].reshape(5, NY, CZ)
    selector = (inflow_map[:, None] == jnp.arange(NY, dtype=jnp.int32)[None, :]).astype(jnp.float32)
    mapped = jnp.einsum("yn,fnz->fyz", selector, outlet, precision=HIGHEST).reshape(5, NY * CZ)
    state = fields.at[1, :, 0, :].set(mapped)
    blocks = state.reshape(2, 5, N_GX, CX, N_YZ, CY, CZ).transpose(0, 2, 4, 1, 3, 5, 6)
    payload = jax.vmap(jax.vmap(jax.vmap(extract_tiles)))(blocks, donor_tiles)
    received = payload.reshape(2, N_GX, N_YZ, N_GX, CAP, 5 * 512).transpose(0, 3, 2, 1, 4, 5).reshape(2, N_GX, N_YZ, SLOTS, 5 * 512)
    placed = jax.vmap(jax.vmap(jax.vmap(place_tiles)))(blocks, received, receptor_tiles)
    fringed = placed.transpose(0, 3, 1, 4, 2, 5, 6).reshape(2, 5, NX, NY, CZ)
    deriv_x = jnp.stack([jnp.asarray(derivative_table(NX, True)), jnp.asarray(derivative_table(NX, False))])
    filter_x = jnp.stack([jnp.asarray(filter_table(NX, True)), jnp.asarray(filter_table(NX, False))])
    x_deriv = jnp.einsum("cab,cfbyz->cfayz", deriv_x, fringed, precision=HIGHEST)
    y_deriv = jnp.einsum("ab,cfxbz->cfxaz", jnp.asarray(derivative_table(NY, False)), fringed, precision=HIGHEST)
    z_deriv = jnp.einsum("ab,cfxyb->cfxya", jnp.asarray(derivative_table(CZ, True)), fringed, precision=HIGHEST)
    rate = -(jnp.einsum("fh,ch...->cf...", jacobians[0], x_deriv, precision=HIGHEST)
             + jnp.einsum("fh,ch...->cf...", jacobians[1], y_deriv, precision=HIGHEST)
             + jnp.einsum("fh,ch...->cf...", jacobians[2], z_deriv, precision=HIGHEST))
    update = fringed + SEGMENT_STEP * rate
    smooth = jnp.einsum("ab,cfxyb->cfxya", jnp.asarray(filter_table(CZ, True)), update, precision=HIGHEST)
    smooth = jnp.einsum("ab,cfxbz->cfxaz", jnp.asarray(filter_table(NY, False)), smooth, precision=HIGHEST)
    smooth = jnp.einsum("cab,cfbyz->cfayz", filter_x, smooth, precision=HIGHEST)
    return smooth.reshape(2, 5, NX, NYZ)
```

```python
import functools

import jax
import jax.numpy as jnp
import ml_dtypes
import numpy as np
from jax import lax
from jax.experimental import pallas as pl
from jax.experimental.pallas import tpu as pltpu
from jax.sharding import PartitionSpec as P

MESH = pl.DeviceIdType.MESH
F32 = jnp.float32
BF16 = jnp.bfloat16

CX = 8
CY = 16
CZ = 256
NG = 16
NK = 8
NX = 128
NY = 128
SLOTS = 64

SEGMENT_STEP = 0.25
SIDE_DERIV = 1.0 / 3.0
SIDE_FILTER = 0.49


def filter_coeffs():
    side = SIDE_FILTER
    return [
        (193 + 126 * side) / 256,
        (105 + 302 * side) / 256,
        15 * (-1 + 2 * side) / 64,
        45 * (1 - 2 * side) / 512,
        5 * (-1 + 2 * side) / 256,
        (1 - 2 * side) / 512,
    ]


DERIV_STENCIL = ((1, 7.0 / 9.0), (-1, -7.0 / 9.0), (2, 1.0 / 36.0), (-2, -1.0 / 36.0))
FILTER_STENCIL = ((0, filter_coeffs()[0]),) + tuple(
    (sign * reach, filter_coeffs()[reach] / 2) for reach in range(1, 6) for sign in (1, -1)
)


def sides(length, periodic, stencil, side):
    left = np.eye(length)
    right = np.zeros((length, length))
    for row in range(length):
        for offset, factor in ((-1, side), (1, side)):
            if periodic or 0 <= row + offset < length:
                left[row, (row + offset) % length] += factor
        for offset, factor in stencil:
            if periodic or 0 <= row + offset < length:
                right[row, (row + offset) % length] += factor
    return left, right


def line_matrix(length, periodic, stencil, side):
    return np.linalg.solve(*sides(length, periodic, stencil, side))


def halves(matrix):
    value = np.asarray(matrix, np.float32)
    high = value.astype(ml_dtypes.bfloat16)
    low = (value - high.astype(np.float32)).astype(ml_dtypes.bfloat16)
    return np.stack([high, low])


def block_table(stencil, side):
    left, right = sides(NY, False, stencil, side)
    reach = max(offset for offset, _ in stencil)
    below = np.zeros((NK, NY))
    above = np.zeros((NK, NY))
    corner_low = np.zeros(NK)
    corner_high = np.zeros(NK)
    for d in range(NK):
        lo, hi = d * CY, (d + 1) * CY
        if d > 0:
            row = np.linalg.solve(left[:lo, :lo].T, np.eye(lo)[lo - 1])
            below[d] = -side * (row @ right[:lo])
            corner_low[d] = row[-1]
        if d < NK - 1:
            row = np.linalg.solve(left[hi:, hi:].T, np.eye(NY - hi)[0])
            above[d] = -side * (row @ right[hi:])
            corner_high[d] = row[0]
    send_up = np.zeros((NK, CY))
    send_down = np.zeros((NK, CY))
    for s in range(NK):
        cells = slice(s * CY, (s + 1) * CY)
        if s < NK - 1:
            value = below[min(s + 2, NK - 1)][cells]
            send_up[s] = value / np.abs(value).max()
        if s > 0:
            value = above[max(s - 2, 0)][cells]
            send_down[s] = value / np.abs(value).max()
    take_low = np.zeros((NK, NK))
    take_high = np.zeros((NK, NK))
    near_low = np.zeros((NK, reach))
    near_high = np.zeros((NK, reach))
    own_low = np.zeros((NK, reach))
    own_high = np.zeros((NK, reach))
    for d in range(NK):
        for s in range(d):
            value, unit = below[d][s * CY : (s + 1) * CY], send_up[s]
            core = unit[: CY - reach]
            take_low[d, s] = (value[: CY - reach] @ core) / (core @ core)
            if s == d - 1:
                near_low[d] = (value - take_low[d, s] * unit)[CY - reach :]
        for s in range(d + 1, NK):
            value, unit = above[d][s * CY : (s + 1) * CY], send_down[s]
            core = unit[reach:]
            take_high[d, s] = (value[reach:] @ core) / (core @ core)
            if s == d + 1:
                near_high[d] = (value - take_high[d, s] * unit)[:reach]
        own_low[d] = below[d][d * CY : d * CY + reach]
        own_high[d] = above[d][(d + 1) * CY - reach : (d + 1) * CY]
    lower = np.zeros((NK, CY))
    inverse = np.zeros((NK, CY))
    for d in range(NK):
        diagonal = np.ones(CY)
        diagonal[0] -= side**2 * corner_low[d]
        diagonal[-1] -= side**2 * corner_high[d]
        inverse[d, 0] = 1 / diagonal[0]
        for y in range(1, CY):
            lower[d, y] = side * inverse[d, y - 1]
            inverse[d, y] = 1 / (diagonal[y] - side * lower[d, y])
    has_low = (np.arange(NK) > 0).astype(np.float64)[:, None]
    has_high = (np.arange(NK) < NK - 1).astype(np.float64)[:, None]
    parts = dict(
        send_up=send_up, send_down=send_down, take_low=take_low, take_high=take_high, near_low=near_low,
        near_high=near_high, own_low=own_low, own_high=own_high, lower=lower, inverse=inverse,
        has_low=has_low, has_high=has_high,
    )
    places, start = {}, 0
    for name, value in parts.items():
        places[name] = start
        start += value.shape[1]
    return np.concatenate(list(parts.values()), axis=1), places, reach


def split(value):
    high = value.astype(BF16)
    low = (value - high.astype(F32)).astype(BF16)
    return high, low


def dot(a, b, dims=((1,), (0,))):
    return lax.dot_general(a, b, (dims, ((), ())), preferred_element_type=F32)


def kernel(
    places_d, places_f, width,
    fields, jac, inflow, donors, receptors, table, dx, fx, dz, fz, out,
    u0, sel, place, ts, tr, u, pu, dy, q, pq, gx_, gz_, pp, ps, sb,
    outlet, inlet, phi_s, phi_d, phi_t, phi_f, low_d, high_d, low_f, high_f,
    tile_s, tile_r, u_s, u_r, q_s, q_r, s_s, s_r, pd_s, pd_r, pf_s, pf_r, h_s, h_r, in_s, in_r,
):
    sect = lax.axis_index("sect")
    g = lax.axis_index("gx")
    k = lax.axis_index("yz")
    here = k * width

    def along_gx(j):
        return lax.rem(g + j, NG)

    def from_gx(j):
        return lax.rem(g + NG - j, NG)

    def along_yz(j):
        return lax.rem(k + j, NK)

    def from_yz(j):
        return lax.rem(k + NK - j, NK)

    is_outlet = jnp.logical_and(sect == 0, g == 0)
    is_inlet = jnp.logical_and(sect == 1, g == 0)

    barrier = pltpu.get_barrier_semaphore()

    @pl.loop(1, NG)
    def _(j):
        pl.semaphore_signal(barrier, inc=1, device_id={"gx": along_gx(j)}, device_id_type=MESH)

    @pl.loop(1, NK)
    def _(j):
        pl.semaphore_signal(barrier, inc=1, device_id={"yz": along_yz(j)}, device_id_type=MESH)

    @pl.when(is_inlet)
    def _():
        @pl.loop(0, NK)
        def _(j):
            pl.semaphore_signal(barrier, inc=1, device_id={"sect": 0, "yz": j}, device_id_type=MESH)

    @pl.when(is_outlet)
    def _():
        for y in range(CY):
            for f in range(5):
                outlet[y : y + 1, f * CZ : (f + 1) * CZ] = fields[0, f, CX - 1 : CX, y * CZ : (y + 1) * CZ]

    @pl.when(jnp.logical_not(is_outlet))
    def _():
        pl.semaphore_wait(barrier, NG + NK - 2)

    @pl.when(is_outlet)
    def _():
        pl.semaphore_wait(barrier, NG + 2 * NK - 2)

        @pl.loop(0, NK)
        def _(j):
            pltpu.make_async_remote_copy(
                outlet, inlet.at[pl.ds(k * CY, CY)], in_s.at[j], in_r.at[k],
                device_id={"sect": 1, "yz": j}, device_id_type=MESH,
            ).start()

    for y in range(CY):
        for f in range(5):
            u0[y, f] = fields[0, f, :, y * CZ : (y + 1) * CZ]

    offset = lax.broadcasted_iota(jnp.int32, (8, CZ), 1) - lax.broadcasted_iota(jnp.int32, (8, CZ), 0)

    @pl.loop(0, SLOTS // 2)
    def _(j):
        for b in range(2):
            rows = []
            for e in range(2):
                slot = 2 * j + e
                first = jnp.where(donors[slot * 3 + 1] == b, donors[slot * 3 + 2], -1000)
                hit = jnp.logical_or(offset == first, offset == first + 1)
                rows.append(jnp.where(hit, 0.5, 0.0))
            sel[b, pl.ds(pl.multiple_of(16 * j, 16), 16), :] = jnp.concatenate(rows, axis=0).astype(BF16)

    ts[:, :, 256:384] = jnp.zeros((NG, 32, 128), F32)

    @pl.when(is_inlet)
    def _():
        @pl.loop(0, NK)
        def _(j):
            pltpu.make_async_remote_copy(
                outlet, inlet.at[pl.ds(j * CY, CY)], in_s.at[j], in_r.at[j],
                device_id={"sect": 1, "yz": j}, device_id_type=MESH,
            ).wait_recv()

        for y in range(CY):
            row = inlet[pl.ds(inflow[y], 1), :]
            for f in range(5):
                u0[y, f, 0:1, :] = row[:, f * CZ : (f + 1) * CZ]

    payload = None
    for b in range(2):
        for part in split(u0[8 * b : 8 * b + 8].reshape(320, CZ)):
            term = dot(sel[b], part, ((1,), (1,)))
            payload = term if payload is None else payload + term
    ts[:, :, 0:320] = payload.reshape(NG, 32, 320)

    def all_to_all(source, target, send, receive, j):
        return pltpu.make_async_remote_copy(
            source.at[along_gx(j)], target.at[g], send.at[j], receive.at[j],
            device_id={"gx": along_gx(j)}, device_id_type=MESH,
        )

    def arrive_all(source, target, send, receive):
        @pl.loop(1, NG)
        def _(j):
            pltpu.make_async_remote_copy(
                source.at[along_gx(j)], target.at[from_gx(j)], send.at[j], receive.at[j],
                device_id={"gx": along_gx(j)}, device_id_type=MESH,
            ).wait_recv()

    @pl.loop(1, NG)
    def _(j):
        all_to_all(ts, tr, tile_s, tile_r, j).start()

    tr[g] = ts[g]

    def place_row(j, counts):
        counts = list(counts)
        for t in range(2):
            rows = []
            for e in range(2):
                goal = (receptors[2 * j + e] - 32 * t) * 8
                one = jnp.where(offset == goal, 1.0, 0.0)
                counts[t] = counts[t] + one
                rows.append(one)
            place[t, pl.ds(pl.multiple_of(16 * j, 16), 16), :] = jnp.concatenate(rows, axis=0).astype(BF16)
        return tuple(counts)

    counts = lax.fori_loop(0, SLOTS // 2, place_row, (jnp.zeros((8, CZ), F32),) * 2)

    arrive_all(ts, tr, tile_s, tile_r)

    received = split(tr[...].reshape(512, 384))
    for t in range(2):
        total = dot(received[0], place[t], ((0,), (0,))) + dot(received[1], place[t], ((0,), (0,)))
        hits = jnp.sum(counts[t], axis=0, keepdims=True)
        scale = (1.0 / jnp.maximum(hits, 1.0)).reshape(1, 1, 1, CZ)
        mean = total[:320].reshape(8, 5, 8, CZ) * scale
        u[8 * t : 8 * t + 8] = jnp.where(hits.reshape(1, 1, 1, CZ) > 0, mean, u0[8 * t : 8 * t + 8])

    @pl.loop(1, NG)
    def _(j):
        all_to_all(u, pu, u_s, u_r, j).start()

    pu[g] = u[g]

    def neighbours(source, low, high, reach, base):
        up = pltpu.make_async_remote_copy(
            source.at[pl.ds(CY - reach, reach)], low, h_s.at[base], h_r.at[base],
            device_id={"yz": along_yz(1)}, device_id_type=MESH,
        )
        down = pltpu.make_async_remote_copy(
            source.at[pl.ds(0, reach)], high, h_s.at[base + 1], h_r.at[base + 1],
            device_id={"yz": from_yz(1)}, device_id_type=MESH,
        )
        return up, down

    def spread(planes, target, send, receive, j):
        peer = along_yz(j)
        which = lax.div(k - peer + NK, NK)
        return pltpu.make_async_remote_copy(
            planes.at[which], target.at[k], send.at[j], receive.at[j], device_id={"yz": peer}, device_id_type=MESH,
        )

    def make_planes(source, planes, places):
        @pl.loop(0, 5)
        def _(f):
            up = down = None
            for y in range(CY):
                row = source[y, f]
                a = table[here + places["send_up"] + y] * row
                b = table[here + places["send_down"] + y] * row
                up, down = (a, b) if up is None else (up + a, down + b)
            planes[0, f] = up
            planes[1, f] = down

    def spread_out(source, planes, target, send, receive, low, high, reach, base):
        for copy in neighbours(source, low, high, reach, base):
            copy.start()

        @pl.loop(1, NK)
        def _(j):
            spread(planes, target, send, receive, j).start()

    def spread_in(source, planes, target, send, receive, low, high, reach, base):
        for copy in neighbours(source, low, high, reach, base):
            copy.wait_recv()

        @pl.loop(1, NK)
        def _(j):
            pltpu.make_async_remote_copy(
                planes.at[0], target.at[from_yz(j)], send.at[j], receive.at[j],
                device_id={"yz": along_yz(j)}, device_id_type=MESH,
            ).wait_recv()

    def y_lines(source, gathered, low, high, places, reach, stencil, side, store):
        def entry(name, index=0):
            return table[here + places[name] + index]

        @pl.loop(0, 5)
        def _(f):
            for half in range(2):
                lanes = slice(128 * half, 128 * half + 128)
                from_low = from_high = None
                for j in range(1, NK):
                    s = from_yz(j)
                    plane = gathered[s, f, :, lanes]
                    a = table[here + places["take_low"] + s] * plane
                    b = table[here + places["take_high"] + s] * plane
                    from_low, from_high = (a, b) if from_low is None else (from_low + a, from_high + b)
                rows = [low[h, f, :, lanes] * entry("has_low") for h in range(reach)]
                rows += [source[y, f, :, lanes] for y in range(CY)]
                rows += [high[h, f, :, lanes] * entry("has_high") for h in range(reach)]
                for h in range(reach):
                    from_low += entry("near_low", h) * rows[h] + entry("own_low", h) * rows[reach + h]
                    from_high += entry("near_high", h) * rows[reach + CY + h] + entry("own_high", h) * rows[CY + h]
                pairs = {}
                for move, factor in stencil:
                    pairs.setdefault(abs(move), {})[move] = factor
                values = []
                for y in range(CY):
                    at = reach + y
                    value = None
                    for move, factors in pairs.items():
                        if move == 0:
                            term = np.float32(factors[0]) * rows[at]
                        elif factors[move] == factors[-move]:
                            term = np.float32(factors[move]) * (rows[at + move] + rows[at - move])
                        else:
                            term = np.float32(factors[move]) * (rows[at + move] - rows[at - move])
                        value = term if value is None else value + term
                    if y == 0:
                        value = value + from_low
                    if y == CY - 1:
                        value = value + from_high
                    if y > 0:
                        value = value - entry("lower", y) * values[-1]
                    values.append(value)
                last = None
                for y in range(CY - 1, -1, -1):
                    value = values[y] if last is None else values[y] - np.float32(side) * last
                    last = value * entry("inverse", y)
                    store(y, f, half, last)

    deriv = (u, phi_s, phi_d, pd_s, pd_r, low_d, high_d, 2, 0)
    make_planes(u, phi_s, places_d)
    spread_out(*deriv)
    spread_in(*deriv)

    def store_dy(y, f, half, value):
        dy[y, f, :, 128 * half : 128 * half + 128] = value

    y_lines(u, phi_d, low_d, high_d, places_d, 2, DERIV_STENCIL, SIDE_DERIV, store_dy)

    def mix(d, f, h):
        return jac[d * 25 + f * 5 + h] * (-SEGMENT_STEP)

    @pl.loop(1, NG + 1)
    def _(j):
        y = along_gx(j)
        slopes = [dy[y, h] for h in range(5)]
        for f in range(5):
            value = mix(1, f, 0) * slopes[0]
            for h in range(1, 5):
                value += mix(1, f, h) * slopes[h]
            q[y, f] = value

        @pl.when(j < NG)
        def _():
            all_to_all(q, pq, q_s, q_r, j).start()

    pq[g] = q[g]

    arrive_all(u, pu, u_s, u_r)
    for f in range(5):
        lines = pu[:, f].reshape(NX, CZ)
        high, low = split(lines)
        gx_[f] = dot(dx[sect, 0], high) + dot(dx[sect, 0], low) + dot(dx[sect, 1], high)
        gz_[f] = dot(high, dz[0]) + dot(low, dz[0]) + dot(high, dz[1])

    @pl.loop(0, 5)
    def _(f):
        value = pu[:, f].reshape(NX, CZ)
        for h in range(5):
            value += jac[f * 5 + h] * (-SEGMENT_STEP) * gx_[h]
            value += jac[50 + f * 5 + h] * (-SEGMENT_STEP) * gz_[h]
        pp[f] = value

    arrive_all(q, pq, q_s, q_r)
    for f in range(5):
        high, low = split(pp[f] + pq[:, f].reshape(NX, CZ))
        smooth = dot(high, fz[0]) + dot(low, fz[0]) + dot(high, fz[1])
        high, low = split(smooth)
        smooth = dot(fx[sect, 0], high) + dot(fx[sect, 0], low) + dot(fx[sect, 1], high)
        ps[:, f] = smooth.reshape(NG, CX, CZ)

    @pl.loop(1, NG)
    def _(j):
        all_to_all(ps, sb, s_s, s_r, j).start()

    sb[g] = ps[g]
    arrive_all(ps, sb, s_s, s_r)

    smooth = (sb, phi_t, phi_f, pf_s, pf_r, low_f, high_f, 5, 2)
    make_planes(sb, phi_t, places_f)
    spread_out(*smooth)
    spread_in(*smooth)

    def store_out(y, f, half, value):
        start = y * CZ + 128 * half
        out[0, f, :, start : start + 128] = value

    y_lines(sb, phi_f, low_f, high_f, places_f, 5, FILTER_STENCIL, SIDE_FILTER, store_out)

    @pl.loop(1, NG)
    def _(j):
        all_to_all(ts, tr, tile_s, tile_r, j).wait_send()
        all_to_all(u, pu, u_s, u_r, j).wait_send()
        all_to_all(q, pq, q_s, q_r, j).wait_send()
        all_to_all(ps, sb, s_s, s_r, j).wait_send()

    @pl.loop(1, NK)
    def _(j):
        spread(phi_s, phi_d, pd_s, pd_r, j).wait_send()
        spread(phi_t, phi_f, pf_s, pf_r, j).wait_send()

    for copy in neighbours(u, low_d, high_d, 2, 0) + neighbours(sb, low_f, high_f, 5, 2):
        copy.wait_send()

    @pl.when(is_outlet)
    def _():
        @pl.loop(0, NK)
        def _(j):
            pltpu.make_async_remote_copy(
                outlet, inlet.at[pl.ds(k * CY, CY)], in_s.at[j], in_r.at[k],
                device_id={"sect": 1, "yz": j}, device_id_type=MESH,
            ).wait_send()


def per_device(fields, jacobians, inflow_map, donor_tiles, receptor_tiles):
    table_d, places_d, reach_d = block_table(DERIV_STENCIL, SIDE_DERIV)
    table_f, places_f, reach_f = block_table(FILTER_STENCIL, SIDE_FILTER)
    places_f = {name: start + table_d.shape[1] for name, start in places_f.items()}
    table = np.concatenate([table_d, table_f], axis=1).astype(np.float32)
    width = table.shape[1]
    dx = np.stack([halves(line_matrix(NX, p, DERIV_STENCIL, SIDE_DERIV)) for p in (True, False)])
    fx = np.stack([halves(line_matrix(NX, p, FILTER_STENCIL, SIDE_FILTER)) for p in (True, False)])
    dz = halves(line_matrix(CZ, True, DERIV_STENCIL, SIDE_DERIV).T)
    fz = halves(line_matrix(CZ, True, FILTER_STENCIL, SIDE_FILTER).T)
    vmem = pl.BlockSpec(memory_space=pltpu.VMEM)
    smem = pl.BlockSpec(memory_space=pltpu.SMEM)
    block = (CY, 5, CX, CZ)
    planes = (5, CX, CZ)

    def buffer(*shape, kind=F32):
        return pltpu.VMEM(shape, kind)

    dma = pltpu.SemaphoreType.DMA
    return pl.pallas_call(
        functools.partial(kernel, places_d, places_f, width),
        out_shape=jax.ShapeDtypeStruct(fields.shape, F32),
        in_specs=[vmem, smem, smem, smem, smem, smem, vmem, vmem, vmem, vmem],
        out_specs=vmem,
        scratch_shapes=[
            buffer(*block),
            buffer(2, 512, CZ, kind=BF16), buffer(2, 512, CZ, kind=BF16),
            buffer(NG, 32, 384), buffer(NG, 32, 384),
            buffer(*block), buffer(*block), buffer(*block), buffer(*block), buffer(*block),
            buffer(5, NX, CZ), buffer(5, NX, CZ), buffer(5, NX, CZ),
            buffer(*block), buffer(*block),
            buffer(CY, 5 * CZ), buffer(NY, 5 * CZ),
            buffer(2, *planes), buffer(NK, *planes), buffer(2, *planes), buffer(NK, *planes),
            buffer(2, *planes), buffer(2, *planes), buffer(5, *planes), buffer(5, *planes),
            dma((NG,)), dma((NG,)), dma((NG,)), dma((NG,)), dma((NG,)), dma((NG,)), dma((NG,)), dma((NG,)),
            dma((NK,)), dma((NK,)), dma((NK,)), dma((NK,)), dma((4,)), dma((4,)), dma((NK,)), dma((NK,)),
        ],
        compiler_params=pltpu.CompilerParams(
            collective_id=0, has_side_effects=True, vmem_limit_bytes=48 * 1024 * 1024
        ),
        name="segment",
    )(
        fields, jacobians.reshape(75), inflow_map, donor_tiles.reshape(3 * SLOTS), receptor_tiles.reshape(SLOTS),
        jnp.asarray(table.reshape(-1)), jnp.asarray(dx), jnp.asarray(fx), jnp.asarray(dz), jnp.asarray(fz),
    )


def solution(mesh):
    in_specs = (
        P("sect", None, "gx", "yz"),
        P(),
        P("yz"),
        P("sect", "gx", "yz", None, None),
        P("sect", "gx", "yz", None),
    )
    out_specs = P("sect", None, "gx", "yz")
    return jax.shard_map(
        per_device, mesh=mesh, in_specs=in_specs, out_specs=out_specs, check_vma=False
    )
```

```python
import functools

import jax
import jax.numpy as jnp
import ml_dtypes
import numpy as np
from jax import lax
from jax.experimental import pallas as pl
from jax.experimental.pallas import tpu as pltpu
from jax.sharding import PartitionSpec as P

MESH = pl.DeviceIdType.MESH
HBM = pltpu.MemorySpace.HBM
F32 = jnp.float32
BF16 = jnp.bfloat16

CX = 8
CY = 16
CZ = 256
NG = 16
NK = 8
NX = 128
NY = 128
SLOTS = 64
GROUPS = ((0, 2), (2, 4), (4, 5))
VMEM_MIB = 62
INLET_ORDER = (4, 3, 5, 2, 6, 1, 7)
DIRECT_DERIV = 0
DIRECT_FILTER = 2

SEGMENT_STEP = 0.25
SIDE_DERIV = 1.0 / 3.0
SIDE_FILTER = 0.49


def filter_coeffs():
    side = SIDE_FILTER
    return [
        (193 + 126 * side) / 256,
        (105 + 302 * side) / 256,
        15 * (-1 + 2 * side) / 64,
        45 * (1 - 2 * side) / 512,
        5 * (-1 + 2 * side) / 256,
        (1 - 2 * side) / 512,
    ]


DERIV_STENCIL = ((1, 7.0 / 9.0), (-1, -7.0 / 9.0), (2, 1.0 / 36.0), (-2, -1.0 / 36.0))
FILTER_STENCIL = ((0, filter_coeffs()[0]),) + tuple(
    (sign * reach, filter_coeffs()[reach] / 2) for reach in range(1, 6) for sign in (1, -1)
)


def sides(length, periodic, stencil, side):
    left = np.eye(length)
    right = np.zeros((length, length))
    for row in range(length):
        for offset, factor in ((-1, side), (1, side)):
            if periodic or 0 <= row + offset < length:
                left[row, (row + offset) % length] += factor
        for offset, factor in stencil:
            if periodic or 0 <= row + offset < length:
                right[row, (row + offset) % length] += factor
    return left, right


def line_matrix(length, periodic, stencil, side):
    return np.linalg.solve(*sides(length, periodic, stencil, side))


def halves(matrix):
    value = np.asarray(matrix, np.float32)
    high = value.astype(ml_dtypes.bfloat16)
    low = (value - high.astype(np.float32)).astype(ml_dtypes.bfloat16)
    return np.stack([high, low])


def block_table(stencil, side):
    left, right = sides(NY, False, stencil, side)
    reach = max(offset for offset, _ in stencil)
    below = np.zeros((NK, NY))
    above = np.zeros((NK, NY))
    corner_low = np.zeros(NK)
    corner_high = np.zeros(NK)
    for d in range(NK):
        lo, hi = d * CY, (d + 1) * CY
        if d > 0:
            row = np.linalg.solve(left[:lo, :lo].T, np.eye(lo)[lo - 1])
            below[d] = -side * (row @ right[:lo])
            corner_low[d] = row[-1]
        if d < NK - 1:
            row = np.linalg.solve(left[hi:, hi:].T, np.eye(NY - hi)[0])
            above[d] = -side * (row @ right[hi:])
            corner_high[d] = row[0]
    send_up = np.zeros((NK, CY))
    send_down = np.zeros((NK, CY))
    for s in range(NK):
        cells = slice(s * CY, (s + 1) * CY)
        if s < NK - 1:
            value = below[min(s + 2, NK - 1)][cells]
            send_up[s] = value / np.abs(value).max()
        if s > 0:
            value = above[max(s - 2, 0)][cells]
            send_down[s] = value / np.abs(value).max()
    take_low = np.zeros((NK, NK))
    take_high = np.zeros((NK, NK))
    near_low = np.zeros((NK, reach))
    near_high = np.zeros((NK, reach))
    own_low = np.zeros((NK, reach))
    own_high = np.zeros((NK, reach))
    for d in range(NK):
        for s in range(d):
            value, unit = below[d][s * CY : (s + 1) * CY], send_up[s]
            core = unit[: CY - reach]
            take_low[d, s] = (value[: CY - reach] @ core) / (core @ core)
            if s == d - 1:
                near_low[d] = (value - take_low[d, s] * unit)[CY - reach :]
        for s in range(d + 1, NK):
            value, unit = above[d][s * CY : (s + 1) * CY], send_down[s]
            core = unit[reach:]
            take_high[d, s] = (value[reach:] @ core) / (core @ core)
            if s == d + 1:
                near_high[d] = (value - take_high[d, s] * unit)[:reach]
        own_low[d] = below[d][d * CY : d * CY + reach]
        own_high[d] = above[d][(d + 1) * CY - reach : (d + 1) * CY]
    lower = np.zeros((NK, CY))
    inverse = np.zeros((NK, CY))
    for d in range(NK):
        diagonal = np.ones(CY)
        diagonal[0] -= side**2 * corner_low[d]
        diagonal[-1] -= side**2 * corner_high[d]
        inverse[d, 0] = 1 / diagonal[0]
        for y in range(1, CY):
            lower[d, y] = side * inverse[d, y - 1]
            inverse[d, y] = 1 / (diagonal[y] - side * lower[d, y])
    has_low = (np.arange(NK) > 0).astype(np.float64)
    has_high = (np.arange(NK) < NK - 1).astype(np.float64)
    parts = dict(
        send_up=send_up, send_down=send_down, take=np.stack([take_low, take_high]), near_low=near_low,
        near_high=near_high, own_low=own_low, own_high=own_high, lower=lower, inverse=inverse,
        has_low=has_low, has_high=has_high,
    )
    places, start = {}, 0
    for name, value in parts.items():
        places[name] = start
        start += value.size
    return np.concatenate([value.reshape(-1) for value in parts.values()]), places


def split(value):
    high = value.astype(BF16)
    low = (value - high.astype(F32)).astype(BF16)
    return high, low


def dot(a, b, dims=((1,), (0,))):
    return lax.dot_general(a, b, (dims, ((), ())), preferred_element_type=F32)


def kernel(
    at_d, at_f,
    fields_hbm, jac_hbm, inflow_hbm, donors_hbm, receptors_hbm, table_hbm, dx_hbm, fx_hbm, dz_hbm, fz_hbm, out,
    fields, jac, inflow, donors, receptors, table, dx, fx, dz, fz, load_sem,
    u0, sel, place, ts, tr, u, pu, v, q, pq, gx_, gz_, pp, ps, sb,
    outlet, inlet, inlet_rows, patch_s, patch_r,
    phi_d, col_d, gam_d, got_d, phi_f, col_f, gam_f, got_f, edge_d, edge_f, planes_d, everyone_d, planes_f, everyone_f,
    tile_ss, tile_rs, u_ss, u_rs, q_ss, q_rs, s_ss, s_rs,
    d1_ss, d1_rs, d2_ss, d2_rs, f1_ss, f1_rs, f2_ss, f2_rs, dh_ss, dh_rs, fh_ss, fh_rs, in_ss, in_rs, patch_ss, patch_rs,
):
    sect = lax.axis_index("sect")
    g = lax.axis_index("gx")
    k = lax.axis_index("yz")

    def along_gx(j):
        return lax.rem(g + j, NG)

    def along_yz(j):
        return lax.rem(k + j, NK)

    def from_yz(j):
        return lax.rem(k + NK - j, NK)

    is_outlet = jnp.logical_and(sect == 0, g == 0)
    is_inlet = jnp.logical_and(sect == 1, g == 0)

    barrier = pltpu.get_barrier_semaphore()

    @pl.loop(1, NG)
    def _(j):
        pl.semaphore_signal(barrier, inc=1, device_id={"gx": along_gx(j)}, device_id_type=MESH)

    @pl.loop(1, NK)
    def _(j):
        pl.semaphore_signal(barrier, inc=1, device_id={"yz": along_yz(j)}, device_id_type=MESH)

    @pl.when(is_inlet)
    def _():
        pl.semaphore_signal(barrier, inc=1, device_id={"sect": 0}, device_id_type=MESH)

    pairs = (
        (fields_hbm, fields), (donors_hbm, donors), (receptors_hbm, receptors), (inflow_hbm, inflow),
        (jac_hbm, jac), (table_hbm, table), (dx_hbm, dx), (dz_hbm, dz), (fz_hbm, fz), (fx_hbm, fx),
    )
    loads = [pltpu.make_async_copy(source, target, load_sem.at[i]) for i, (source, target) in enumerate(pairs)]
    for load in loads:
        load.start()
    loads[0].wait()

    mine = pl.ds(pl.multiple_of(k * CY, CY), CY)

    def inflow_copy():
        return pltpu.make_async_remote_copy(
            outlet, inlet.at[mine], in_ss.at[0], in_rs.at[0], device_id={"sect": 1}, device_id_type=MESH,
        )

    def inlet_copies():
        whole = inlet.at[0 : NY - CY]
        return pltpu.make_async_remote_copy(
            whole, whole, in_ss.at[1], in_rs.at[1], device_id={"yz": along_yz(1)}, device_id_type=MESH,
        )

    @pl.when(is_outlet)
    def _():
        for y in range(CY):
            for f in range(5):
                outlet[y : y + 1, f * CZ : (f + 1) * CZ] = fields[0, f, CX - 1 : CX, y * CZ : (y + 1) * CZ]

        pl.semaphore_wait(barrier, NG + NK - 1)
        inflow_copy().start()

    for y in range(CY):
        for f in range(5):
            u0[y, f] = fields[0, f, :, y * CZ : (y + 1) * CZ]

    @pl.when(is_inlet)
    def _():
        for y in range(CY):
            for f in range(5):
                u0[y, f, 0:1, :] = jnp.zeros((1, CZ), F32)

    offset = lax.broadcasted_iota(jnp.int32, (8, CZ), 1) - lax.broadcasted_iota(jnp.int32, (8, CZ), 0)
    loads[1].wait()

    @pl.loop(0, SLOTS // 2)
    def _(j):
        for b in range(2):
            rows = []
            for e in range(2):
                slot = 2 * j + e
                first = jnp.where(donors[0, 0, 1, 0, slot] == b, donors[0, 0, 2, 0, slot], -1000)
                hit = jnp.logical_or(offset == first, offset == first + 1)
                rows.append(jnp.where(hit, 0.5, 0.0))
            sel[b, pl.ds(pl.multiple_of(16 * j, 16), 16), :] = jnp.concatenate(rows, axis=0).astype(BF16)

    payload = None
    for b in range(2):
        lines = jnp.concatenate([u0[8 * b : 8 * b + 8].reshape(320, CZ), jnp.zeros((64, CZ), F32)], axis=0)
        for part in split(lines):
            term = dot(sel[b], part, ((1,), (1,)))
            payload = term if payload is None else payload + term
    ts[:, 0:32, :] = payload[:, 0:256].reshape(NG, 32, 256)
    rest = payload[:, 256:384].reshape(NG, 4, 8, 128)
    left = lax.broadcasted_iota(jnp.int32, (NG, 8, 128), 2) < 64
    for e in range(2):
        moved = pltpu.roll(rest[:, 2 * e + 1].reshape(NG * 8, 128), 64, 1).reshape(NG, 8, 128)
        ts[:, 32:40, 128 * e : 128 * e + 128] = jnp.where(left, rest[:, 2 * e], moved)

    @pl.when(jnp.logical_not(is_outlet))
    def _():
        pl.semaphore_wait(barrier, NG + NK - 2)

    leaving = []
    coming = {}

    def batch(name, source, target, send, receive):
        whole = pltpu.make_async_remote_copy(
            source, target, send, receive, device_id={"gx": along_gx(1)}, device_id_type=MESH
        )
        leaving.append(whole.wait_send)
        coming[name] = whole.wait_recv

    def arrive(name):
        coming.pop(name)()

    for j in range(1, NG):
        pltpu.make_async_remote_copy(
            ts.at[along_gx(j)], tr.at[g], tile_ss.at[0], tile_rs.at[0],
            device_id={"gx": along_gx(j)}, device_id_type=MESH,
        ).start()
    batch("tiles", ts.at[1:NG], tr.at[1:NG], tile_ss.at[0], tile_rs.at[0])

    tr[g] = ts[g]

    @pl.when(is_inlet)
    def _():
        inflow_copy().wait_recv()
        for j in INLET_ORDER:
            pltpu.make_async_remote_copy(
                inlet.at[mine], inlet.at[mine], in_ss.at[1], in_rs.at[1],
                device_id={"yz": along_yz(j)}, device_id_type=MESH,
            ).start()

    loads[2].wait()

    def place_row(j, counts):
        counts = list(counts)
        for t in range(2):
            rows = []
            for e in range(2):
                goal = (receptors[2 * j + e] - 32 * t) * 8
                one = jnp.where(offset == goal, 1.0, 0.0)
                counts[t] = counts[t] + one
                rows.append(one)
            place[t, pl.ds(pl.multiple_of(16 * j, 16), 16), :] = jnp.concatenate(rows, axis=0).astype(BF16)
        return tuple(counts)

    counts = lax.fori_loop(0, SLOTS // 2, place_row, (jnp.zeros((8, CZ), F32),) * 2)

    loads[3].wait()

    def patch_copy(j):
        return pltpu.make_async_remote_copy(
            patch_s.at[j], patch_r, patch_ss.at[j], patch_rs.at[0], device_id={"gx": j}, device_id_type=MESH,
        )

    @pl.when(is_inlet)
    def _():
        inlet_rows[:, 32:48, :] = jnp.zeros((2, 16, CZ), F32)

        inlet_copies().wait_recv()

        for y in range(CY):
            row = inlet[pl.ds(inflow[y], 1), :]
            for f in range(5):
                cells = row[:, f * CZ : (f + 1) * CZ]
                at = (y % 8) * 5 + f
                u0[y, f, 0:1, :] = cells
                inlet_rows[y // 8, at : at + 1, :] = cells
        total = None
        for b in range(2):
            lines = jnp.concatenate([inlet_rows[b], jnp.zeros((80, CZ), F32)], axis=0)
            for part in split(lines):
                term = dot(sel[b], part, ((1,), (1,)))
                total = term if total is None else total + term
        patch_s[...] = total.reshape(NG, 32, 128)

        @pl.loop(1, NG)
        def _(j):
            patch_copy(j).start()

        patch_r[...] = patch_s[0]

    arrive("tiles")

    main = tr[:, 0:32, :].reshape(512, 256)
    rest = []
    for e in range(2):
        two = tr[:, 32:40, 128 * e : 128 * e + 128]
        rest += [two, pltpu.roll(two.reshape(NG * 8, 128), 64, 1).reshape(NG, 8, 128)]
    rest = jnp.stack(rest, axis=1).reshape(512, 128)
    halves_of = [split(main), split(rest)]
    for t in range(2):
        total = jnp.concatenate(
            [
                dot(high, place[t], ((0,), (0,))) + dot(low, place[t], ((0,), (0,)))
                for high, low in halves_of
            ],
            axis=0,
        )
        hits = jnp.sum(counts[t], axis=0, keepdims=True)
        scale = (1.0 / jnp.maximum(hits, 1.0)).reshape(1, 1, 1, CZ)
        mean = total[:320].reshape(8, 5, 8, CZ) * scale
        value = jnp.where(hits.reshape(1, 1, 1, CZ) > 0, mean, u0[8 * t : 8 * t + 8])
        for f in range(5):
            u[f, 8 * t : 8 * t + 8] = value[:, f]

    @pl.when(sect == 1)
    def _():
        @pl.when(g > 0)
        def _():
            patch_copy(g).wait_recv()

        column = lax.broadcasted_iota(jnp.int32, (128, 384), 1)
        spread = (column == 8 * lax.broadcasted_iota(jnp.int32, (128, 384), 0)).astype(F32).astype(BF16)
        wide = None
        for part in split(patch_r[...]):
            term = dot(part, spread)
            wide = term if wide is None else wide + term
        high, low = split(wide)
        for t in range(2):
            rows = place[t, 0:32, :]
            total = dot(high, rows, ((0,), (0,))) + dot(low, rows, ((0,), (0,)))
            hits = jnp.sum(counts[t], axis=0, keepdims=True)
            value = (total * (1.0 / jnp.maximum(hits, 1.0)))[:320].reshape(8, 5, 8, CZ)
            for f in range(5):
                u[f, 8 * t : 8 * t + 8] += value[:, f]

    def start_all(name, source, target, send, receive, lo, hi, at):
        for j in range(1, NG):
            pltpu.make_async_remote_copy(
                source.at[lo:hi, along_gx(j)], target.at[lo:hi, g], send.at[at], receive.at[at],
                device_id={"gx": along_gx(j)}, device_id_type=MESH,
            ).start()
        batch((name, at), source.at[lo:hi, 1:NG], target.at[lo:hi, 1:NG], send.at[at], receive.at[at])
        target[lo:hi, g] = source[lo:hi, g]

    start_all("u", u, pu, u_ss, u_rs, 0, 5, 0)

    loads[4].wait()
    loads[5].wait()

    def mix(d, f, h):
        return jac[f, d, h] * (-SEGMENT_STEP)

    @pl.loop(0, CY)
    def _(y):
        cells = [u[h, y] for h in range(5)]
        for f in range(5):
            value = mix(1, f, 0) * cells[0]
            for h in range(1, 5):
                value += mix(1, f, h) * cells[h]
            v[f, y] = value

    def halo(operator, i):
        name, source, edge, reach = operator["name"], operator["source"], operator["edge"], operator["reach"]
        send, receive = operator["halo"]
        lo, hi = GROUPS[i]
        pltpu.make_async_remote_copy(
            source.at[lo:hi, CY - reach : CY], edge.at[lo:hi, 0:reach], send.at[i], receive.at[i],
            device_id={"yz": along_yz(1)}, device_id_type=MESH,
        ).start()
        pltpu.make_async_remote_copy(
            source.at[lo:hi, 0:reach], edge.at[lo:hi, reach : 2 * reach], send.at[i], receive.at[i],
            device_id={"yz": from_yz(1)}, device_id_type=MESH,
        ).start()
        batch((name, "halo", i), source.at[lo:hi, 0 : 2 * reach], edge.at[lo:hi], send.at[i], receive.at[i])

    def hops(name, source, target, sems, i):
        send, receive = sems
        for j in range(1, NK):
            pltpu.make_async_remote_copy(
                source.at[i, along_yz(j)], target.at[i, k], send.at[i], receive.at[i],
                device_id={"yz": along_yz(j)}, device_id_type=MESH,
            ).start()
        batch((name, i), source.at[i, 1:NK], target.at[i, 1:NK], send.at[i], receive.at[i])
        target[i, k] = source[i, k]

    def first_half(operator, i):
        source, phi, places = operator["source"], operator["phi"], operator["places"]
        lo, hi = GROUPS[i]
        direct = operator["direct"] == i
        planes, everyone = operator["planes"], operator["everyone"]
        for f in range(lo, hi if direct else lo + 2):
            for half in range(2):
                tile = (f - lo) * 2 + half
                if f >= hi:
                    phi[i, tile] = jnp.zeros((8, 128), F32)
                    phi[i, 4 + tile] = jnp.zeros((8, 128), F32)
                    continue
                up = down = None
                for y in range(CY):
                    row = source[f, y, :, 128 * half : 128 * half + 128]
                    a = table[places["send_up"] + k * CY + y] * row
                    b = table[places["send_down"] + k * CY + y] * row
                    up, down = (a, b) if up is None else (up + a, down + b)
                if direct:
                    planes[0, f - lo, :, 128 * half : 128 * half + 128] = up
                    planes[1, f - lo, :, 128 * half : 128 * half + 128] = down
                else:
                    phi[i, tile] = up
                    phi[i, 4 + tile] = down

        if direct:
            send, receive = operator["first"]
            for j in range(1, NK):
                peer = along_yz(j)
                pltpu.make_async_remote_copy(
                    planes.at[lax.div(k - peer + NK, NK)], everyone.at[k], send.at[i], receive.at[i],
                    device_id={"yz": peer}, device_id_type=MESH,
                ).start()
            whole = everyone.at[1:NK]
            batch((operator["name"] + "2", i), whole, whole, send.at[i], receive.at[i])
            halo(operator, i)
            return

        hops(operator["name"] + "1", phi, operator["col"], operator["first"], i)
        halo(operator, i)

    def second_half(operator, i):
        if operator["direct"] == i:
            return
        col, gam, places = operator["col"], operator["gam"], operator["places"]
        arrive((operator["name"] + "1", i))
        upward = lax.div(k, 4)
        tiles = [col[i, s] for s in range(NK)]

        @pl.loop(0, NK)
        def _(d):
            base = places["take"] + upward * (NK * NK) + d * NK
            total = table[base] * tiles[0]
            for s in range(1, NK):
                total += table[base + s] * tiles[s]
            gam[i, d] = total

        hops(operator["name"] + "2", gam, operator["got"], operator["second"], i)

    def y_lines(operator, i, stencil, side, store):
        source, got, edge, reach, places = (
            operator["source"], operator["got"], operator["edge"], operator["reach"], operator["places"],
        )
        lo, hi = GROUPS[i]
        arrive((operator["name"], "halo", i))
        arrive((operator["name"] + "2", i))

        def entry(name, count, index=0):
            return table[places[name] + k * count + index]

        for f in range(lo, hi):
            for half in range(2):
                lanes = slice(128 * half, 128 * half + 128)
                tile = (f - lo) * 2 + half
                if operator["direct"] == i:
                    from_low = from_high = None
                    for j in range(1, NK):
                        block = along_yz(j)
                        plane = operator["everyone"][block, f - lo, :, lanes]
                        a = table[places["take"] + k * NK + block] * plane
                        b = table[places["take"] + NK * NK + k * NK + block] * plane
                        from_low, from_high = (a, b) if from_low is None else (from_low + a, from_high + b)
                else:
                    from_low = got[i, tile]
                    from_high = got[i, 4 + tile]
                rows = [edge[f, h, :, lanes] * entry("has_low", 1) for h in range(reach)]
                rows += [source[f, y, :, lanes] for y in range(CY)]
                rows += [edge[f, reach + h, :, lanes] * entry("has_high", 1) for h in range(reach)]
                for h in range(reach):
                    from_low += entry("near_low", reach, h) * rows[h] + entry("own_low", reach, h) * rows[reach + h]
                    from_high += (
                        entry("near_high", reach, h) * rows[reach + CY + h]
                        + entry("own_high", reach, h) * rows[CY + h]
                    )
                moves = {}
                for move, factor in stencil:
                    moves.setdefault(abs(move), {})[move] = factor
                values = []
                for y in range(CY):
                    at = reach + y
                    value = None
                    for move, factors in moves.items():
                        if move == 0:
                            term = np.float32(factors[0]) * rows[at]
                        elif factors[move] == factors[-move]:
                            term = np.float32(factors[move]) * (rows[at + move] + rows[at - move])
                        else:
                            term = np.float32(factors[move]) * (rows[at + move] - rows[at - move])
                        value = term if value is None else value + term
                    if y == 0:
                        value = value + from_low
                    if y == CY - 1:
                        value = value + from_high
                    if y > 0:
                        value = value - entry("lower", CY, y) * values[-1]
                    values.append(value)
                last = None
                for y in range(CY - 1, -1, -1):
                    value = values[y] if last is None else values[y] - np.float32(side) * last
                    last = value * entry("inverse", CY, y)
                    store(y, f, half, last)

    deriv = dict(
        name="d", source=v, phi=phi_d, col=col_d, gam=gam_d, got=got_d, edge=edge_d, reach=2, places=at_d,
        first=(d1_ss, d1_rs), second=(d2_ss, d2_rs), halo=(dh_ss, dh_rs),
        direct=DIRECT_DERIV, planes=planes_d, everyone=everyone_d,
    )
    smooth = dict(
        name="f", source=sb, phi=phi_f, col=col_f, gam=gam_f, got=got_f, edge=edge_f, reach=5, places=at_f,
        first=(f1_ss, f1_rs), second=(f2_ss, f2_rs), halo=(fh_ss, fh_rs),
        direct=DIRECT_FILTER, planes=planes_f, everyone=everyone_f,
    )

    def store_q(y, f, half, value):
        q[f, y, :, 128 * half : 128 * half + 128] = value

    def store_out(y, f, half, value):
        start = y * CZ + 128 * half
        out[0, f, :, start : start + 128] = value

    count = len(GROUPS)
    def q_lines(i):
        y_lines(deriv, i, DERIV_STENCIL, SIDE_DERIV, store_q)
        start_all("q", q, pq, q_ss, q_rs, *GROUPS[i], i)

    for i in range(count):
        first_half(deriv, i)
    for i in range(1, count):
        second_half(deriv, i)
    for i in range(count):
        q_lines(i)

    for load in loads[6:]:
        load.wait()
    arrive(("u", 0))
    for f in range(5):
        high, low = split(pu[f].reshape(NX, CZ))
        gx_[f] = dot(dx[sect, 0], high) + dot(dx[sect, 0], low) + dot(dx[sect, 1], high)
        gz_[f] = dot(high, dz[0]) + dot(low, dz[0]) + dot(high, dz[1])

    @pl.loop(0, 5)
    def _(f):
        value = pu[f].reshape(NX, CZ)
        for h in range(5):
            value += mix(0, f, h) * gx_[h]
            value += mix(2, f, h) * gz_[h]
        pp[f] = value

    for i in range(count):
        lo, hi = GROUPS[i]
        arrive(("q", i))
        for f in range(lo, hi):
            high, low = split(pp[f] + pq[f].reshape(NX, CZ))
            value = dot(high, fz[0]) + dot(low, fz[0]) + dot(high, fz[1])
            high, low = split(value)
            value = dot(fx[sect, 0], high) + dot(fx[sect, 0], low) + dot(fx[sect, 1], high)
            ps[f] = value.reshape(NG, CX, CZ)
        start_all("s", ps, sb, s_ss, s_rs, lo, hi, i)

    for i in range(count):
        arrive(("s", i))
        first_half(smooth, i)
        if i > 0:
            second_half(smooth, i - 1)
    for i in range(count):
        y_lines(smooth, i, FILTER_STENCIL, SIDE_FILTER, store_out)

    for wait in leaving:
        wait()

    @pl.when(is_outlet)
    def _():
        inflow_copy().wait_send()

    @pl.when(is_inlet)
    def _():
        inlet_copies().wait_send()

        @pl.loop(1, NG)
        def _(j):
            patch_copy(j).wait_send()


def per_device(fields, jacobians, inflow_map, donor_tiles, receptor_tiles):
    table_d, places_d = block_table(DERIV_STENCIL, SIDE_DERIV)
    table_f, places_f = block_table(FILTER_STENCIL, SIDE_FILTER)
    places_f = {name: start + table_d.size for name, start in places_f.items()}
    table = np.concatenate([table_d, table_f]).astype(np.float32)
    dx = np.stack([halves(line_matrix(NX, p, DERIV_STENCIL, SIDE_DERIV)) for p in (True, False)])
    fx = np.stack([halves(line_matrix(NX, p, FILTER_STENCIL, SIDE_FILTER)) for p in (True, False)])
    dz = halves(line_matrix(CZ, True, DERIV_STENCIL, SIDE_DERIV).T)
    fz = halves(line_matrix(CZ, True, FILTER_STENCIL, SIDE_FILTER).T)
    block = (5, CY, CX, CZ)
    count = len(GROUPS)

    def buffer(*shape, kind=F32):
        return pltpu.VMEM(shape, kind)

    def scalars(*shape, kind=jnp.int32):
        return pltpu.SMEM(shape, kind)

    def dma(length):
        return pltpu.SemaphoreType.DMA((length,))

    tiles = [buffer(count, NK, 8, 128)] * 4
    inputs = (
        fields, jnp.transpose(jacobians, (1, 0, 2)), inflow_map, jnp.transpose(donor_tiles, (0, 1, 4, 2, 3)),
        receptor_tiles.reshape(SLOTS), jnp.asarray(table), jnp.asarray(dx), jnp.asarray(fx), jnp.asarray(dz),
        jnp.asarray(fz),
    )
    return pl.pallas_call(
        functools.partial(kernel, places_d, places_f),
        out_shape=jax.ShapeDtypeStruct(fields.shape, F32),
        in_specs=[pl.BlockSpec(memory_space=HBM)] * len(inputs),
        out_specs=pl.BlockSpec(memory_space=pltpu.VMEM),
        scratch_shapes=[
            buffer(*fields.shape), scalars(5, 3, 5, kind=F32), scalars(16), scalars(1, 1, 3, 1, SLOTS), scalars(SLOTS),
            scalars(table.size, kind=F32),
            buffer(*dx.shape, kind=BF16), buffer(*fx.shape, kind=BF16),
            buffer(*dz.shape, kind=BF16), buffer(*fz.shape, kind=BF16), dma(10),
            buffer(CY, 5, CX, CZ),
            buffer(2, 512, CZ, kind=BF16), buffer(2, 512, CZ, kind=BF16),
            buffer(NG, 40, 256), buffer(NG, 40, 256),
            buffer(*block), buffer(*block), buffer(*block), buffer(*block), buffer(*block),
            buffer(5, NX, CZ), buffer(5, NX, CZ), buffer(5, NX, CZ),
            buffer(*block), buffer(*block),
            buffer(CY, 5 * CZ), buffer(NY, 5 * CZ), buffer(2, 48, CZ), buffer(NG, 32, 128), buffer(32, 128),
            *tiles, *tiles,
            buffer(5, 4, CX, CZ), buffer(5, 10, CX, CZ),
            buffer(2, 2, CX, CZ), buffer(NK, 2, CX, CZ), buffer(2, 1, CX, CZ), buffer(NK, 1, CX, CZ),
            *([dma(1)] * 4), *([dma(count)] * 16), dma(2), dma(2), dma(NG), dma(1),
        ],
        compiler_params=pltpu.CompilerParams(
            collective_id=0, has_side_effects=True, vmem_limit_bytes=VMEM_MIB * 1024 * 1024
        ),
        name="segment",
    )(*inputs)


def solution(mesh):
    in_specs = (
        P("sect", None, "gx", "yz"),
        P(),
        P("yz"),
        P("sect", "gx", "yz", None, None),
        P("sect", "gx", "yz", None),
    )
    out_specs = P("sect", None, "gx", "yz")
    return jax.shard_map(
        per_device, mesh=mesh, in_specs=in_specs, out_specs=out_specs, check_vma=False
    )
```

```python
import functools

import jax
import jax.numpy as jnp
import ml_dtypes
import numpy as np
from jax import lax
from jax.experimental import pallas as pl
from jax.experimental.pallas import tpu as pltpu
from jax.sharding import PartitionSpec as P

MESH = pl.DeviceIdType.MESH
HBM = pltpu.MemorySpace.HBM
F32 = jnp.float32
BF16 = jnp.bfloat16

CX = 8
CY = 16
CZ = 256
NG = 16
NK = 8
NX = 128
NY = 128
SLOTS = 64
GROUPS = ((0, 2), (2, 4), (4, 5))
VMEM_MIB = 62
INLET_ORDER = (4, 3, 5, 2, 6, 1, 7)
DIRECT_DERIV = (0, 1, 2)
DIRECT_FILTER = (2,)

SEGMENT_STEP = 0.25
SIDE_DERIV = 1.0 / 3.0
SIDE_FILTER = 0.49


def filter_coeffs():
    side = SIDE_FILTER
    return [
        (193 + 126 * side) / 256,
        (105 + 302 * side) / 256,
        15 * (-1 + 2 * side) / 64,
        45 * (1 - 2 * side) / 512,
        5 * (-1 + 2 * side) / 256,
        (1 - 2 * side) / 512,
    ]


DERIV_STENCIL = ((1, 7.0 / 9.0), (-1, -7.0 / 9.0), (2, 1.0 / 36.0), (-2, -1.0 / 36.0))
FILTER_STENCIL = ((0, filter_coeffs()[0]),) + tuple(
    (sign * reach, filter_coeffs()[reach] / 2) for reach in range(1, 6) for sign in (1, -1)
)


def sides(length, periodic, stencil, side):
    left = np.eye(length)
    right = np.zeros((length, length))
    for row in range(length):
        for offset, factor in ((-1, side), (1, side)):
            if periodic or 0 <= row + offset < length:
                left[row, (row + offset) % length] += factor
        for offset, factor in stencil:
            if periodic or 0 <= row + offset < length:
                right[row, (row + offset) % length] += factor
    return left, right


def line_matrix(length, periodic, stencil, side):
    return np.linalg.solve(*sides(length, periodic, stencil, side))


def halves(matrix):
    value = np.asarray(matrix, np.float32)
    high = value.astype(ml_dtypes.bfloat16)
    low = (value - high.astype(np.float32)).astype(ml_dtypes.bfloat16)
    return np.stack([high, low])


def block_table(stencil, side):
    left, right = sides(NY, False, stencil, side)
    reach = max(offset for offset, _ in stencil)
    below = np.zeros((NK, NY))
    above = np.zeros((NK, NY))
    corner_low = np.zeros(NK)
    corner_high = np.zeros(NK)
    for d in range(NK):
        lo, hi = d * CY, (d + 1) * CY
        if d > 0:
            row = np.linalg.solve(left[:lo, :lo].T, np.eye(lo)[lo - 1])
            below[d] = -side * (row @ right[:lo])
            corner_low[d] = row[-1]
        if d < NK - 1:
            row = np.linalg.solve(left[hi:, hi:].T, np.eye(NY - hi)[0])
            above[d] = -side * (row @ right[hi:])
            corner_high[d] = row[0]
    send_up = np.zeros((NK, CY))
    send_down = np.zeros((NK, CY))
    for s in range(NK):
        cells = slice(s * CY, (s + 1) * CY)
        if s < NK - 1:
            value = below[min(s + 2, NK - 1)][cells]
            send_up[s] = value / np.abs(value).max()
        if s > 0:
            value = above[max(s - 2, 0)][cells]
            send_down[s] = value / np.abs(value).max()
    take_low = np.zeros((NK, NK))
    take_high = np.zeros((NK, NK))
    near_low = np.zeros((NK, reach))
    near_high = np.zeros((NK, reach))
    own_low = np.zeros((NK, reach))
    own_high = np.zeros((NK, reach))
    for d in range(NK):
        for s in range(d):
            value, unit = below[d][s * CY : (s + 1) * CY], send_up[s]
            core = unit[: CY - reach]
            take_low[d, s] = (value[: CY - reach] @ core) / (core @ core)
            if s == d - 1:
                near_low[d] = (value - take_low[d, s] * unit)[CY - reach :]
        for s in range(d + 1, NK):
            value, unit = above[d][s * CY : (s + 1) * CY], send_down[s]
            core = unit[reach:]
            take_high[d, s] = (value[reach:] @ core) / (core @ core)
            if s == d + 1:
                near_high[d] = (value - take_high[d, s] * unit)[:reach]
        own_low[d] = below[d][d * CY : d * CY + reach]
        own_high[d] = above[d][(d + 1) * CY - reach : (d + 1) * CY]
    lower = np.zeros((NK, CY))
    inverse = np.zeros((NK, CY))
    for d in range(NK):
        diagonal = np.ones(CY)
        diagonal[0] -= side**2 * corner_low[d]
        diagonal[-1] -= side**2 * corner_high[d]
        inverse[d, 0] = 1 / diagonal[0]
        for y in range(1, CY):
            lower[d, y] = side * inverse[d, y - 1]
            inverse[d, y] = 1 / (diagonal[y] - side * lower[d, y])
    has_low = (np.arange(NK) > 0).astype(np.float64)
    has_high = (np.arange(NK) < NK - 1).astype(np.float64)
    parts = dict(
        send_up=send_up, send_down=send_down, take=np.stack([take_low, take_high]), near_low=near_low,
        near_high=near_high, own_low=own_low, own_high=own_high, lower=lower, inverse=inverse,
        has_low=has_low, has_high=has_high,
    )
    places, start = {}, 0
    for name, value in parts.items():
        places[name] = start
        start += value.size
    return np.concatenate([value.reshape(-1) for value in parts.values()]), places


def split(value):
    high = value.astype(BF16)
    low = (value - high.astype(F32)).astype(BF16)
    return high, low


def dot(a, b, dims=((1,), (0,))):
    return lax.dot_general(a, b, (dims, ((), ())), preferred_element_type=F32)


def kernel(
    at_d, at_f,
    fields_hbm, jac_hbm, inflow_hbm, donors_hbm, receptors_hbm, table_hbm, dx_hbm, fx_hbm, dz_hbm, fz_hbm, out,
    fields, jac, inflow, donors, receptors, table, dx, fx, dz, fz, load_sem,
    u0, sel, place, ts, tr, u, pu, v, q, pq, gx_, gz_, pp, ps, sb,
    outlet, inlet, inlet_rows, patch_s, patch_r,
    phi_d, col_d, gam_d, got_d, phi_f, col_f, gam_f, got_f, edge_d, edge_f, planes_d, everyone_d, planes_f, everyone_f,
    du, pdu, dv, planes_x, everyone_x, edge_x,
    tile_ss, tile_rs, u_ss, u_rs, q_ss, q_rs, s_ss, s_rs,
    d1_ss, d1_rs, d2_ss, d2_rs, f1_ss, f1_rs, f2_ss, f2_rs, dh_ss, dh_rs, fh_ss, fh_rs, in_ss, in_rs, patch_ss, patch_rs,
    du_ss, du_rs, x_ss, x_rs,
):
    sect = lax.axis_index("sect")
    g = lax.axis_index("gx")
    k = lax.axis_index("yz")

    def along_gx(j):
        return lax.rem(g + j, NG)

    def along_yz(j):
        return lax.rem(k + j, NK)

    def from_yz(j):
        return lax.rem(k + NK - j, NK)

    is_outlet = jnp.logical_and(sect == 0, g == 0)
    is_inlet = jnp.logical_and(sect == 1, g == 0)

    barrier = pltpu.get_barrier_semaphore()

    @pl.loop(1, NG)
    def _(j):
        pl.semaphore_signal(barrier, inc=1, device_id={"gx": along_gx(j)}, device_id_type=MESH)

    @pl.loop(1, NK)
    def _(j):
        pl.semaphore_signal(barrier, inc=1, device_id={"yz": along_yz(j)}, device_id_type=MESH)

    @pl.when(is_inlet)
    def _():
        pl.semaphore_signal(barrier, inc=1, device_id={"sect": 0}, device_id_type=MESH)

    pairs = (
        (fields_hbm, fields), (donors_hbm, donors), (receptors_hbm, receptors), (inflow_hbm, inflow),
        (jac_hbm, jac), (table_hbm, table), (dx_hbm, dx), (dz_hbm, dz), (fz_hbm, fz), (fx_hbm, fx),
    )
    loads = [pltpu.make_async_copy(source, target, load_sem.at[i]) for i, (source, target) in enumerate(pairs)]
    for load in loads:
        load.start()
    loads[0].wait()

    mine = pl.ds(pl.multiple_of(k * CY, CY), CY)

    def inflow_copy():
        return pltpu.make_async_remote_copy(
            outlet, inlet.at[mine], in_ss.at[0], in_rs.at[0], device_id={"sect": 1}, device_id_type=MESH,
        )

    def inlet_copies():
        whole = inlet.at[0 : NY - CY]
        return pltpu.make_async_remote_copy(
            whole, whole, in_ss.at[1], in_rs.at[1], device_id={"yz": along_yz(1)}, device_id_type=MESH,
        )

    @pl.when(is_outlet)
    def _():
        for y in range(CY):
            for f in range(5):
                outlet[y : y + 1, f * CZ : (f + 1) * CZ] = fields[0, f, CX - 1 : CX, y * CZ : (y + 1) * CZ]

        pl.semaphore_wait(barrier, NG + NK - 1)
        inflow_copy().start()

    for y in range(CY):
        for f in range(5):
            u0[y, f] = fields[0, f, :, y * CZ : (y + 1) * CZ]

    @pl.when(is_inlet)
    def _():
        for y in range(CY):
            for f in range(5):
                u0[y, f, 0:1, :] = jnp.zeros((1, CZ), F32)

    offset = lax.broadcasted_iota(jnp.int32, (8, CZ), 1) - lax.broadcasted_iota(jnp.int32, (8, CZ), 0)
    loads[1].wait()

    @pl.loop(0, SLOTS // 2)
    def _(j):
        for b in range(2):
            rows = []
            for e in range(2):
                slot = 2 * j + e
                first = jnp.where(donors[0, 0, 1, 0, slot] == b, donors[0, 0, 2, 0, slot], -1000)
                hit = jnp.logical_or(offset == first, offset == first + 1)
                rows.append(jnp.where(hit, 0.5, 0.0))
            sel[b, pl.ds(pl.multiple_of(16 * j, 16), 16), :] = jnp.concatenate(rows, axis=0).astype(BF16)

    payload = None
    for b in range(2):
        lines = jnp.concatenate([u0[8 * b : 8 * b + 8].reshape(320, CZ), jnp.zeros((64, CZ), F32)], axis=0)
        for part in split(lines):
            term = dot(sel[b], part, ((1,), (1,)))
            payload = term if payload is None else payload + term
    ts[:, 0:32, :] = payload[:, 0:256].reshape(NG, 32, 256)
    rest = payload[:, 256:384].reshape(NG, 4, 8, 128)
    left = lax.broadcasted_iota(jnp.int32, (NG, 8, 128), 2) < 64
    for e in range(2):
        moved = pltpu.roll(rest[:, 2 * e + 1].reshape(NG * 8, 128), 64, 1).reshape(NG, 8, 128)
        ts[:, 32:40, 128 * e : 128 * e + 128] = jnp.where(left, rest[:, 2 * e], moved)

    @pl.when(jnp.logical_not(is_outlet))
    def _():
        pl.semaphore_wait(barrier, NG + NK - 2)

    leaving = []
    coming = {}

    def batch(name, source, target, send, receive):
        whole = pltpu.make_async_remote_copy(
            source, target, send, receive, device_id={"gx": along_gx(1)}, device_id_type=MESH
        )
        leaving.append(whole.wait_send)
        coming[name] = whole.wait_recv

    def arrive(name):
        coming.pop(name)()

    for j in range(1, NG):
        pltpu.make_async_remote_copy(
            ts.at[along_gx(j)], tr.at[g], tile_ss.at[0], tile_rs.at[0],
            device_id={"gx": along_gx(j)}, device_id_type=MESH,
        ).start()
    batch("tiles", ts.at[1:NG], tr.at[1:NG], tile_ss.at[0], tile_rs.at[0])

    tr[g] = ts[g]

    @pl.when(is_inlet)
    def _():
        inflow_copy().wait_recv()
        for j in INLET_ORDER:
            pltpu.make_async_remote_copy(
                inlet.at[mine], inlet.at[mine], in_ss.at[1], in_rs.at[1],
                device_id={"yz": along_yz(j)}, device_id_type=MESH,
            ).start()

    loads[2].wait()

    def place_row(j, counts):
        counts = list(counts)
        for t in range(2):
            rows = []
            for e in range(2):
                goal = (receptors[2 * j + e] - 32 * t) * 8
                one = jnp.where(offset == goal, 1.0, 0.0)
                counts[t] = counts[t] + one
                rows.append(one)
            place[t, pl.ds(pl.multiple_of(16 * j, 16), 16), :] = jnp.concatenate(rows, axis=0).astype(BF16)
        return tuple(counts)

    counts = lax.fori_loop(0, SLOTS // 2, place_row, (jnp.zeros((8, CZ), F32),) * 2)

    loads[3].wait()

    def patch_copy(j):
        return pltpu.make_async_remote_copy(
            patch_s.at[j], patch_r, patch_ss.at[j], patch_rs.at[0], device_id={"gx": j}, device_id_type=MESH,
        )

    arrive("tiles")

    main = tr[:, 0:32, :].reshape(512, 256)
    rest = []
    for e in range(2):
        two = tr[:, 32:40, 128 * e : 128 * e + 128]
        rest += [two, pltpu.roll(two.reshape(NG * 8, 128), 64, 1).reshape(NG, 8, 128)]
    rest = jnp.stack(rest, axis=1).reshape(512, 128)
    halves_of = [split(main), split(rest)]
    for t in range(2):
        total = jnp.concatenate(
            [
                dot(high, place[t], ((0,), (0,))) + dot(low, place[t], ((0,), (0,)))
                for high, low in halves_of
            ],
            axis=0,
        )
        hits = jnp.sum(counts[t], axis=0, keepdims=True)
        scale = (1.0 / jnp.maximum(hits, 1.0)).reshape(1, 1, 1, CZ)
        mean = total[:320].reshape(8, 5, 8, CZ) * scale
        value = jnp.where(hits.reshape(1, 1, 1, CZ) > 0, mean, u0[8 * t : 8 * t + 8])
        for f in range(5):
            u[f, 8 * t : 8 * t + 8] = value[:, f]

    def start_all(name, source, target, send, receive, lo, hi, at):
        for j in range(1, NG):
            pltpu.make_async_remote_copy(
                source.at[lo:hi, along_gx(j)], target.at[lo:hi, g], send.at[at], receive.at[at],
                device_id={"gx": along_gx(j)}, device_id_type=MESH,
            ).start()
        batch((name, at), source.at[lo:hi, 1:NG], target.at[lo:hi, 1:NG], send.at[at], receive.at[at])
        target[lo:hi, g] = source[lo:hi, g]

    loads[4].wait()
    loads[5].wait()

    def mix(d, f, h):
        return jac[f, d, h] * (-SEGMENT_STEP)

    @pl.loop(0, CY)
    def _(y):
        cells = [u[h, y] for h in range(5)]
        for f in range(5):
            value = mix(1, f, 0) * cells[0]
            for h in range(1, 5):
                value += mix(1, f, h) * cells[h]
            v[f, y] = value

    def halo(operator, i):
        name, source, edge, reach = operator["name"], operator["source"], operator["edge"], operator["reach"]
        send, receive = operator["halo"]
        lo, hi = GROUPS[i]
        pltpu.make_async_remote_copy(
            source.at[lo:hi, CY - reach : CY], edge.at[lo:hi, 0:reach], send.at[i], receive.at[i],
            device_id={"yz": along_yz(1)}, device_id_type=MESH,
        ).start()
        pltpu.make_async_remote_copy(
            source.at[lo:hi, 0:reach], edge.at[lo:hi, reach : 2 * reach], send.at[i], receive.at[i],
            device_id={"yz": from_yz(1)}, device_id_type=MESH,
        ).start()
        batch((name, "halo", i), source.at[lo:hi, 0 : 2 * reach], edge.at[lo:hi], send.at[i], receive.at[i])

    def hops(name, source, target, sems, i):
        send, receive = sems
        for j in range(1, NK):
            pltpu.make_async_remote_copy(
                source.at[i, along_yz(j)], target.at[i, k], send.at[i], receive.at[i],
                device_id={"yz": along_yz(j)}, device_id_type=MESH,
            ).start()
        batch((name, i), source.at[i, 1:NK], target.at[i, 1:NK], send.at[i], receive.at[i])
        target[i, k] = source[i, k]

    def first_half(operator, i):
        source, phi, places = operator["source"], operator["phi"], operator["places"]
        lo, hi = GROUPS[i]
        direct = i in operator["direct"]
        planes, everyone = operator["planes"], operator["everyone"]
        for f in range(lo, hi if direct else lo + 2):
            for half in range(2):
                tile = (f - lo) * 2 + half
                if f >= hi:
                    phi[i, tile] = jnp.zeros((8, 128), F32)
                    phi[i, 4 + tile] = jnp.zeros((8, 128), F32)
                    continue
                up = down = None
                for y in range(CY):
                    row = source[f, y, :, 128 * half : 128 * half + 128]
                    a = table[places["send_up"] + k * CY + y] * row
                    b = table[places["send_down"] + k * CY + y] * row
                    up, down = (a, b) if up is None else (up + a, down + b)
                if direct:
                    planes[0, f, :, 128 * half : 128 * half + 128] = up
                    planes[1, f, :, 128 * half : 128 * half + 128] = down
                else:
                    phi[i, tile] = up
                    phi[i, 4 + tile] = down

        if direct:
            send, receive = operator["first"]
            for j in range(1, NK):
                peer = along_yz(j)
                pltpu.make_async_remote_copy(
                    planes.at[lax.div(k - peer + NK, NK), lo:hi], everyone.at[k, lo:hi], send.at[i], receive.at[i],
                    device_id={"yz": peer}, device_id_type=MESH,
                ).start()
            whole = everyone.at[1:NK, lo:hi]
            batch((operator["name"] + "2", i), whole, whole, send.at[i], receive.at[i])
            halo(operator, i)
            return

        hops(operator["name"] + "1", phi, operator["col"], operator["first"], i)
        halo(operator, i)

    def second_half(operator, i):
        if i in operator["direct"]:
            return
        col, gam, places = operator["col"], operator["gam"], operator["places"]
        arrive((operator["name"] + "1", i))
        upward = lax.div(k, 4)
        tiles = [col[i, s] for s in range(NK)]

        @pl.loop(0, NK)
        def _(d):
            base = places["take"] + upward * (NK * NK) + d * NK
            total = table[base] * tiles[0]
            for s in range(1, NK):
                total += table[base + s] * tiles[s]
            gam[i, d] = total

        hops(operator["name"] + "2", gam, operator["got"], operator["second"], i)

    def y_lines(operator, i, stencil, side, store):
        source, got, edge, reach, places = (
            operator["source"], operator["got"], operator["edge"], operator["reach"], operator["places"],
        )
        lo, hi = GROUPS[i]
        if operator["name"] == "f":
            arrive(("f", "halo", i))
            arrive(("f2", i))

        def entry(name, count, index=0):
            return table[places[name] + k * count + index]

        for f in range(lo, hi):
            for half in range(2):
                lanes = slice(128 * half, 128 * half + 128)
                tile = (f - lo) * 2 + half
                if i in operator["direct"]:
                    from_low = from_high = None
                    for j in range(1, NK):
                        block = along_yz(j)
                        plane = operator["everyone"][block, f, :, lanes]
                        a = table[places["take"] + k * NK + block] * plane
                        b = table[places["take"] + NK * NK + k * NK + block] * plane
                        from_low, from_high = (a, b) if from_low is None else (from_low + a, from_high + b)
                else:
                    from_low = got[i, tile]
                    from_high = got[i, 4 + tile]
                rows = [edge[f, h, :, lanes] * entry("has_low", 1) for h in range(reach)]
                rows += [source[f, y, :, lanes] for y in range(CY)]
                rows += [edge[f, reach + h, :, lanes] * entry("has_high", 1) for h in range(reach)]
                for h in range(reach):
                    from_low += entry("near_low", reach, h) * rows[h] + entry("own_low", reach, h) * rows[reach + h]
                    from_high += (
                        entry("near_high", reach, h) * rows[reach + CY + h]
                        + entry("own_high", reach, h) * rows[CY + h]
                    )
                moves = {}
                for move, factor in stencil:
                    moves.setdefault(abs(move), {})[move] = factor
                values = []
                for y in range(CY):
                    at = reach + y
                    value = None
                    for move, factors in moves.items():
                        if move == 0:
                            term = np.float32(factors[0]) * rows[at]
                        elif factors[move] == factors[-move]:
                            term = np.float32(factors[move]) * (rows[at + move] + rows[at - move])
                        else:
                            term = np.float32(factors[move]) * (rows[at + move] - rows[at - move])
                        value = term if value is None else value + term
                    if y == 0:
                        value = value + from_low
                    if y == CY - 1:
                        value = value + from_high
                    if y > 0:
                        value = value - entry("lower", CY, y) * values[-1]
                    values.append(value)
                last = None
                for y in range(CY - 1, -1, -1):
                    value = values[y] if last is None else values[y] - np.float32(side) * last
                    last = value * entry("inverse", CY, y)
                    store(y, f, half, last)

    deriv = dict(
        name="d", source=v, phi=phi_d, col=col_d, gam=gam_d, got=got_d, edge=edge_d, reach=2, places=at_d,
        first=(d1_ss, d1_rs), second=(d2_ss, d2_rs), halo=(dh_ss, dh_rs),
        direct=DIRECT_DERIV, planes=planes_d, everyone=everyone_d,
    )
    smooth = dict(
        name="f", source=sb, phi=phi_f, col=col_f, gam=gam_f, got=got_f, edge=edge_f, reach=5, places=at_f,
        first=(f1_ss, f1_rs), second=(f2_ss, f2_rs), halo=(fh_ss, fh_rs),
        direct=DIRECT_FILTER, planes=planes_f, everyone=everyone_f,
    )

    def store_q(y, f, half, value):
        q[f, y, :, 128 * half : 128 * half + 128] = value

    def store_out(y, f, half, value):
        start = y * CZ + 128 * half
        out[0, f, :, start : start + 128] = value

    count = len(GROUPS)
    def q_lines(i):
        y_lines(deriv, i, DERIV_STENCIL, SIDE_DERIV, store_q)
        start_all("q", q, pq, q_ss, q_rs, *GROUPS[i], i)

    before = len(leaving)
    for i in range(count):
        first_half(deriv, i)
    early = len(leaving)

    @pl.when(is_inlet)
    def _():
        inlet_rows[...] = jnp.zeros((2, 64, CZ), F32)
        inlet_copies().wait_recv()
        for y in range(CY):
            row = inlet[pl.ds(inflow[y], 1), :]
            for f in range(5):
                at = (y % 8) * 8 + f
                inlet_rows[y // 8, at : at + 1, :] = row[:, f * CZ : (f + 1) * CZ]
        total = None
        for b in range(2):
            lines = jnp.concatenate([inlet_rows[b], jnp.zeros((64, CZ), F32)], axis=0)
            for part in split(lines):
                term = dot(sel[b], part, ((1,), (1,)))
                total = term if total is None else total + term
        total = total.reshape(NG, 2, 16, 128)
        moved = pltpu.roll(total[:, 1].reshape(NG * 16, 128), 64, 1).reshape(NG, 16, 128)
        side = lax.broadcasted_iota(jnp.int32, (NG, 16, 128), 2) < 64
        patch_s[...] = jnp.where(side, total[:, 0], moved)

        @pl.loop(1, NG)
        def _(j):
            patch_copy(j).start()

        patch_r[...] = patch_s[0]

    start_all("u", u, pu, u_ss, u_rs, 0, 5, 0)
    def plane_copy(j):
        return pltpu.make_async_remote_copy(
            du.at[along_gx(j)], pdu.at[g], du_ss.at[0], du_rs.at[0],
            device_id={"gx": along_gx(j)}, device_id_type=MESH,
        )

    def plane_copies():
        return pltpu.make_async_remote_copy(
            du.at[1:NG], pdu.at[1:NG], du_ss.at[0], du_rs.at[0], device_id={"gx": along_gx(1)}, device_id_type=MESH,
        )

    @pl.when(sect == 1)
    def _():
        @pl.when(g > 0)
        def _():
            patch_copy(g).wait_recv()

        packed = patch_r[...]
        high, low = split(jnp.concatenate([packed, pltpu.roll(packed, 64, 1)], axis=0))
        for t in range(2):
            rows = place[t, 0:32, :]
            total = dot(high, rows, ((0,), (0,))) + dot(low, rows, ((0,), (0,)))
            hits = jnp.sum(counts[t], axis=0, keepdims=True)
            value = (total[:64] * (1.0 / jnp.maximum(hits, 1.0))).reshape(8, 8, CZ)
            du[8 * t : 8 * t + 8] = value

            @pl.when(g == 0)
            def _():
                taken = hits.reshape(1, 1, CZ) > 0
                du[8 * t : 8 * t + 8] = jnp.where(taken, value, inlet_rows[t].reshape(8, 8, CZ))

        row_of = lax.broadcasted_iota(jnp.int32, (8, CZ), 0)
        factors = []
        for h in range(5):
            factor = jnp.zeros((8, CZ), F32)
            for f in range(5):
                factor = jnp.where(row_of == f, mix(1, f, h), factor)
            factors.append(factor)
        for y in range(CY):
            value = factors[0] * du[y, 0:1, :]
            for h in range(1, 5):
                value += factors[h] * du[y, h : h + 1, :]
            dv[y] = value
        up = down = None
        for y in range(CY):
            a = table[at_d["send_up"] + k * CY + y] * dv[y]
            b = table[at_d["send_down"] + k * CY + y] * dv[y]
            up, down = (a, b) if up is None else (up + a, down + b)
        planes_x[0] = up
        planes_x[1] = down
        for j in range(1, NK):
            peer = along_yz(j)
            pltpu.make_async_remote_copy(
                planes_x.at[lax.div(k - peer + NK, NK)], everyone_x.at[k], x_ss.at[0], x_rs.at[0],
                device_id={"yz": peer}, device_id_type=MESH,
            ).start()
        pltpu.make_async_remote_copy(
            dv.at[CY - 2 : CY], edge_x.at[0:2], x_ss.at[1], x_rs.at[1],
            device_id={"yz": along_yz(1)}, device_id_type=MESH,
        ).start()
        pltpu.make_async_remote_copy(
            dv.at[0:2], edge_x.at[2:4], x_ss.at[1], x_rs.at[1],
            device_id={"yz": from_yz(1)}, device_id_type=MESH,
        ).start()

    def extra_copies():
        return [
            pltpu.make_async_remote_copy(
                whole, whole, x_ss.at[i], x_rs.at[i], device_id={"yz": along_yz(1)}, device_id_type=MESH,
            )
            for i, whole in enumerate((everyone_x.at[1:NK], edge_x))
        ]

    for wait in leaving[before:early]:
        wait()
    del leaving[before:early]

    for i in range(count):
        arrive(("d", "halo", i))
        arrive(("d2", i))

    @pl.when(sect == 1)
    def _():
        @pl.loop(1, NG)
        def _(j):
            plane_copy(j).start()

        pdu[g] = du[g]
        for y in range(CY):
            for f in range(5):
                v[f, y, 0:1, :] = v[f, y, 0:1, :] + dv[y, f : f + 1, :]
        for copy in extra_copies():
            copy.wait_recv()
        for f in range(5):
            for h in range(4):
                edge_d[f, h, 0:1, :] = edge_d[f, h, 0:1, :] + edge_x[h, f : f + 1, :]
            for j in range(1, NK):
                block = along_yz(j)
                everyone_d[block, f, 0:1, :] = everyone_d[block, f, 0:1, :] + everyone_x[block, f : f + 1, :]

    for i in range(count):
        second_half(deriv, i)
    for i in range(count):
        q_lines(i)

    for load in loads[6:]:
        load.wait()
    arrive(("u", 0))

    @pl.when(sect == 1)
    def _():
        plane_copies().wait_recv()

        @pl.loop(0, NG)
        def _(r):
            for f in range(5):
                pu[f, r, 0:1, :] = pu[f, r, 0:1, :] + pdu[r, f : f + 1, :]

    for f in range(5):
        high, low = split(pu[f].reshape(NX, CZ))
        gx_[f] = dot(dx[sect, 0], high) + dot(dx[sect, 0], low) + dot(dx[sect, 1], high)
        gz_[f] = dot(high, dz[0]) + dot(low, dz[0]) + dot(high, dz[1])

    @pl.loop(0, 5)
    def _(f):
        value = pu[f].reshape(NX, CZ)
        for h in range(5):
            value += mix(0, f, h) * gx_[h]
            value += mix(2, f, h) * gz_[h]
        pp[f] = value

    for i in range(count):
        lo, hi = GROUPS[i]
        arrive(("q", i))
        for f in range(lo, hi):
            high, low = split(pp[f] + pq[f].reshape(NX, CZ))
            value = dot(high, fz[0]) + dot(low, fz[0]) + dot(high, fz[1])
            high, low = split(value)
            value = dot(fx[sect, 0], high) + dot(fx[sect, 0], low) + dot(fx[sect, 1], high)
            ps[f] = value.reshape(NG, CX, CZ)
        start_all("s", ps, sb, s_ss, s_rs, lo, hi, i)

    for i in range(count):
        arrive(("s", i))
        first_half(smooth, i)
        if i > 0:
            second_half(smooth, i - 1)
    for i in range(count):
        y_lines(smooth, i, FILTER_STENCIL, SIDE_FILTER, store_out)

    for wait in leaving:
        wait()

    @pl.when(sect == 1)
    def _():
        plane_copies().wait_send()
        for copy in extra_copies():
            copy.wait_send()

    @pl.when(is_outlet)
    def _():
        inflow_copy().wait_send()

    @pl.when(is_inlet)
    def _():
        inlet_copies().wait_send()

        @pl.loop(1, NG)
        def _(j):
            patch_copy(j).wait_send()


def per_device(fields, jacobians, inflow_map, donor_tiles, receptor_tiles):
    table_d, places_d = block_table(DERIV_STENCIL, SIDE_DERIV)
    table_f, places_f = block_table(FILTER_STENCIL, SIDE_FILTER)
    places_f = {name: start + table_d.size for name, start in places_f.items()}
    table = np.concatenate([table_d, table_f]).astype(np.float32)
    dx = np.stack([halves(line_matrix(NX, p, DERIV_STENCIL, SIDE_DERIV)) for p in (True, False)])
    fx = np.stack([halves(line_matrix(NX, p, FILTER_STENCIL, SIDE_FILTER)) for p in (True, False)])
    dz = halves(line_matrix(CZ, True, DERIV_STENCIL, SIDE_DERIV).T)
    fz = halves(line_matrix(CZ, True, FILTER_STENCIL, SIDE_FILTER).T)
    block = (5, CY, CX, CZ)
    count = len(GROUPS)

    def buffer(*shape, kind=F32):
        return pltpu.VMEM(shape, kind)

    def scalars(*shape, kind=jnp.int32):
        return pltpu.SMEM(shape, kind)

    def dma(length):
        return pltpu.SemaphoreType.DMA((length,))

    tiles = [buffer(count, NK, 8, 128)] * 4
    inputs = (
        fields, jnp.transpose(jacobians, (1, 0, 2)), inflow_map, jnp.transpose(donor_tiles, (0, 1, 4, 2, 3)),
        receptor_tiles.reshape(SLOTS), jnp.asarray(table), jnp.asarray(dx), jnp.asarray(fx), jnp.asarray(dz),
        jnp.asarray(fz),
    )
    return pl.pallas_call(
        functools.partial(kernel, places_d, places_f),
        out_shape=jax.ShapeDtypeStruct(fields.shape, F32),
        in_specs=[pl.BlockSpec(memory_space=HBM)] * len(inputs),
        out_specs=pl.BlockSpec(memory_space=pltpu.VMEM),
        scratch_shapes=[
            buffer(*fields.shape), scalars(5, 3, 5, kind=F32), scalars(16), scalars(1, 1, 3, 1, SLOTS), scalars(SLOTS),
            scalars(table.size, kind=F32),
            buffer(*dx.shape, kind=BF16), buffer(*fx.shape, kind=BF16),
            buffer(*dz.shape, kind=BF16), buffer(*fz.shape, kind=BF16), dma(10),
            buffer(CY, 5, CX, CZ),
            buffer(2, 512, CZ, kind=BF16), buffer(2, 512, CZ, kind=BF16),
            buffer(NG, 40, 256), buffer(NG, 40, 256),
            buffer(*block), buffer(*block), buffer(*block), buffer(*block), buffer(*block),
            buffer(5, NX, CZ), buffer(5, NX, CZ), buffer(5, NX, CZ),
            buffer(*block), buffer(*block),
            buffer(CY, 5 * CZ), buffer(NY, 5 * CZ), buffer(2, 64, CZ), buffer(NG, 16, 128), buffer(16, 128),
            *tiles, *tiles,
            buffer(5, 4, CX, CZ), buffer(5, 10, CX, CZ),
            *([buffer(2, 5, CX, CZ), buffer(NK, 5, CX, CZ)] * 2),
            buffer(CY, 8, CZ), buffer(NG, 8, CZ), buffer(CY, 8, CZ), buffer(2, 8, CZ), buffer(NK, 8, CZ), buffer(4, 8, CZ),
            *([dma(1)] * 4), *([dma(count)] * 16), dma(2), dma(2), dma(NG), dma(1), dma(1), dma(1), dma(2), dma(2),
        ],
        compiler_params=pltpu.CompilerParams(
            collective_id=0, has_side_effects=True, vmem_limit_bytes=VMEM_MIB * 1024 * 1024
        ),
        name="segment",
    )(*inputs)


def solution(mesh):
    in_specs = (
        P("sect", None, "gx", "yz"),
        P(),
        P("yz"),
        P("sect", "gx", "yz", None, None),
        P("sect", "gx", "yz", None),
    )
    out_specs = P("sect", None, "gx", "yz")
    return jax.shard_map(
        per_device, mesh=mesh, in_specs=in_specs, out_specs=out_specs, check_vma=False
    )
```

```python
import functools

import jax
import jax.numpy as jnp
import ml_dtypes
import numpy as np
from jax import lax
from jax.experimental import pallas as pl
from jax.experimental.pallas import tpu as pltpu
from jax.sharding import PartitionSpec as P

MESH = pl.DeviceIdType.MESH
HBM = pltpu.MemorySpace.HBM
F32 = jnp.float32
BF16 = jnp.bfloat16

CX = 8
CY = 16
CZ = 256
NG = 16
NK = 8
NX = 128
NY = 128
SLOTS = 64
GROUPS = ((0, 2), (2, 4), (4, 5))
VMEM_MIB = 62
GX_ORDER = (8, 4, 12, 6, 10, 2, 14, 7, 9, 5, 11, 3, 13, 1, 15)
INLET_ORDER = (4, 3, 5, 2, 6, 1, 7)
DIRECT_FILTER = (2,)

SEGMENT_STEP = 0.25
SIDE_DERIV = 1.0 / 3.0
SIDE_FILTER = 0.49


def filter_coeffs():
    side = SIDE_FILTER
    return [
        (193 + 126 * side) / 256,
        (105 + 302 * side) / 256,
        15 * (-1 + 2 * side) / 64,
        45 * (1 - 2 * side) / 512,
        5 * (-1 + 2 * side) / 256,
        (1 - 2 * side) / 512,
    ]


DERIV_STENCIL = ((1, 7.0 / 9.0), (-1, -7.0 / 9.0), (2, 1.0 / 36.0), (-2, -1.0 / 36.0))
FILTER_STENCIL = ((0, filter_coeffs()[0]),) + tuple(
    (sign * reach, filter_coeffs()[reach] / 2) for reach in range(1, 6) for sign in (1, -1)
)


def sides(length, periodic, stencil, side):
    left = np.eye(length)
    right = np.zeros((length, length))
    for row in range(length):
        for offset, factor in ((-1, side), (1, side)):
            if periodic or 0 <= row + offset < length:
                left[row, (row + offset) % length] += factor
        for offset, factor in stencil:
            if periodic or 0 <= row + offset < length:
                right[row, (row + offset) % length] += factor
    return left, right


def line_matrix(length, periodic, stencil, side):
    return np.linalg.solve(*sides(length, periodic, stencil, side))


def halves(matrix):
    value = np.asarray(matrix, np.float32)
    high = value.astype(ml_dtypes.bfloat16)
    low = (value - high.astype(np.float32)).astype(ml_dtypes.bfloat16)
    return np.stack([high, low])


def block_table(stencil, side):
    left, right = sides(NY, False, stencil, side)
    reach = max(offset for offset, _ in stencil)
    below = np.zeros((NK, NY))
    above = np.zeros((NK, NY))
    corner_low = np.zeros(NK)
    corner_high = np.zeros(NK)
    for d in range(NK):
        lo, hi = d * CY, (d + 1) * CY
        if d > 0:
            row = np.linalg.solve(left[:lo, :lo].T, np.eye(lo)[lo - 1])
            below[d] = -side * (row @ right[:lo])
            corner_low[d] = row[-1]
        if d < NK - 1:
            row = np.linalg.solve(left[hi:, hi:].T, np.eye(NY - hi)[0])
            above[d] = -side * (row @ right[hi:])
            corner_high[d] = row[0]
    send_up = np.zeros((NK, CY))
    send_down = np.zeros((NK, CY))
    for s in range(NK):
        cells = slice(s * CY, (s + 1) * CY)
        if s < NK - 1:
            value = below[min(s + 2, NK - 1)][cells]
            send_up[s] = value / np.abs(value).max()
        if s > 0:
            value = above[max(s - 2, 0)][cells]
            send_down[s] = value / np.abs(value).max()
    take_low = np.zeros((NK, NK))
    take_high = np.zeros((NK, NK))
    near_low = np.zeros((NK, reach))
    near_high = np.zeros((NK, reach))
    own_low = np.zeros((NK, reach))
    own_high = np.zeros((NK, reach))
    for d in range(NK):
        for s in range(d):
            value, unit = below[d][s * CY : (s + 1) * CY], send_up[s]
            core = unit[: CY - reach]
            take_low[d, s] = (value[: CY - reach] @ core) / (core @ core)
            if s == d - 1:
                near_low[d] = (value - take_low[d, s] * unit)[CY - reach :]
        for s in range(d + 1, NK):
            value, unit = above[d][s * CY : (s + 1) * CY], send_down[s]
            core = unit[reach:]
            take_high[d, s] = (value[reach:] @ core) / (core @ core)
            if s == d + 1:
                near_high[d] = (value - take_high[d, s] * unit)[:reach]
        own_low[d] = below[d][d * CY : d * CY + reach]
        own_high[d] = above[d][(d + 1) * CY - reach : (d + 1) * CY]
    lower = np.zeros((NK, CY))
    inverse = np.zeros((NK, CY))
    for d in range(NK):
        diagonal = np.ones(CY)
        diagonal[0] -= side**2 * corner_low[d]
        diagonal[-1] -= side**2 * corner_high[d]
        inverse[d, 0] = 1 / diagonal[0]
        for y in range(1, CY):
            lower[d, y] = side * inverse[d, y - 1]
            inverse[d, y] = 1 / (diagonal[y] - side * lower[d, y])
    has_low = (np.arange(NK) > 0).astype(np.float64)
    has_high = (np.arange(NK) < NK - 1).astype(np.float64)
    parts = dict(
        send_up=send_up, send_down=send_down, take=np.stack([take_low, take_high]), near_low=near_low,
        near_high=near_high, own_low=own_low, own_high=own_high, lower=lower, inverse=inverse,
        has_low=has_low, has_high=has_high,
    )
    places, start = {}, 0
    for name, value in parts.items():
        places[name] = start
        start += value.size
    return np.concatenate([value.reshape(-1) for value in parts.values()]), places


def split(value):
    high = value.astype(BF16)
    low = (value - high.astype(F32)).astype(BF16)
    return high, low


def dot(a, b, dims=((1,), (0,))):
    return lax.dot_general(a, b, (dims, ((), ())), preferred_element_type=F32)


def kernel(
    at_d, at_f,
    fields_hbm, jac_hbm, inflow_hbm, donors_hbm, receptors_hbm, table_hbm, dx_hbm, fx_hbm, dz_hbm, fz_hbm, out,
    fields, jac, inflow, donors, receptors, table, dx, fx, dz, fz, load_sem,
    u0, sel, place, ts, tr, u, pu, v, q, pq, gx_, gz_, pp, ps, sb,
    outlet, inlet, inlet_rows, patch_s, patch_r,
    phi_d, col_d, gam_d, got_d, phi_f, col_f, gam_f, got_f, edge_d, edge_f, planes_f, everyone_f,
    du, pdu, dv, planes_x, everyone_x, edge_x,
    tile_ss, tile_rs, u_ss, u_rs, q_ss, q_rs, s_ss, s_rs,
    d1_ss, d1_rs, d2_ss, d2_rs, f1_ss, f1_rs, f2_ss, f2_rs, dh_ss, dh_rs, fh_ss, fh_rs, in_ss, in_rs, patch_ss, patch_rs,
    du_ss, du_rs, x_ss, x_rs,
):
    sect = lax.axis_index("sect")
    g = lax.axis_index("gx")
    k = lax.axis_index("yz")

    def along_gx(j):
        return lax.rem(g + j, NG)

    def along_yz(j):
        return lax.rem(k + j, NK)

    def from_yz(j):
        return lax.rem(k + NK - j, NK)

    is_outlet = jnp.logical_and(sect == 0, g == 0)
    is_inlet = jnp.logical_and(sect == 1, g == 0)

    barrier = pltpu.get_barrier_semaphore()

    @pl.loop(1, NG)
    def _(j):
        pl.semaphore_signal(barrier, inc=1, device_id={"gx": along_gx(j)}, device_id_type=MESH)

    @pl.loop(1, NK)
    def _(j):
        pl.semaphore_signal(barrier, inc=1, device_id={"yz": along_yz(j)}, device_id_type=MESH)

    @pl.when(is_inlet)
    def _():
        pl.semaphore_signal(barrier, inc=1, device_id={"sect": 0}, device_id_type=MESH)

    pairs = (
        (fields_hbm, fields), (donors_hbm, donors), (receptors_hbm, receptors), (inflow_hbm, inflow),
        (jac_hbm, jac), (table_hbm, table), (dx_hbm, dx), (dz_hbm, dz), (fz_hbm, fz), (fx_hbm, fx),
    )
    loads = [pltpu.make_async_copy(source, target, load_sem.at[i]) for i, (source, target) in enumerate(pairs)]
    for load in loads:
        load.start()
    loads[0].wait()

    mine = pl.ds(pl.multiple_of(k * CY, CY), CY)

    def inflow_copy():
        return pltpu.make_async_remote_copy(
            outlet, inlet.at[mine], in_ss.at[0], in_rs.at[0], device_id={"sect": 1}, device_id_type=MESH,
        )

    def inlet_copies():
        whole = inlet.at[0 : NY - CY]
        return pltpu.make_async_remote_copy(
            whole, whole, in_ss.at[1], in_rs.at[1], device_id={"yz": along_yz(1)}, device_id_type=MESH,
        )

    @pl.when(is_outlet)
    def _():
        for y in range(CY):
            for f in range(5):
                outlet[y : y + 1, f * CZ : (f + 1) * CZ] = fields[0, f, CX - 1 : CX, y * CZ : (y + 1) * CZ]

        pl.semaphore_wait(barrier, NG + NK - 1)
        inflow_copy().start()

    for y in range(CY):
        for f in range(5):
            u0[y, f] = fields[0, f, :, y * CZ : (y + 1) * CZ]

    @pl.when(is_inlet)
    def _():
        for y in range(CY):
            for f in range(5):
                u0[y, f, 0:1, :] = jnp.zeros((1, CZ), F32)

    offset = lax.broadcasted_iota(jnp.int32, (8, CZ), 1) - lax.broadcasted_iota(jnp.int32, (8, CZ), 0)
    loads[1].wait()

    @pl.loop(0, SLOTS // 2)
    def _(j):
        for b in range(2):
            rows = []
            for e in range(2):
                slot = 2 * j + e
                first = jnp.where(donors[0, 0, 1, 0, slot] == b, donors[0, 0, 2, 0, slot], -1000)
                hit = jnp.logical_or(offset == first, offset == first + 1)
                rows.append(jnp.where(hit, 0.5, 0.0))
            sel[b, pl.ds(pl.multiple_of(16 * j, 16), 16), :] = jnp.concatenate(rows, axis=0).astype(BF16)

    payload = None
    for b in range(2):
        lines = jnp.concatenate([u0[8 * b : 8 * b + 8].reshape(320, CZ), jnp.zeros((64, CZ), F32)], axis=0)
        for part in split(lines):
            term = dot(sel[b], part, ((1,), (1,)))
            payload = term if payload is None else payload + term
    ts[:, 0:32, :] = payload[:, 0:256].reshape(NG, 32, 256)
    rest = payload[:, 256:384].reshape(NG, 4, 8, 128)
    left = lax.broadcasted_iota(jnp.int32, (NG, 8, 128), 2) < 64
    for e in range(2):
        moved = pltpu.roll(rest[:, 2 * e + 1].reshape(NG * 8, 128), 64, 1).reshape(NG, 8, 128)
        ts[:, 32:40, 128 * e : 128 * e + 128] = jnp.where(left, rest[:, 2 * e], moved)

    @pl.when(jnp.logical_not(is_outlet))
    def _():
        pl.semaphore_wait(barrier, NG + NK - 2)

    leaving = []
    coming = {}

    def batch(name, source, target, send, receive):
        whole = pltpu.make_async_remote_copy(
            source, target, send, receive, device_id={"gx": along_gx(1)}, device_id_type=MESH
        )
        leaving.append(whole.wait_send)
        coming[name] = whole.wait_recv

    def arrive(name):
        coming.pop(name)()

    for j in GX_ORDER:
        pltpu.make_async_remote_copy(
            ts.at[along_gx(j)], tr.at[g], tile_ss.at[0], tile_rs.at[0],
            device_id={"gx": along_gx(j)}, device_id_type=MESH,
        ).start()
    batch("tiles", ts.at[1:NG], tr.at[1:NG], tile_ss.at[0], tile_rs.at[0])

    tr[g] = ts[g]

    @pl.when(is_inlet)
    def _():
        inflow_copy().wait_recv()
        for j in INLET_ORDER:
            pltpu.make_async_remote_copy(
                inlet.at[mine], inlet.at[mine], in_ss.at[1], in_rs.at[1],
                device_id={"yz": along_yz(j)}, device_id_type=MESH,
            ).start()

    loads[2].wait()

    def place_row(j, counts):
        counts = list(counts)
        for t in range(2):
            rows = []
            for e in range(2):
                goal = (receptors[2 * j + e] - 32 * t) * 8
                one = jnp.where(offset == goal, 1.0, 0.0)
                counts[t] = counts[t] + one
                rows.append(one)
            place[t, pl.ds(pl.multiple_of(16 * j, 16), 16), :] = jnp.concatenate(rows, axis=0).astype(BF16)
        return tuple(counts)

    counts = lax.fori_loop(0, SLOTS // 2, place_row, (jnp.zeros((8, CZ), F32),) * 2)

    loads[3].wait()

    def patch_copy(j):
        return pltpu.make_async_remote_copy(
            patch_s.at[j], patch_r, patch_ss.at[j], patch_rs.at[0], device_id={"gx": j}, device_id_type=MESH,
        )

    arrive("tiles")

    main = tr[:, 0:32, :].reshape(512, 256)
    rest = []
    for e in range(2):
        two = tr[:, 32:40, 128 * e : 128 * e + 128]
        rest += [two, pltpu.roll(two.reshape(NG * 8, 128), 64, 1).reshape(NG, 8, 128)]
    rest = jnp.stack(rest, axis=1).reshape(512, 128)
    halves_of = [split(main), split(rest)]
    for t in range(2):
        total = jnp.concatenate(
            [
                dot(high, place[t], ((0,), (0,))) + dot(low, place[t], ((0,), (0,)))
                for high, low in halves_of
            ],
            axis=0,
        )
        hits = jnp.sum(counts[t], axis=0, keepdims=True)
        scale = (1.0 / jnp.maximum(hits, 1.0)).reshape(1, 1, 1, CZ)
        mean = total[:320].reshape(8, 5, 8, CZ) * scale
        value = jnp.where(hits.reshape(1, 1, 1, CZ) > 0, mean, u0[8 * t : 8 * t + 8])
        for f in range(5):
            u[f, 8 * t : 8 * t + 8] = value[:, f]

    def start_all(name, source, target, send, receive, lo, hi, at):
        for j in GX_ORDER:
            pltpu.make_async_remote_copy(
                source.at[lo:hi, along_gx(j)], target.at[lo:hi, g], send.at[at], receive.at[at],
                device_id={"gx": along_gx(j)}, device_id_type=MESH,
            ).start()
        batch((name, at), source.at[lo:hi, 1:NG], target.at[lo:hi, 1:NG], send.at[at], receive.at[at])
        target[lo:hi, g] = source[lo:hi, g]

    loads[4].wait()
    loads[5].wait()

    def mix(d, f, h):
        return jac[f, d, h] * (-SEGMENT_STEP)

    @pl.loop(0, CY)
    def _(y):
        cells = [u[h, y] for h in range(5)]
        for f in range(5):
            value = mix(1, f, 0) * cells[0]
            for h in range(1, 5):
                value += mix(1, f, h) * cells[h]
            v[f, y] = value

    def halo(operator, i):
        name, source, edge, reach = operator["name"], operator["source"], operator["edge"], operator["reach"]
        send, receive = operator["halo"]
        lo, hi = GROUPS[i]
        pltpu.make_async_remote_copy(
            source.at[lo:hi, CY - reach : CY], edge.at[lo:hi, 0:reach], send.at[i], receive.at[i],
            device_id={"yz": along_yz(1)}, device_id_type=MESH,
        ).start()
        pltpu.make_async_remote_copy(
            source.at[lo:hi, 0:reach], edge.at[lo:hi, reach : 2 * reach], send.at[i], receive.at[i],
            device_id={"yz": from_yz(1)}, device_id_type=MESH,
        ).start()
        batch((name, "halo", i), source.at[lo:hi, 0 : 2 * reach], edge.at[lo:hi], send.at[i], receive.at[i])

    def hops(name, source, target, sems, i):
        send, receive = sems
        for j in range(1, NK):
            pltpu.make_async_remote_copy(
                source.at[i, along_yz(j)], target.at[i, k], send.at[i], receive.at[i],
                device_id={"yz": along_yz(j)}, device_id_type=MESH,
            ).start()
        batch((name, i), source.at[i, 1:NK], target.at[i, 1:NK], send.at[i], receive.at[i])
        target[i, k] = source[i, k]

    def first_half(operator, i):
        source, phi, places = operator["source"], operator["phi"], operator["places"]
        lo, hi = GROUPS[i]
        direct = i in operator["direct"]
        planes, everyone = operator["planes"], operator["everyone"]
        for f in range(lo, hi if direct else lo + 2):
            for half in range(2):
                tile = (f - lo) * 2 + half
                if f >= hi:
                    phi[i, tile] = jnp.zeros((8, 128), F32)
                    phi[i, 4 + tile] = jnp.zeros((8, 128), F32)
                    continue
                up = down = None
                for y in range(CY):
                    row = source[f, y, :, 128 * half : 128 * half + 128]
                    a = table[places["send_up"] + k * CY + y] * row
                    b = table[places["send_down"] + k * CY + y] * row
                    up, down = (a, b) if up is None else (up + a, down + b)
                if direct:
                    planes[0, f, :, 128 * half : 128 * half + 128] = up
                    planes[1, f, :, 128 * half : 128 * half + 128] = down
                else:
                    phi[i, tile] = up
                    phi[i, 4 + tile] = down

        if direct:
            send, receive = operator["first"]
            for j in range(1, NK):
                peer = along_yz(j)
                pltpu.make_async_remote_copy(
                    planes.at[lax.div(k - peer + NK, NK), lo:hi], everyone.at[k, lo:hi], send.at[i], receive.at[i],
                    device_id={"yz": peer}, device_id_type=MESH,
                ).start()
            whole = everyone.at[1:NK, lo:hi]
            batch((operator["name"] + "2", i), whole, whole, send.at[i], receive.at[i])
            halo(operator, i)
            return

        hops(operator["name"] + "1", phi, operator["col"], operator["first"], i)
        halo(operator, i)

    def second_half(operator, i):
        if i in operator["direct"]:
            return
        col, gam, places = operator["col"], operator["gam"], operator["places"]
        arrive((operator["name"] + "1", i))
        upward = lax.div(k, 4)
        tiles = [col[i, s] for s in range(NK)]

        @pl.loop(0, NK)
        def _(d):
            base = places["take"] + upward * (NK * NK) + d * NK
            total = table[base] * tiles[0]
            for s in range(1, NK):
                total += table[base + s] * tiles[s]
            gam[i, d] = total

        hops(operator["name"] + "2", gam, operator["got"], operator["second"], i)

    def y_lines(operator, i, stencil, side, store):
        source, got, edge, reach, places = (
            operator["source"], operator["got"], operator["edge"], operator["reach"], operator["places"],
        )
        lo, hi = GROUPS[i]
        if operator["name"] == "f":
            arrive(("f", "halo", i))
            arrive(("f2", i))

        def entry(name, count, index=0):
            return table[places[name] + k * count + index]

        for f in range(lo, hi):
            for half in range(2):
                lanes = slice(128 * half, 128 * half + 128)
                tile = (f - lo) * 2 + half
                if i in operator["direct"]:
                    from_low = from_high = None
                    for j in range(1, NK):
                        block = along_yz(j)
                        plane = operator["everyone"][block, f, :, lanes]
                        a = table[places["take"] + k * NK + block] * plane
                        b = table[places["take"] + NK * NK + k * NK + block] * plane
                        from_low, from_high = (a, b) if from_low is None else (from_low + a, from_high + b)
                else:
                    from_low = got[i, tile]
                    from_high = got[i, 4 + tile]
                rows = [edge[f, h, :, lanes] * entry("has_low", 1) for h in range(reach)]
                rows += [source[f, y, :, lanes] for y in range(CY)]
                rows += [edge[f, reach + h, :, lanes] * entry("has_high", 1) for h in range(reach)]
                for h in range(reach):
                    from_low += entry("near_low", reach, h) * rows[h] + entry("own_low", reach, h) * rows[reach + h]
                    from_high += (
                        entry("near_high", reach, h) * rows[reach + CY + h]
                        + entry("own_high", reach, h) * rows[CY + h]
                    )
                moves = {}
                for move, factor in stencil:
                    moves.setdefault(abs(move), {})[move] = factor
                values = []
                for y in range(CY):
                    at = reach + y
                    value = None
                    for move, factors in moves.items():
                        if move == 0:
                            term = np.float32(factors[0]) * rows[at]
                        elif factors[move] == factors[-move]:
                            term = np.float32(factors[move]) * (rows[at + move] + rows[at - move])
                        else:
                            term = np.float32(factors[move]) * (rows[at + move] - rows[at - move])
                        value = term if value is None else value + term
                    if y == 0:
                        value = value + from_low
                    if y == CY - 1:
                        value = value + from_high
                    if y > 0:
                        value = value - entry("lower", CY, y) * values[-1]
                    values.append(value)
                last = None
                for y in range(CY - 1, -1, -1):
                    value = values[y] if last is None else values[y] - np.float32(side) * last
                    last = value * entry("inverse", CY, y)
                    store(y, f, half, last)

    deriv = dict(
        name="d", source=v, phi=phi_d, col=col_d, gam=gam_d, got=got_d, edge=edge_d, reach=2, places=at_d,
        first=(d1_ss, d1_rs), second=(d2_ss, d2_rs), halo=(dh_ss, dh_rs),
        direct=(), planes=None, everyone=None,
    )
    smooth = dict(
        name="f", source=sb, phi=phi_f, col=col_f, gam=gam_f, got=got_f, edge=edge_f, reach=5, places=at_f,
        first=(f1_ss, f1_rs), second=(f2_ss, f2_rs), halo=(fh_ss, fh_rs),
        direct=DIRECT_FILTER, planes=planes_f, everyone=everyone_f,
    )

    def store_q(y, f, half, value):
        q[f, y, :, 128 * half : 128 * half + 128] = value

    def store_out(y, f, half, value):
        start = y * CZ + 128 * half
        out[0, f, :, start : start + 128] = value

    count = len(GROUPS)
    def q_lines(i):
        y_lines(deriv, i, DERIV_STENCIL, SIDE_DERIV, store_q)
        start_all("q", q, pq, q_ss, q_rs, *GROUPS[i], i)

    def send_u():
        for j in GX_ORDER:
            pltpu.make_async_remote_copy(
                u.at[:, along_gx(j)], pu.at[:, g], u_ss.at[0], u_rs.at[0],
                device_id={"gx": along_gx(j)}, device_id_type=MESH,
            ).start()

    batch(("u", 0), u.at[:, 1:NG], pu.at[:, 1:NG], u_ss.at[0], u_rs.at[0])
    pu[:, g] = u[:, g]

    @pl.when(jnp.logical_not(is_inlet))
    def _():
        send_u()

    before = len(leaving)
    for i in range(count):
        first_half(deriv, i)
    early = len(leaving)

    @pl.when(is_inlet)
    def _():
        inlet_rows[...] = jnp.zeros((2, 64, CZ), F32)
        inlet_copies().wait_recv()
        for y in range(CY):
            row = inlet[pl.ds(inflow[y], 1), :]
            for f in range(5):
                at = (y % 8) * 8 + f
                inlet_rows[y // 8, at : at + 1, :] = row[:, f * CZ : (f + 1) * CZ]
        total = None
        for b in range(2):
            lines = jnp.concatenate([inlet_rows[b], jnp.zeros((64, CZ), F32)], axis=0)
            for part in split(lines):
                term = dot(sel[b], part, ((1,), (1,)))
                total = term if total is None else total + term
        total = total.reshape(NG, 2, 16, 128)
        moved = pltpu.roll(total[:, 1].reshape(NG * 16, 128), 64, 1).reshape(NG, 16, 128)
        side = lax.broadcasted_iota(jnp.int32, (NG, 16, 128), 2) < 64
        patch_s[...] = jnp.where(side, total[:, 0], moved)

        @pl.loop(1, NG)
        def _(j):
            patch_copy(j).start()

        patch_r[...] = patch_s[0]

    @pl.when(is_inlet)
    def _():
        send_u()

    for i in range(count):
        second_half(deriv, i)
    def plane_copy(j):
        return pltpu.make_async_remote_copy(
            du.at[along_gx(j)], pdu.at[g], du_ss.at[0], du_rs.at[0],
            device_id={"gx": along_gx(j)}, device_id_type=MESH,
        )

    def plane_copies():
        return pltpu.make_async_remote_copy(
            du.at[1:NG], pdu.at[1:NG], du_ss.at[0], du_rs.at[0], device_id={"gx": along_gx(1)}, device_id_type=MESH,
        )

    @pl.when(sect == 1)
    def _():
        @pl.when(g > 0)
        def _():
            patch_copy(g).wait_recv()

        packed = patch_r[...]
        high, low = split(jnp.concatenate([packed, pltpu.roll(packed, 64, 1)], axis=0))
        for t in range(2):
            rows = place[t, 0:32, :]
            total = dot(high, rows, ((0,), (0,))) + dot(low, rows, ((0,), (0,)))
            hits = jnp.sum(counts[t], axis=0, keepdims=True)
            value = (total[:64] * (1.0 / jnp.maximum(hits, 1.0))).reshape(8, 8, CZ)
            du[8 * t : 8 * t + 8] = value

            @pl.when(g == 0)
            def _():
                taken = hits.reshape(1, 1, CZ) > 0
                du[8 * t : 8 * t + 8] = jnp.where(taken, value, inlet_rows[t].reshape(8, 8, CZ))

        row_of = lax.broadcasted_iota(jnp.int32, (8, CZ), 0)
        factors = []
        for h in range(5):
            factor = jnp.zeros((8, CZ), F32)
            for f in range(5):
                factor = jnp.where(row_of == f, mix(1, f, h), factor)
            factors.append(factor)
        for y in range(CY):
            value = factors[0] * du[y, 0:1, :]
            for h in range(1, 5):
                value += factors[h] * du[y, h : h + 1, :]
            dv[y] = value
        up = down = None
        for y in range(CY):
            a = table[at_d["send_up"] + k * CY + y] * dv[y]
            b = table[at_d["send_down"] + k * CY + y] * dv[y]
            up, down = (a, b) if up is None else (up + a, down + b)
        planes_x[0] = up
        planes_x[1] = down
        for j in range(1, NK):
            peer = along_yz(j)
            pltpu.make_async_remote_copy(
                planes_x.at[lax.div(k - peer + NK, NK)], everyone_x.at[k], x_ss.at[0], x_rs.at[0],
                device_id={"yz": peer}, device_id_type=MESH,
            ).start()
        pltpu.make_async_remote_copy(
            dv.at[CY - 2 : CY], edge_x.at[0:2], x_ss.at[1], x_rs.at[1],
            device_id={"yz": along_yz(1)}, device_id_type=MESH,
        ).start()
        pltpu.make_async_remote_copy(
            dv.at[0:2], edge_x.at[2:4], x_ss.at[1], x_rs.at[1],
            device_id={"yz": from_yz(1)}, device_id_type=MESH,
        ).start()

    def extra_copies():
        return [
            pltpu.make_async_remote_copy(
                whole, whole, x_ss.at[i], x_rs.at[i], device_id={"yz": along_yz(1)}, device_id_type=MESH,
            )
            for i, whole in enumerate((everyone_x.at[1:NK], edge_x))
        ]

    for wait in leaving[before:early]:
        wait()
    del leaving[before:early]

    for i in range(count):
        arrive(("d", "halo", i))
        arrive(("d2", i))

    @pl.when(sect == 1)
    def _():
        @pl.loop(1, NG)
        def _(j):
            plane_copy(j).start()

        pdu[g] = du[g]
        for y in range(CY):
            for f in range(5):
                v[f, y, 0:1, :] = v[f, y, 0:1, :] + dv[y, f : f + 1, :]
        for copy in extra_copies():
            copy.wait_recv()
        for f in range(5):
            for h in range(4):
                edge_d[f, h, 0:1, :] = edge_d[f, h, 0:1, :] + edge_x[h, f : f + 1, :]
        from_low = from_high = None
        for j in range(1, NK):
            block = along_yz(j)
            plane = everyone_x[block]
            a = table[at_d["take"] + k * NK + block] * plane
            b = table[at_d["take"] + NK * NK + k * NK + block] * plane
            from_low, from_high = (a, b) if from_low is None else (from_low + a, from_high + b)
        for i, (lo, hi) in enumerate(GROUPS):
            for f in range(lo, hi):
                for half in range(2):
                    tile = (f - lo) * 2 + half
                    lanes = slice(128 * half, 128 * half + 128)
                    got_d[i, tile, 0:1, :] = got_d[i, tile, 0:1, :] + from_low[f : f + 1, lanes]
                    got_d[i, 4 + tile, 0:1, :] = got_d[i, 4 + tile, 0:1, :] + from_high[f : f + 1, lanes]

    for i in range(count):
        q_lines(i)

    for load in loads[6:]:
        load.wait()
    arrive(("u", 0))

    @pl.when(sect == 1)
    def _():
        plane_copies().wait_recv()

        @pl.loop(0, NG)
        def _(r):
            for f in range(5):
                pu[f, r, 0:1, :] = pu[f, r, 0:1, :] + pdu[r, f : f + 1, :]

    for f in range(5):
        high, low = split(pu[f].reshape(NX, CZ))
        gx_[f] = dot(dx[sect, 0], high) + dot(dx[sect, 0], low) + dot(dx[sect, 1], high)
        gz_[f] = dot(high, dz[0]) + dot(low, dz[0]) + dot(high, dz[1])

    @pl.loop(0, 5)
    def _(f):
        value = pu[f].reshape(NX, CZ)
        for h in range(5):
            value += mix(0, f, h) * gx_[h]
            value += mix(2, f, h) * gz_[h]
        pp[f] = value

    for i in range(count):
        lo, hi = GROUPS[i]
        arrive(("q", i))
        for f in range(lo, hi):
            high, low = split(pp[f] + pq[f].reshape(NX, CZ))
            value = dot(high, fz[0]) + dot(low, fz[0]) + dot(high, fz[1])
            high, low = split(value)
            value = dot(fx[sect, 0], high) + dot(fx[sect, 0], low) + dot(fx[sect, 1], high)
            ps[f] = value.reshape(NG, CX, CZ)
        start_all("s", ps, sb, s_ss, s_rs, lo, hi, i)

    for i in range(count):
        arrive(("s", i))
        first_half(smooth, i)
        if i > 0:
            second_half(smooth, i - 1)
    for i in range(count):
        y_lines(smooth, i, FILTER_STENCIL, SIDE_FILTER, store_out)

    for wait in leaving:
        wait()

    @pl.when(sect == 1)
    def _():
        plane_copies().wait_send()
        for copy in extra_copies():
            copy.wait_send()

    @pl.when(is_outlet)
    def _():
        inflow_copy().wait_send()

    @pl.when(is_inlet)
    def _():
        inlet_copies().wait_send()

        @pl.loop(1, NG)
        def _(j):
            patch_copy(j).wait_send()


def per_device(fields, jacobians, inflow_map, donor_tiles, receptor_tiles):
    table_d, places_d = block_table(DERIV_STENCIL, SIDE_DERIV)
    table_f, places_f = block_table(FILTER_STENCIL, SIDE_FILTER)
    places_f = {name: start + table_d.size for name, start in places_f.items()}
    table = np.concatenate([table_d, table_f]).astype(np.float32)
    dx = np.stack([halves(line_matrix(NX, p, DERIV_STENCIL, SIDE_DERIV)) for p in (True, False)])
    fx = np.stack([halves(line_matrix(NX, p, FILTER_STENCIL, SIDE_FILTER)) for p in (True, False)])
    dz = halves(line_matrix(CZ, True, DERIV_STENCIL, SIDE_DERIV).T)
    fz = halves(line_matrix(CZ, True, FILTER_STENCIL, SIDE_FILTER).T)
    block = (5, CY, CX, CZ)
    count = len(GROUPS)

    def buffer(*shape, kind=F32):
        return pltpu.VMEM(shape, kind)

    def scalars(*shape, kind=jnp.int32):
        return pltpu.SMEM(shape, kind)

    def dma(length):
        return pltpu.SemaphoreType.DMA((length,))

    tiles = [buffer(count, NK, 8, 128)] * 4
    inputs = (
        fields, jnp.transpose(jacobians, (1, 0, 2)), inflow_map, jnp.transpose(donor_tiles, (0, 1, 4, 2, 3)),
        receptor_tiles.reshape(SLOTS), jnp.asarray(table), jnp.asarray(dx), jnp.asarray(fx), jnp.asarray(dz),
        jnp.asarray(fz),
    )
    return pl.pallas_call(
        functools.partial(kernel, places_d, places_f),
        out_shape=jax.ShapeDtypeStruct(fields.shape, F32),
        in_specs=[pl.BlockSpec(memory_space=HBM)] * len(inputs),
        out_specs=pl.BlockSpec(memory_space=pltpu.VMEM),
        scratch_shapes=[
            buffer(*fields.shape), scalars(5, 3, 5, kind=F32), scalars(16), scalars(1, 1, 3, 1, SLOTS), scalars(SLOTS),
            scalars(table.size, kind=F32),
            buffer(*dx.shape, kind=BF16), buffer(*fx.shape, kind=BF16),
            buffer(*dz.shape, kind=BF16), buffer(*fz.shape, kind=BF16), dma(10),
            buffer(CY, 5, CX, CZ),
            buffer(2, 512, CZ, kind=BF16), buffer(2, 512, CZ, kind=BF16),
            buffer(NG, 40, 256), buffer(NG, 40, 256),
            buffer(*block), buffer(*block), buffer(*block), buffer(*block), buffer(*block),
            buffer(5, NX, CZ), buffer(5, NX, CZ), buffer(5, NX, CZ),
            buffer(*block), buffer(*block),
            buffer(CY, 5 * CZ), buffer(NY, 5 * CZ), buffer(2, 64, CZ), buffer(NG, 16, 128), buffer(16, 128),
            *tiles, *tiles,
            buffer(5, 4, CX, CZ), buffer(5, 10, CX, CZ),
            buffer(2, 5, CX, CZ), buffer(NK, 5, CX, CZ),
            buffer(CY, 8, CZ), buffer(NG, 8, CZ), buffer(CY, 8, CZ), buffer(2, 8, CZ), buffer(NK, 8, CZ), buffer(4, 8, CZ),
            *([dma(1)] * 4), *([dma(count)] * 16), dma(2), dma(2), dma(NG), dma(1), dma(1), dma(1), dma(2), dma(2),
        ],
        compiler_params=pltpu.CompilerParams(
            collective_id=0, has_side_effects=True, vmem_limit_bytes=VMEM_MIB * 1024 * 1024
        ),
        name="segment",
    )(*inputs)


def solution(mesh):
    in_specs = (
        P("sect", None, "gx", "yz"),
        P(),
        P("yz"),
        P("sect", "gx", "yz", None, None),
        P("sect", "gx", "yz", None),
    )
    out_specs = P("sect", None, "gx", "yz")
    return jax.shard_map(
        per_device, mesh=mesh, in_specs=in_specs, out_specs=out_specs, check_vma=False
    )
```

```python
import functools

import jax
import jax.numpy as jnp
import ml_dtypes
import numpy as np
from jax import lax
from jax.experimental import pallas as pl
from jax.experimental.pallas import tpu as pltpu
from jax.sharding import PartitionSpec as P

MESH = pl.DeviceIdType.MESH
HBM = pltpu.MemorySpace.HBM
F32 = jnp.float32
BF16 = jnp.bfloat16

CX = 8
CY = 16
CZ = 256
NG = 16
NK = 8
NX = 128
NY = 128
SLOTS = 64
GROUPS = ((0, 2), (2, 4), (4, 5))
VMEM_MIB = 62
GX_ORDER = (8, 4, 12, 6, 10, 2, 14, 7, 9, 5, 11, 3, 13, 1, 15)
INLET_ORDER = (4, 5, 3, 6, 2, 7, 1)
DIRECT_FILTER = (1, 2)

SEGMENT_STEP = 0.25
SIDE_DERIV = 1.0 / 3.0
SIDE_FILTER = 0.49


def filter_coeffs():
    side = SIDE_FILTER
    return [
        (193 + 126 * side) / 256,
        (105 + 302 * side) / 256,
        15 * (-1 + 2 * side) / 64,
        45 * (1 - 2 * side) / 512,
        5 * (-1 + 2 * side) / 256,
        (1 - 2 * side) / 512,
    ]


DERIV_STENCIL = ((1, 7.0 / 9.0), (-1, -7.0 / 9.0), (2, 1.0 / 36.0), (-2, -1.0 / 36.0))
FILTER_STENCIL = ((0, filter_coeffs()[0]),) + tuple(
    (sign * reach, filter_coeffs()[reach] / 2) for reach in range(1, 6) for sign in (1, -1)
)


def sides(length, periodic, stencil, side):
    left = np.eye(length)
    right = np.zeros((length, length))
    for row in range(length):
        for offset, factor in ((-1, side), (1, side)):
            if periodic or 0 <= row + offset < length:
                left[row, (row + offset) % length] += factor
        for offset, factor in stencil:
            if periodic or 0 <= row + offset < length:
                right[row, (row + offset) % length] += factor
    return left, right


def line_matrix(length, periodic, stencil, side):
    return np.linalg.solve(*sides(length, periodic, stencil, side))


def halves(matrix):
    value = np.asarray(matrix, np.float32)
    high = value.astype(ml_dtypes.bfloat16)
    low = (value - high.astype(np.float32)).astype(ml_dtypes.bfloat16)
    return np.stack([high, low])


def block_table(stencil, side):
    left, right = sides(NY, False, stencil, side)
    reach = max(offset for offset, _ in stencil)
    below = np.zeros((NK, NY))
    above = np.zeros((NK, NY))
    corner_low = np.zeros(NK)
    corner_high = np.zeros(NK)
    for d in range(NK):
        lo, hi = d * CY, (d + 1) * CY
        if d > 0:
            row = np.linalg.solve(left[:lo, :lo].T, np.eye(lo)[lo - 1])
            below[d] = -side * (row @ right[:lo])
            corner_low[d] = row[-1]
        if d < NK - 1:
            row = np.linalg.solve(left[hi:, hi:].T, np.eye(NY - hi)[0])
            above[d] = -side * (row @ right[hi:])
            corner_high[d] = row[0]
    send_up = np.zeros((NK, CY))
    send_down = np.zeros((NK, CY))
    for s in range(NK):
        cells = slice(s * CY, (s + 1) * CY)
        if s < NK - 1:
            value = below[min(s + 2, NK - 1)][cells]
            send_up[s] = value / np.abs(value).max()
        if s > 0:
            value = above[max(s - 2, 0)][cells]
            send_down[s] = value / np.abs(value).max()
    take_low = np.zeros((NK, NK))
    take_high = np.zeros((NK, NK))
    near_low = np.zeros((NK, reach))
    near_high = np.zeros((NK, reach))
    own_low = np.zeros((NK, reach))
    own_high = np.zeros((NK, reach))
    for d in range(NK):
        for s in range(d):
            value, unit = below[d][s * CY : (s + 1) * CY], send_up[s]
            core = unit[: CY - reach]
            take_low[d, s] = (value[: CY - reach] @ core) / (core @ core)
            if s == d - 1:
                near_low[d] = (value - take_low[d, s] * unit)[CY - reach :]
        for s in range(d + 1, NK):
            value, unit = above[d][s * CY : (s + 1) * CY], send_down[s]
            core = unit[reach:]
            take_high[d, s] = (value[reach:] @ core) / (core @ core)
            if s == d + 1:
                near_high[d] = (value - take_high[d, s] * unit)[:reach]
        own_low[d] = below[d][d * CY : d * CY + reach]
        own_high[d] = above[d][(d + 1) * CY - reach : (d + 1) * CY]
    lower = np.zeros((NK, CY))
    inverse = np.zeros((NK, CY))
    for d in range(NK):
        diagonal = np.ones(CY)
        diagonal[0] -= side**2 * corner_low[d]
        diagonal[-1] -= side**2 * corner_high[d]
        inverse[d, 0] = 1 / diagonal[0]
        for y in range(1, CY):
            lower[d, y] = side * inverse[d, y - 1]
            inverse[d, y] = 1 / (diagonal[y] - side * lower[d, y])
    has_low = (np.arange(NK) > 0).astype(np.float64)
    has_high = (np.arange(NK) < NK - 1).astype(np.float64)
    parts = dict(
        send_up=send_up, send_down=send_down, take=np.stack([take_low, take_high]), near_low=near_low,
        near_high=near_high, own_low=own_low, own_high=own_high, lower=lower, inverse=inverse,
        has_low=has_low, has_high=has_high,
    )
    places, start = {}, 0
    for name, value in parts.items():
        places[name] = start
        start += value.size
    return np.concatenate([value.reshape(-1) for value in parts.values()]), places


def split(value):
    high = value.astype(BF16)
    low = (value - high.astype(F32)).astype(BF16)
    return high, low


def dot(a, b, dims=((1,), (0,))):
    return lax.dot_general(a, b, (dims, ((), ())), preferred_element_type=F32)


def kernel(
    at_d, at_f,
    fields_hbm, jac_hbm, inflow_hbm, donors_hbm, receptors_hbm, table_hbm, dx_hbm, fx_hbm, dz_hbm, fz_hbm, out,
    fields, jac, inflow, donors, receptors, table, dx, fx, dz, fz, load_sem,
    u0, sel, place, ts, tr, u, pu, v, q, pq, gx_, gz_, pp, ps, sb,
    outlet, inlet, inlet_rows, patch_s, patch_r,
    phi_d, col_d, gam_d, got_d, phi_f, col_f, gam_f, got_f, edge_d, edge_f, planes_f, everyone_f,
    du, pdu, dv, planes_x, everyone_x, edge_x,
    tile_ss, tile_rs, u_ss, u_rs, q_ss, q_rs, s_ss, s_rs,
    d1_ss, d1_rs, d2_ss, d2_rs, f1_ss, f1_rs, f2_ss, f2_rs, dh_ss, dh_rs, fh_ss, fh_rs, in_ss, in_rs, patch_ss, patch_rs,
    du_ss, du_rs, x_ss, x_rs,
):
    sect = lax.axis_index("sect")
    g = lax.axis_index("gx")
    k = lax.axis_index("yz")

    def along_gx(j):
        return lax.rem(g + j, NG)

    def along_yz(j):
        return lax.rem(k + j, NK)

    def from_yz(j):
        return lax.rem(k + NK - j, NK)

    is_outlet = jnp.logical_and(sect == 0, g == 0)
    is_inlet = jnp.logical_and(sect == 1, g == 0)

    barrier = pltpu.get_barrier_semaphore()

    @pl.loop(1, NG)
    def _(j):
        pl.semaphore_signal(barrier, inc=1, device_id={"gx": along_gx(j)}, device_id_type=MESH)

    @pl.loop(1, NK)
    def _(j):
        pl.semaphore_signal(barrier, inc=1, device_id={"yz": along_yz(j)}, device_id_type=MESH)

    @pl.when(is_inlet)
    def _():
        pl.semaphore_signal(barrier, inc=1, device_id={"sect": 0}, device_id_type=MESH)

    pairs = (
        (fields_hbm, fields), (donors_hbm, donors), (receptors_hbm, receptors), (inflow_hbm, inflow),
        (jac_hbm, jac), (table_hbm, table), (dx_hbm, dx), (dz_hbm, dz), (fz_hbm, fz), (fx_hbm, fx),
    )
    loads = [pltpu.make_async_copy(source, target, load_sem.at[i]) for i, (source, target) in enumerate(pairs)]
    for load in loads:
        load.start()
    loads[0].wait()

    mine = pl.ds(pl.multiple_of(k * CY, CY), CY)

    def inflow_copy():
        return pltpu.make_async_remote_copy(
            outlet, inlet.at[mine], in_ss.at[0], in_rs.at[0], device_id={"sect": 1}, device_id_type=MESH,
        )

    def inlet_copies():
        whole = inlet.at[0 : NY - CY]
        return pltpu.make_async_remote_copy(
            whole, whole, in_ss.at[1], in_rs.at[1], device_id={"yz": along_yz(1)}, device_id_type=MESH,
        )

    @pl.when(is_outlet)
    def _():
        for y in range(CY):
            for f in range(5):
                outlet[y : y + 1, f * CZ : (f + 1) * CZ] = fields[0, f, CX - 1 : CX, y * CZ : (y + 1) * CZ]

        pl.semaphore_wait(barrier, NG + NK - 1)
        inflow_copy().start()

    for y in range(CY):
        for f in range(5):
            u0[y, f] = fields[0, f, :, y * CZ : (y + 1) * CZ]

    @pl.when(is_inlet)
    def _():
        for y in range(CY):
            for f in range(5):
                u0[y, f, 0:1, :] = jnp.zeros((1, CZ), F32)

    offset = lax.broadcasted_iota(jnp.int32, (8, CZ), 1) - lax.broadcasted_iota(jnp.int32, (8, CZ), 0)
    loads[1].wait()

    @pl.loop(0, SLOTS // 2)
    def _(j):
        for b in range(2):
            rows = []
            for e in range(2):
                slot = 2 * j + e
                first = jnp.where(donors[0, 0, 1, 0, slot] == b, donors[0, 0, 2, 0, slot], -1000)
                hit = jnp.logical_or(offset == first, offset == first + 1)
                rows.append(jnp.where(hit, 0.5, 0.0))
            sel[b, pl.ds(pl.multiple_of(16 * j, 16), 16), :] = jnp.concatenate(rows, axis=0).astype(BF16)

    payload = None
    for b in range(2):
        lines = jnp.concatenate([u0[8 * b : 8 * b + 8].reshape(320, CZ), jnp.zeros((64, CZ), F32)], axis=0)
        for part in split(lines):
            term = dot(sel[b], part, ((1,), (1,)))
            payload = term if payload is None else payload + term
    ts[:, 0:32, :] = payload[:, 0:256].reshape(NG, 32, 256)
    rest = payload[:, 256:384].reshape(NG, 4, 8, 128)
    left = lax.broadcasted_iota(jnp.int32, (NG, 8, 128), 2) < 64
    for e in range(2):
        moved = pltpu.roll(rest[:, 2 * e + 1].reshape(NG * 8, 128), 64, 1).reshape(NG, 8, 128)
        ts[:, 32:40, 128 * e : 128 * e + 128] = jnp.where(left, rest[:, 2 * e], moved)

    @pl.when(jnp.logical_not(is_outlet))
    def _():
        pl.semaphore_wait(barrier, NG + NK - 2)

    leaving = []
    coming = {}

    def batch(name, source, target, send, receive):
        whole = pltpu.make_async_remote_copy(
            source, target, send, receive, device_id={"gx": along_gx(1)}, device_id_type=MESH
        )
        leaving.append(whole.wait_send)
        coming[name] = whole.wait_recv

    def arrive(name):
        coming.pop(name)()

    for j in GX_ORDER:
        pltpu.make_async_remote_copy(
            ts.at[along_gx(j)], tr.at[g], tile_ss.at[0], tile_rs.at[0],
            device_id={"gx": along_gx(j)}, device_id_type=MESH,
        ).start()
    batch("tiles", ts.at[1:NG], tr.at[1:NG], tile_ss.at[0], tile_rs.at[0])

    tr[g] = ts[g]

    @pl.when(is_inlet)
    def _():
        inflow_copy().wait_recv()
        for j in INLET_ORDER:
            pltpu.make_async_remote_copy(
                inlet.at[mine], inlet.at[mine], in_ss.at[1], in_rs.at[1],
                device_id={"yz": along_yz(j)}, device_id_type=MESH,
            ).start()

    loads[2].wait()

    def place_row(j, counts):
        counts = list(counts)
        for t in range(2):
            rows = []
            for e in range(2):
                goal = (receptors[2 * j + e] - 32 * t) * 8
                one = jnp.where(offset == goal, 1.0, 0.0)
                counts[t] = counts[t] + one
                rows.append(one)
            place[t, pl.ds(pl.multiple_of(16 * j, 16), 16), :] = jnp.concatenate(rows, axis=0).astype(BF16)
        return tuple(counts)

    counts = lax.fori_loop(0, SLOTS // 2, place_row, (jnp.zeros((8, CZ), F32),) * 2)

    loads[3].wait()

    def patch_copy(j):
        return pltpu.make_async_remote_copy(
            patch_s.at[j], patch_r, patch_ss.at[j], patch_rs.at[0], device_id={"gx": j}, device_id_type=MESH,
        )

    arrive("tiles")

    main = tr[:, 0:32, :].reshape(512, 256)
    rest = []
    for e in range(2):
        two = tr[:, 32:40, 128 * e : 128 * e + 128]
        rest += [two, pltpu.roll(two.reshape(NG * 8, 128), 64, 1).reshape(NG, 8, 128)]
    rest = jnp.stack(rest, axis=1).reshape(512, 128)
    halves_of = [split(main), split(rest)]
    for t in range(2):
        total = jnp.concatenate(
            [
                dot(high, place[t], ((0,), (0,))) + dot(low, place[t], ((0,), (0,)))
                for high, low in halves_of
            ],
            axis=0,
        )
        hits = jnp.sum(counts[t], axis=0, keepdims=True)
        scale = (1.0 / jnp.maximum(hits, 1.0)).reshape(1, 1, 1, CZ)
        mean = total[:320].reshape(8, 5, 8, CZ) * scale
        value = jnp.where(hits.reshape(1, 1, 1, CZ) > 0, mean, u0[8 * t : 8 * t + 8])
        for f in range(5):
            u[f, 8 * t : 8 * t + 8] = value[:, f]

    def start_all(name, source, target, send, receive, lo, hi, at):
        for j in GX_ORDER:
            pltpu.make_async_remote_copy(
                source.at[lo:hi, along_gx(j)], target.at[lo:hi, g], send.at[at], receive.at[at],
                device_id={"gx": along_gx(j)}, device_id_type=MESH,
            ).start()
        batch((name, at), source.at[lo:hi, 1:NG], target.at[lo:hi, 1:NG], send.at[at], receive.at[at])
        target[lo:hi, g] = source[lo:hi, g]

    loads[4].wait()
    loads[5].wait()

    def mix(d, f, h):
        return jac[f, d, h] * (-SEGMENT_STEP)

    @pl.loop(0, CY)
    def _(y):
        cells = [u[h, y] for h in range(5)]
        for f in range(5):
            value = mix(1, f, 0) * cells[0]
            for h in range(1, 5):
                value += mix(1, f, h) * cells[h]
            v[f, y] = value

    def halo(operator, i):
        name, source, edge, reach = operator["name"], operator["source"], operator["edge"], operator["reach"]
        send, receive = operator["halo"]
        lo, hi = GROUPS[i]
        pltpu.make_async_remote_copy(
            source.at[lo:hi, CY - reach : CY], edge.at[lo:hi, 0:reach], send.at[i], receive.at[i],
            device_id={"yz": along_yz(1)}, device_id_type=MESH,
        ).start()
        pltpu.make_async_remote_copy(
            source.at[lo:hi, 0:reach], edge.at[lo:hi, reach : 2 * reach], send.at[i], receive.at[i],
            device_id={"yz": from_yz(1)}, device_id_type=MESH,
        ).start()
        batch((name, "halo", i), source.at[lo:hi, 0 : 2 * reach], edge.at[lo:hi], send.at[i], receive.at[i])

    def hops(name, source, target, sems, i):
        send, receive = sems
        for j in range(1, NK):
            pltpu.make_async_remote_copy(
                source.at[i, along_yz(j)], target.at[i, k], send.at[i], receive.at[i],
                device_id={"yz": along_yz(j)}, device_id_type=MESH,
            ).start()
        batch((name, i), source.at[i, 1:NK], target.at[i, 1:NK], send.at[i], receive.at[i])
        target[i, k] = source[i, k]

    def first_half(operator, i):
        source, phi, places = operator["source"], operator["phi"], operator["places"]
        lo, hi = GROUPS[i]
        direct = i in operator["direct"]
        planes, everyone = operator["planes"], operator["everyone"]
        for f in range(lo, hi if direct else lo + 2):
            for half in range(2):
                tile = (f - lo) * 2 + half
                if f >= hi:
                    phi[i, tile] = jnp.zeros((8, 128), F32)
                    phi[i, 4 + tile] = jnp.zeros((8, 128), F32)
                    continue
                up = down = None
                for y in range(CY):
                    row = source[f, y, :, 128 * half : 128 * half + 128]
                    a = table[places["send_up"] + k * CY + y] * row
                    b = table[places["send_down"] + k * CY + y] * row
                    up, down = (a, b) if up is None else (up + a, down + b)
                if direct:
                    planes[0, f, :, 128 * half : 128 * half + 128] = up
                    planes[1, f, :, 128 * half : 128 * half + 128] = down
                else:
                    phi[i, tile] = up
                    phi[i, 4 + tile] = down

        if direct:
            send, receive = operator["first"]
            for j in range(1, NK):
                peer = along_yz(j)
                pltpu.make_async_remote_copy(
                    planes.at[lax.div(k - peer + NK, NK), lo:hi], everyone.at[k, lo:hi], send.at[i], receive.at[i],
                    device_id={"yz": peer}, device_id_type=MESH,
                ).start()
            whole = everyone.at[1:NK, lo:hi]
            batch((operator["name"] + "2", i), whole, whole, send.at[i], receive.at[i])
            halo(operator, i)
            return

        hops(operator["name"] + "1", phi, operator["col"], operator["first"], i)
        halo(operator, i)

    def second_half(operator, i):
        if i in operator["direct"]:
            return
        col, gam, places = operator["col"], operator["gam"], operator["places"]
        arrive((operator["name"] + "1", i))
        upward = lax.div(k, 4)
        tiles = [col[i, s] for s in range(NK)]

        @pl.loop(0, NK)
        def _(d):
            base = places["take"] + upward * (NK * NK) + d * NK
            total = table[base] * tiles[0]
            for s in range(1, NK):
                total += table[base + s] * tiles[s]
            gam[i, d] = total

        hops(operator["name"] + "2", gam, operator["got"], operator["second"], i)

    def y_lines(operator, i, stencil, side, store):
        source, got, edge, reach, places = (
            operator["source"], operator["got"], operator["edge"], operator["reach"], operator["places"],
        )
        lo, hi = GROUPS[i]
        if operator["name"] == "f":
            arrive(("f", "halo", i))
            arrive(("f2", i))

        def entry(name, count, index=0):
            return table[places[name] + k * count + index]

        for f in range(lo, hi):
            for half in range(2):
                lanes = slice(128 * half, 128 * half + 128)
                tile = (f - lo) * 2 + half
                if i in operator["direct"]:
                    from_low = from_high = None
                    for j in range(1, NK):
                        block = along_yz(j)
                        plane = operator["everyone"][block, f, :, lanes]
                        a = table[places["take"] + k * NK + block] * plane
                        b = table[places["take"] + NK * NK + k * NK + block] * plane
                        from_low, from_high = (a, b) if from_low is None else (from_low + a, from_high + b)
                else:
                    from_low = got[i, tile]
                    from_high = got[i, 4 + tile]
                rows = [edge[f, h, :, lanes] * entry("has_low", 1) for h in range(reach)]
                rows += [source[f, y, :, lanes] for y in range(CY)]
                rows += [edge[f, reach + h, :, lanes] * entry("has_high", 1) for h in range(reach)]
                for h in range(reach):
                    from_low += entry("near_low", reach, h) * rows[h] + entry("own_low", reach, h) * rows[reach + h]
                    from_high += (
                        entry("near_high", reach, h) * rows[reach + CY + h]
                        + entry("own_high", reach, h) * rows[CY + h]
                    )
                moves = {}
                for move, factor in stencil:
                    moves.setdefault(abs(move), {})[move] = factor
                values = []
                for y in range(CY):
                    at = reach + y
                    value = None
                    for move, factors in moves.items():
                        if move == 0:
                            term = np.float32(factors[0]) * rows[at]
                        elif factors[move] == factors[-move]:
                            term = np.float32(factors[move]) * (rows[at + move] + rows[at - move])
                        else:
                            term = np.float32(factors[move]) * (rows[at + move] - rows[at - move])
                        value = term if value is None else value + term
                    if y == 0:
                        value = value + from_low
                    if y == CY - 1:
                        value = value + from_high
                    if y > 0:
                        value = value - entry("lower", CY, y) * values[-1]
                    values.append(value)
                last = None
                for y in range(CY - 1, -1, -1):
                    value = values[y] if last is None else values[y] - np.float32(side) * last
                    last = value * entry("inverse", CY, y)
                    store(y, f, half, last)

    deriv = dict(
        name="d", source=v, phi=phi_d, col=col_d, gam=gam_d, got=got_d, edge=edge_d, reach=2, places=at_d,
        first=(d1_ss, d1_rs), second=(d2_ss, d2_rs), halo=(dh_ss, dh_rs),
        direct=(), planes=None, everyone=None,
    )
    smooth = dict(
        name="f", source=sb, phi=phi_f, col=col_f, gam=gam_f, got=got_f, edge=edge_f, reach=5, places=at_f,
        first=(f1_ss, f1_rs), second=(f2_ss, f2_rs), halo=(fh_ss, fh_rs),
        direct=DIRECT_FILTER, planes=planes_f, everyone=everyone_f,
    )

    def store_q(y, f, half, value):
        q[f, y, :, 128 * half : 128 * half + 128] = value

    def store_out(y, f, half, value):
        start = y * CZ + 128 * half
        out[0, f, :, start : start + 128] = value

    count = len(GROUPS)
    def q_lines(i):
        y_lines(deriv, i, DERIV_STENCIL, SIDE_DERIV, store_q)
        start_all("q", q, pq, q_ss, q_rs, *GROUPS[i], i)

    def send_u():
        for j in GX_ORDER:
            pltpu.make_async_remote_copy(
                u.at[:, along_gx(j)], pu.at[:, g], u_ss.at[0], u_rs.at[0],
                device_id={"gx": along_gx(j)}, device_id_type=MESH,
            ).start()

    batch(("u", 0), u.at[:, 1:NG], pu.at[:, 1:NG], u_ss.at[0], u_rs.at[0])
    pu[:, g] = u[:, g]

    @pl.when(jnp.logical_not(is_inlet))
    def _():
        send_u()

    before = len(leaving)
    for i in range(count):
        first_half(deriv, i)
    early = len(leaving)

    @pl.when(is_inlet)
    def _():
        inlet_rows[...] = jnp.zeros((2, 64, CZ), F32)
        inlet_copies().wait_recv()
        for y in range(CY):
            row = inlet[pl.ds(inflow[y], 1), :]
            for f in range(5):
                at = (y % 8) * 8 + f
                inlet_rows[y // 8, at : at + 1, :] = row[:, f * CZ : (f + 1) * CZ]
        total = None
        for b in range(2):
            lines = jnp.concatenate([inlet_rows[b], jnp.zeros((64, CZ), F32)], axis=0)
            for part in split(lines):
                term = dot(sel[b], part, ((1,), (1,)))
                total = term if total is None else total + term
        total = total.reshape(NG, 2, 16, 128)
        moved = pltpu.roll(total[:, 1].reshape(NG * 16, 128), 64, 1).reshape(NG, 16, 128)
        side = lax.broadcasted_iota(jnp.int32, (NG, 16, 128), 2) < 64
        patch_s[...] = jnp.where(side, total[:, 0], moved)

        @pl.loop(1, NG)
        def _(j):
            patch_copy(j).start()

        patch_r[...] = patch_s[0]

    @pl.when(is_inlet)
    def _():
        send_u()

    for i in range(count):
        second_half(deriv, i)
    def plane_copy(j):
        return pltpu.make_async_remote_copy(
            du.at[along_gx(j)], pdu.at[g], du_ss.at[0], du_rs.at[0],
            device_id={"gx": along_gx(j)}, device_id_type=MESH,
        )

    def plane_copies():
        return pltpu.make_async_remote_copy(
            du.at[1:NG], pdu.at[1:NG], du_ss.at[0], du_rs.at[0], device_id={"gx": along_gx(1)}, device_id_type=MESH,
        )

    @pl.when(sect == 1)
    def _():
        @pl.when(g > 0)
        def _():
            patch_copy(g).wait_recv()

        packed = patch_r[...]
        high, low = split(jnp.concatenate([packed, pltpu.roll(packed, 64, 1)], axis=0))
        for t in range(2):
            rows = place[t, 0:32, :]
            total = dot(high, rows, ((0,), (0,))) + dot(low, rows, ((0,), (0,)))
            hits = jnp.sum(counts[t], axis=0, keepdims=True)
            value = (total[:64] * (1.0 / jnp.maximum(hits, 1.0))).reshape(8, 8, CZ)
            du[8 * t : 8 * t + 8] = value

            @pl.when(g == 0)
            def _():
                taken = hits.reshape(1, 1, CZ) > 0
                du[8 * t : 8 * t + 8] = jnp.where(taken, value, inlet_rows[t].reshape(8, 8, CZ))

        row_of = lax.broadcasted_iota(jnp.int32, (8, CZ), 0)
        factors = []
        for h in range(5):
            factor = jnp.zeros((8, CZ), F32)
            for f in range(5):
                factor = jnp.where(row_of == f, mix(1, f, h), factor)
            factors.append(factor)
        for y in range(CY):
            value = factors[0] * du[y, 0:1, :]
            for h in range(1, 5):
                value += factors[h] * du[y, h : h + 1, :]
            dv[y] = value
        up = down = None
        for y in range(CY):
            a = table[at_d["send_up"] + k * CY + y] * dv[y]
            b = table[at_d["send_down"] + k * CY + y] * dv[y]
            up, down = (a, b) if up is None else (up + a, down + b)
        planes_x[0] = up
        planes_x[1] = down
        for j in range(1, NK):
            peer = along_yz(j)
            pltpu.make_async_remote_copy(
                planes_x.at[lax.div(k - peer + NK, NK)], everyone_x.at[k], x_ss.at[0], x_rs.at[0],
                device_id={"yz": peer}, device_id_type=MESH,
            ).start()
        pltpu.make_async_remote_copy(
            dv.at[CY - 2 : CY], edge_x.at[0:2], x_ss.at[1], x_rs.at[1],
            device_id={"yz": along_yz(1)}, device_id_type=MESH,
        ).start()
        pltpu.make_async_remote_copy(
            dv.at[0:2], edge_x.at[2:4], x_ss.at[1], x_rs.at[1],
            device_id={"yz": from_yz(1)}, device_id_type=MESH,
        ).start()

    def extra_copies():
        return [
            pltpu.make_async_remote_copy(
                whole, whole, x_ss.at[i], x_rs.at[i], device_id={"yz": along_yz(1)}, device_id_type=MESH,
            )
            for i, whole in enumerate((everyone_x.at[1:NK], edge_x))
        ]

    for wait in leaving[before:early]:
        wait()
    del leaving[before:early]

    for i in range(count):
        arrive(("d", "halo", i))
        arrive(("d2", i))

    @pl.when(sect == 1)
    def _():
        @pl.loop(1, NG)
        def _(j):
            plane_copy(j).start()

        pdu[g] = du[g]
        for y in range(CY):
            for f in range(5):
                v[f, y, 0:1, :] = v[f, y, 0:1, :] + dv[y, f : f + 1, :]
        for copy in extra_copies():
            copy.wait_recv()
        for f in range(5):
            for h in range(4):
                edge_d[f, h, 0:1, :] = edge_d[f, h, 0:1, :] + edge_x[h, f : f + 1, :]
        from_low = from_high = None
        for j in range(1, NK):
            block = along_yz(j)
            plane = everyone_x[block]
            a = table[at_d["take"] + k * NK + block] * plane
            b = table[at_d["take"] + NK * NK + k * NK + block] * plane
            from_low, from_high = (a, b) if from_low is None else (from_low + a, from_high + b)
        for i, (lo, hi) in enumerate(GROUPS):
            for f in range(lo, hi):
                for half in range(2):
                    tile = (f - lo) * 2 + half
                    lanes = slice(128 * half, 128 * half + 128)
                    got_d[i, tile, 0:1, :] = got_d[i, tile, 0:1, :] + from_low[f : f + 1, lanes]
                    got_d[i, 4 + tile, 0:1, :] = got_d[i, 4 + tile, 0:1, :] + from_high[f : f + 1, lanes]

    for i in range(count):
        q_lines(i)

    for load in loads[6:]:
        load.wait()
    arrive(("u", 0))

    @pl.when(sect == 1)
    def _():
        plane_copies().wait_recv()

        @pl.loop(0, NG)
        def _(r):
            for f in range(5):
                pu[f, r, 0:1, :] = pu[f, r, 0:1, :] + pdu[r, f : f + 1, :]

    for f in range(5):
        high, low = split(pu[f].reshape(NX, CZ))
        gx_[f] = dot(dx[sect, 0], high) + dot(dx[sect, 0], low) + dot(dx[sect, 1], high)
        gz_[f] = dot(high, dz[0]) + dot(low, dz[0]) + dot(high, dz[1])

    @pl.loop(0, 5)
    def _(f):
        value = pu[f].reshape(NX, CZ)
        for h in range(5):
            value += mix(0, f, h) * gx_[h]
            value += mix(2, f, h) * gz_[h]
        pp[f] = value

    for i in range(count):
        lo, hi = GROUPS[i]
        arrive(("q", i))
        for f in range(lo, hi):
            high, low = split(pp[f] + pq[f].reshape(NX, CZ))
            value = dot(high, fz[0]) + dot(low, fz[0]) + dot(high, fz[1])
            high, low = split(value)
            value = dot(fx[sect, 0], high) + dot(fx[sect, 0], low) + dot(fx[sect, 1], high)
            ps[f] = value.reshape(NG, CX, CZ)
        start_all("s", ps, sb, s_ss, s_rs, lo, hi, i)

    for i in range(count):
        arrive(("s", i))
        first_half(smooth, i)
        if i > 0:
            second_half(smooth, i - 1)
    for i in range(count):
        y_lines(smooth, i, FILTER_STENCIL, SIDE_FILTER, store_out)

    for wait in leaving:
        wait()

    @pl.when(sect == 1)
    def _():
        plane_copies().wait_send()
        for copy in extra_copies():
            copy.wait_send()

    @pl.when(is_outlet)
    def _():
        inflow_copy().wait_send()

    @pl.when(is_inlet)
    def _():
        inlet_copies().wait_send()

        @pl.loop(1, NG)
        def _(j):
            patch_copy(j).wait_send()


def per_device(fields, jacobians, inflow_map, donor_tiles, receptor_tiles):
    table_d, places_d = block_table(DERIV_STENCIL, SIDE_DERIV)
    table_f, places_f = block_table(FILTER_STENCIL, SIDE_FILTER)
    places_f = {name: start + table_d.size for name, start in places_f.items()}
    table = np.concatenate([table_d, table_f]).astype(np.float32)
    dx = np.stack([halves(line_matrix(NX, p, DERIV_STENCIL, SIDE_DERIV)) for p in (True, False)])
    fx = np.stack([halves(line_matrix(NX, p, FILTER_STENCIL, SIDE_FILTER)) for p in (True, False)])
    dz = halves(line_matrix(CZ, True, DERIV_STENCIL, SIDE_DERIV).T)
    fz = halves(line_matrix(CZ, True, FILTER_STENCIL, SIDE_FILTER).T)
    block = (5, CY, CX, CZ)
    count = len(GROUPS)

    def buffer(*shape, kind=F32):
        return pltpu.VMEM(shape, kind)

    def scalars(*shape, kind=jnp.int32):
        return pltpu.SMEM(shape, kind)

    def dma(length):
        return pltpu.SemaphoreType.DMA((length,))

    tiles = [buffer(count, NK, 8, 128)] * 4
    inputs = (
        fields, jnp.transpose(jacobians, (1, 0, 2)), inflow_map, jnp.transpose(donor_tiles, (0, 1, 4, 2, 3)),
        receptor_tiles.reshape(SLOTS), jnp.asarray(table), jnp.asarray(dx), jnp.asarray(fx), jnp.asarray(dz),
        jnp.asarray(fz),
    )
    return pl.pallas_call(
        functools.partial(kernel, places_d, places_f),
        out_shape=jax.ShapeDtypeStruct(fields.shape, F32),
        in_specs=[pl.BlockSpec(memory_space=HBM)] * len(inputs),
        out_specs=pl.BlockSpec(memory_space=pltpu.VMEM),
        scratch_shapes=[
            buffer(*fields.shape), scalars(5, 3, 5, kind=F32), scalars(16), scalars(1, 1, 3, 1, SLOTS), scalars(SLOTS),
            scalars(table.size, kind=F32),
            buffer(*dx.shape, kind=BF16), buffer(*fx.shape, kind=BF16),
            buffer(*dz.shape, kind=BF16), buffer(*fz.shape, kind=BF16), dma(10),
            buffer(CY, 5, CX, CZ),
            buffer(2, 512, CZ, kind=BF16), buffer(2, 512, CZ, kind=BF16),
            buffer(NG, 40, 256), buffer(NG, 40, 256),
            buffer(*block), buffer(*block), buffer(*block), buffer(*block), buffer(*block),
            buffer(5, NX, CZ), buffer(5, NX, CZ), buffer(5, NX, CZ),
            buffer(*block), buffer(*block),
            buffer(CY, 5 * CZ), buffer(NY, 5 * CZ), buffer(2, 64, CZ), buffer(NG, 16, 128), buffer(16, 128),
            *tiles, *tiles,
            buffer(5, 4, CX, CZ), buffer(5, 10, CX, CZ),
            buffer(2, 5, CX, CZ), buffer(NK, 5, CX, CZ),
            buffer(CY, 8, CZ), buffer(NG, 8, CZ), buffer(CY, 8, CZ), buffer(2, 8, CZ), buffer(NK, 8, CZ), buffer(4, 8, CZ),
            *([dma(1)] * 4), *([dma(count)] * 16), dma(2), dma(2), dma(NG), dma(1), dma(1), dma(1), dma(2), dma(2),
        ],
        compiler_params=pltpu.CompilerParams(
            collective_id=0, has_side_effects=True, vmem_limit_bytes=VMEM_MIB * 1024 * 1024
        ),
        name="segment",
    )(*inputs)


def solution(mesh):
    in_specs = (
        P("sect", None, "gx", "yz"),
        P(),
        P("yz"),
        P("sect", "gx", "yz", None, None),
        P("sect", "gx", "yz", None),
    )
    out_specs = P("sect", None, "gx", "yz")
    return jax.shard_map(
        per_device, mesh=mesh, in_specs=in_specs, out_specs=out_specs, check_vma=False
    )
```

```python
import functools

import jax
import jax.numpy as jnp
import ml_dtypes
import numpy as np
from jax import lax
from jax.experimental import pallas as pl
from jax.experimental.pallas import tpu as pltpu
from jax.sharding import PartitionSpec as P

MESH = pl.DeviceIdType.MESH
HBM = pltpu.MemorySpace.HBM
F32 = jnp.float32
BF16 = jnp.bfloat16

CX = 8
CY = 16
CZ = 256
NG = 16
NK = 8
NX = 128
NY = 128
SLOTS = 64
GROUPS = ((0, 2), (2, 4), (4, 5))
VMEM_MIB = 62
GX_ORDER = (8, 4, 12, 6, 10, 2, 14, 7, 9, 5, 11, 3, 13, 1, 15)
INLET_ORDER = (4, 3, 5, 2, 6, 1, 7)
DIRECT_FILTER = (2,)

SEGMENT_STEP = 0.25
SIDE_DERIV = 1.0 / 3.0
SIDE_FILTER = 0.49


def filter_coeffs():
    side = SIDE_FILTER
    return [
        (193 + 126 * side) / 256,
        (105 + 302 * side) / 256,
        15 * (-1 + 2 * side) / 64,
        45 * (1 - 2 * side) / 512,
        5 * (-1 + 2 * side) / 256,
        (1 - 2 * side) / 512,
    ]


DERIV_STENCIL = ((1, 7.0 / 9.0), (-1, -7.0 / 9.0), (2, 1.0 / 36.0), (-2, -1.0 / 36.0))
FILTER_STENCIL = ((0, filter_coeffs()[0]),) + tuple(
    (sign * reach, filter_coeffs()[reach] / 2) for reach in range(1, 6) for sign in (1, -1)
)


def sides(length, periodic, stencil, side):
    left = np.eye(length)
    right = np.zeros((length, length))
    for row in range(length):
        for offset, factor in ((-1, side), (1, side)):
            if periodic or 0 <= row + offset < length:
                left[row, (row + offset) % length] += factor
        for offset, factor in stencil:
            if periodic or 0 <= row + offset < length:
                right[row, (row + offset) % length] += factor
    return left, right


def line_matrix(length, periodic, stencil, side):
    return np.linalg.solve(*sides(length, periodic, stencil, side))


def halves(matrix):
    value = np.asarray(matrix, np.float32)
    high = value.astype(ml_dtypes.bfloat16)
    low = (value - high.astype(np.float32)).astype(ml_dtypes.bfloat16)
    return np.stack([high, low])


def block_table(stencil, side):
    left, right = sides(NY, False, stencil, side)
    reach = max(offset for offset, _ in stencil)
    below = np.zeros((NK, NY))
    above = np.zeros((NK, NY))
    corner_low = np.zeros(NK)
    corner_high = np.zeros(NK)
    for d in range(NK):
        lo, hi = d * CY, (d + 1) * CY
        if d > 0:
            row = np.linalg.solve(left[:lo, :lo].T, np.eye(lo)[lo - 1])
            below[d] = -side * (row @ right[:lo])
            corner_low[d] = row[-1]
        if d < NK - 1:
            row = np.linalg.solve(left[hi:, hi:].T, np.eye(NY - hi)[0])
            above[d] = -side * (row @ right[hi:])
            corner_high[d] = row[0]
    send_up = np.zeros((NK, CY))
    send_down = np.zeros((NK, CY))
    for s in range(NK):
        cells = slice(s * CY, (s + 1) * CY)
        if s < NK - 1:
            value = below[min(s + 2, NK - 1)][cells]
            send_up[s] = value / np.abs(value).max()
        if s > 0:
            value = above[max(s - 2, 0)][cells]
            send_down[s] = value / np.abs(value).max()
    take_low = np.zeros((NK, NK))
    take_high = np.zeros((NK, NK))
    near_low = np.zeros((NK, reach))
    near_high = np.zeros((NK, reach))
    own_low = np.zeros((NK, reach))
    own_high = np.zeros((NK, reach))
    for d in range(NK):
        for s in range(d):
            value, unit = below[d][s * CY : (s + 1) * CY], send_up[s]
            core = unit[: CY - reach]
            take_low[d, s] = (value[: CY - reach] @ core) / (core @ core)
            if s == d - 1:
                near_low[d] = (value - take_low[d, s] * unit)[CY - reach :]
        for s in range(d + 1, NK):
            value, unit = above[d][s * CY : (s + 1) * CY], send_down[s]
            core = unit[reach:]
            take_high[d, s] = (value[reach:] @ core) / (core @ core)
            if s == d + 1:
                near_high[d] = (value - take_high[d, s] * unit)[:reach]
        own_low[d] = below[d][d * CY : d * CY + reach]
        own_high[d] = above[d][(d + 1) * CY - reach : (d + 1) * CY]
    lower = np.zeros((NK, CY))
    inverse = np.zeros((NK, CY))
    for d in range(NK):
        diagonal = np.ones(CY)
        diagonal[0] -= side**2 * corner_low[d]
        diagonal[-1] -= side**2 * corner_high[d]
        inverse[d, 0] = 1 / diagonal[0]
        for y in range(1, CY):
            lower[d, y] = side * inverse[d, y - 1]
            inverse[d, y] = 1 / (diagonal[y] - side * lower[d, y])
    has_low = (np.arange(NK) > 0).astype(np.float64)
    has_high = (np.arange(NK) < NK - 1).astype(np.float64)
    parts = dict(
        send_up=send_up, send_down=send_down, take=np.stack([take_low, take_high]), near_low=near_low,
        near_high=near_high, own_low=own_low, own_high=own_high, lower=lower, inverse=inverse,
        has_low=has_low, has_high=has_high,
    )
    places, start = {}, 0
    for name, value in parts.items():
        places[name] = start
        start += value.size
    return np.concatenate([value.reshape(-1) for value in parts.values()]), places


def split(value):
    high = value.astype(BF16)
    low = (value - high.astype(F32)).astype(BF16)
    return high, low


def dot(a, b, dims=((1,), (0,))):
    return lax.dot_general(a, b, (dims, ((), ())), preferred_element_type=F32)


def kernel(
    at_d, at_f,
    fields_hbm, jac_hbm, inflow_hbm, donors_hbm, receptors_hbm, table_hbm, dx_hbm, fx_hbm, dz_hbm, fz_hbm, out,
    fields, jac, inflow, donors, receptors, table, dx, fx, dz, fz, load_sem,
    u0, sel, place, ts, tr, u, pu, v, q, pq, gx_, gz_, pp, ps, sb,
    outlet, inlet, inlet_rows, patch_s, patch_r,
    phi_d, col_d, gam_d, got_d, phi_f, col_f, gam_f, got_f, edge_d, edge_f, planes_f, everyone_f,
    du, pdu, dv, planes_x, everyone_x, edge_x,
    tile_ss, tile_rs, u_ss, u_rs, q_ss, q_rs, s_ss, s_rs,
    d1_ss, d1_rs, d2_ss, d2_rs, f1_ss, f1_rs, f2_ss, f2_rs, dh_ss, dh_rs, fh_ss, fh_rs, in_ss, in_rs, patch_ss, patch_rs,
    du_ss, du_rs, x_ss, x_rs, result, out_ss,
):
    sect = lax.axis_index("sect")
    g = lax.axis_index("gx")
    k = lax.axis_index("yz")

    def along_gx(j):
        return lax.rem(g + j, NG)

    def along_yz(j):
        return lax.rem(k + j, NK)

    def from_yz(j):
        return lax.rem(k + NK - j, NK)

    is_outlet = jnp.logical_and(sect == 0, g == 0)
    is_inlet = jnp.logical_and(sect == 1, g == 0)

    barrier = pltpu.get_barrier_semaphore()

    @pl.loop(1, NG)
    def _(j):
        pl.semaphore_signal(barrier, inc=1, device_id={"gx": along_gx(j)}, device_id_type=MESH)

    @pl.loop(1, NK)
    def _(j):
        pl.semaphore_signal(barrier, inc=1, device_id={"yz": along_yz(j)}, device_id_type=MESH)

    @pl.when(is_inlet)
    def _():
        pl.semaphore_signal(barrier, inc=1, device_id={"sect": 0}, device_id_type=MESH)

    pairs = (
        (fields_hbm, fields), (donors_hbm, donors), (receptors_hbm, receptors), (inflow_hbm, inflow),
        (jac_hbm, jac), (table_hbm, table), (dx_hbm, dx), (dz_hbm, dz), (fz_hbm, fz), (fx_hbm, fx),
    )
    loads = [pltpu.make_async_copy(source, target, load_sem.at[i]) for i, (source, target) in enumerate(pairs)]
    for load in loads:
        load.start()
    loads[0].wait()

    mine = pl.ds(pl.multiple_of(k * CY, CY), CY)

    def inflow_copy():
        return pltpu.make_async_remote_copy(
            outlet, inlet.at[mine], in_ss.at[0], in_rs.at[0], device_id={"sect": 1}, device_id_type=MESH,
        )

    def inlet_copies():
        whole = inlet.at[0 : NY - CY]
        return pltpu.make_async_remote_copy(
            whole, whole, in_ss.at[1], in_rs.at[1], device_id={"yz": along_yz(1)}, device_id_type=MESH,
        )

    @pl.when(is_outlet)
    def _():
        for y in range(CY):
            for f in range(5):
                outlet[y : y + 1, f * CZ : (f + 1) * CZ] = fields[0, f, CX - 1 : CX, y * CZ : (y + 1) * CZ]

        pl.semaphore_wait(barrier, NG + NK - 1)
        inflow_copy().start()

    for y in range(CY):
        for f in range(5):
            u0[y, f] = fields[0, f, :, y * CZ : (y + 1) * CZ]

    @pl.when(is_inlet)
    def _():
        for y in range(CY):
            for f in range(5):
                u0[y, f, 0:1, :] = jnp.zeros((1, CZ), F32)

    offset = lax.broadcasted_iota(jnp.int32, (8, CZ), 1) - lax.broadcasted_iota(jnp.int32, (8, CZ), 0)
    loads[1].wait()

    @pl.loop(0, SLOTS // 2)
    def _(j):
        for b in range(2):
            rows = []
            for e in range(2):
                slot = 2 * j + e
                first = jnp.where(donors[0, 0, 1, 0, slot] == b, donors[0, 0, 2, 0, slot], -1000)
                hit = jnp.logical_or(offset == first, offset == first + 1)
                rows.append(jnp.where(hit, 0.5, 0.0))
            sel[b, pl.ds(pl.multiple_of(16 * j, 16), 16), :] = jnp.concatenate(rows, axis=0).astype(BF16)

    payload = None
    for b in range(2):
        lines = jnp.concatenate([u0[8 * b : 8 * b + 8].reshape(320, CZ), jnp.zeros((64, CZ), F32)], axis=0)
        for part in split(lines):
            term = dot(sel[b], part, ((1,), (1,)))
            payload = term if payload is None else payload + term
    ts[:, 0:32, :] = payload[:, 0:256].reshape(NG, 32, 256)
    rest = payload[:, 256:384].reshape(NG, 4, 8, 128)
    left = lax.broadcasted_iota(jnp.int32, (NG, 8, 128), 2) < 64
    for e in range(2):
        moved = pltpu.roll(rest[:, 2 * e + 1].reshape(NG * 8, 128), 64, 1).reshape(NG, 8, 128)
        ts[:, 32:40, 128 * e : 128 * e + 128] = jnp.where(left, rest[:, 2 * e], moved)

    @pl.when(jnp.logical_not(is_outlet))
    def _():
        pl.semaphore_wait(barrier, NG + NK - 2)

    leaving = []
    coming = {}

    def batch(name, source, target, send, receive):
        whole = pltpu.make_async_remote_copy(
            source, target, send, receive, device_id={"gx": along_gx(1)}, device_id_type=MESH
        )
        leaving.append(whole.wait_send)
        coming[name] = whole.wait_recv

    def arrive(name):
        coming.pop(name)()

    for j in GX_ORDER:
        pltpu.make_async_remote_copy(
            ts.at[along_gx(j)], tr.at[g], tile_ss.at[0], tile_rs.at[0],
            device_id={"gx": along_gx(j)}, device_id_type=MESH,
        ).start()
    batch("tiles", ts.at[1:NG], tr.at[1:NG], tile_ss.at[0], tile_rs.at[0])

    tr[g] = ts[g]

    @pl.when(is_inlet)
    def _():
        inflow_copy().wait_recv()
        for j in INLET_ORDER:
            pltpu.make_async_remote_copy(
                inlet.at[mine], inlet.at[mine], in_ss.at[1], in_rs.at[1],
                device_id={"yz": along_yz(j)}, device_id_type=MESH,
            ).start()

    loads[2].wait()

    def place_row(j, counts):
        counts = list(counts)
        for t in range(2):
            rows = []
            for e in range(2):
                goal = (receptors[2 * j + e] - 32 * t) * 8
                one = jnp.where(offset == goal, 1.0, 0.0)
                counts[t] = counts[t] + one
                rows.append(one)
            place[t, pl.ds(pl.multiple_of(16 * j, 16), 16), :] = jnp.concatenate(rows, axis=0).astype(BF16)
        return tuple(counts)

    counts = lax.fori_loop(0, SLOTS // 2, place_row, (jnp.zeros((8, CZ), F32),) * 2)

    loads[3].wait()

    def patch_copy(j):
        return pltpu.make_async_remote_copy(
            patch_s.at[j], patch_r, patch_ss.at[j], patch_rs.at[0], device_id={"gx": j}, device_id_type=MESH,
        )

    arrive("tiles")

    main = tr[:, 0:32, :].reshape(512, 256)
    rest = []
    for e in range(2):
        two = tr[:, 32:40, 128 * e : 128 * e + 128]
        rest += [two, pltpu.roll(two.reshape(NG * 8, 128), 64, 1).reshape(NG, 8, 128)]
    rest = jnp.stack(rest, axis=1).reshape(512, 128)
    halves_of = [split(main), split(rest)]
    for t in range(2):
        total = jnp.concatenate(
            [
                dot(high, place[t], ((0,), (0,))) + dot(low, place[t], ((0,), (0,)))
                for high, low in halves_of
            ],
            axis=0,
        )
        hits = jnp.sum(counts[t], axis=0, keepdims=True)
        scale = (1.0 / jnp.maximum(hits, 1.0)).reshape(1, 1, 1, CZ)
        mean = total[:320].reshape(8, 5, 8, CZ) * scale
        value = jnp.where(hits.reshape(1, 1, 1, CZ) > 0, mean, u0[8 * t : 8 * t + 8])
        for f in range(5):
            u[f, 8 * t : 8 * t + 8] = value[:, f]

    def start_all(name, source, target, send, receive, lo, hi, at):
        for j in GX_ORDER:
            pltpu.make_async_remote_copy(
                source.at[lo:hi, along_gx(j)], target.at[lo:hi, g], send.at[at], receive.at[at],
                device_id={"gx": along_gx(j)}, device_id_type=MESH,
            ).start()
        batch((name, at), source.at[lo:hi, 1:NG], target.at[lo:hi, 1:NG], send.at[at], receive.at[at])
        target[lo:hi, g] = source[lo:hi, g]

    loads[4].wait()
    loads[5].wait()

    def mix(d, f, h):
        return jac[f, d, h] * (-SEGMENT_STEP)

    @pl.loop(0, CY)
    def _(y):
        cells = [u[h, y] for h in range(5)]
        for f in range(5):
            value = mix(1, f, 0) * cells[0]
            for h in range(1, 5):
                value += mix(1, f, h) * cells[h]
            v[f, y] = value

    def halo(operator, i):
        name, source, edge, reach = operator["name"], operator["source"], operator["edge"], operator["reach"]
        send, receive = operator["halo"]
        lo, hi = GROUPS[i]
        pltpu.make_async_remote_copy(
            source.at[lo:hi, CY - reach : CY], edge.at[lo:hi, 0:reach], send.at[i], receive.at[i],
            device_id={"yz": along_yz(1)}, device_id_type=MESH,
        ).start()
        pltpu.make_async_remote_copy(
            source.at[lo:hi, 0:reach], edge.at[lo:hi, reach : 2 * reach], send.at[i], receive.at[i],
            device_id={"yz": from_yz(1)}, device_id_type=MESH,
        ).start()
        batch((name, "halo", i), source.at[lo:hi, 0 : 2 * reach], edge.at[lo:hi], send.at[i], receive.at[i])

    def hops(name, source, target, sems, i):
        send, receive = sems
        for j in range(1, NK):
            pltpu.make_async_remote_copy(
                source.at[i, along_yz(j)], target.at[i, k], send.at[i], receive.at[i],
                device_id={"yz": along_yz(j)}, device_id_type=MESH,
            ).start()
        batch((name, i), source.at[i, 1:NK], target.at[i, 1:NK], send.at[i], receive.at[i])
        target[i, k] = source[i, k]

    def first_half(operator, i):
        source, phi, places = operator["source"], operator["phi"], operator["places"]
        lo, hi = GROUPS[i]
        direct = i in operator["direct"]
        planes, everyone = operator["planes"], operator["everyone"]
        for f in range(lo, hi if direct else lo + 2):
            for half in range(2):
                tile = (f - lo) * 2 + half
                if f >= hi:
                    phi[i, tile] = jnp.zeros((8, 128), F32)
                    phi[i, 4 + tile] = jnp.zeros((8, 128), F32)
                    continue
                up = down = None
                for y in range(CY):
                    row = source[f, y, :, 128 * half : 128 * half + 128]
                    a = table[places["send_up"] + k * CY + y] * row
                    b = table[places["send_down"] + k * CY + y] * row
                    up, down = (a, b) if up is None else (up + a, down + b)
                if direct:
                    planes[0, f, :, 128 * half : 128 * half + 128] = up
                    planes[1, f, :, 128 * half : 128 * half + 128] = down
                else:
                    phi[i, tile] = up
                    phi[i, 4 + tile] = down

        if direct:
            send, receive = operator["first"]
            for j in range(1, NK):
                peer = along_yz(j)
                pltpu.make_async_remote_copy(
                    planes.at[lax.div(k - peer + NK, NK), lo:hi], everyone.at[k, lo:hi], send.at[i], receive.at[i],
                    device_id={"yz": peer}, device_id_type=MESH,
                ).start()
            whole = everyone.at[1:NK, lo:hi]
            batch((operator["name"] + "2", i), whole, whole, send.at[i], receive.at[i])
            halo(operator, i)
            return

        hops(operator["name"] + "1", phi, operator["col"], operator["first"], i)
        halo(operator, i)

    def second_half(operator, i):
        if i in operator["direct"]:
            return
        col, gam, places = operator["col"], operator["gam"], operator["places"]
        arrive((operator["name"] + "1", i))
        upward = lax.div(k, 4)
        tiles = [col[i, s] for s in range(NK)]

        @pl.loop(0, NK)
        def _(d):
            base = places["take"] + upward * (NK * NK) + d * NK
            total = table[base] * tiles[0]
            for s in range(1, NK):
                total += table[base + s] * tiles[s]
            gam[i, d] = total

        hops(operator["name"] + "2", gam, operator["got"], operator["second"], i)

    def y_lines(operator, i, stencil, side, store):
        source, got, edge, reach, places = (
            operator["source"], operator["got"], operator["edge"], operator["reach"], operator["places"],
        )
        lo, hi = GROUPS[i]
        if operator["name"] == "f":
            arrive(("f", "halo", i))
            arrive(("f2", i))

        def entry(name, count, index=0):
            return table[places[name] + k * count + index]

        for f in range(lo, hi):
            for half in range(2):
                lanes = slice(128 * half, 128 * half + 128)
                tile = (f - lo) * 2 + half
                if i in operator["direct"]:
                    from_low = from_high = None
                    for j in range(1, NK):
                        block = along_yz(j)
                        plane = operator["everyone"][block, f, :, lanes]
                        a = table[places["take"] + k * NK + block] * plane
                        b = table[places["take"] + NK * NK + k * NK + block] * plane
                        from_low, from_high = (a, b) if from_low is None else (from_low + a, from_high + b)
                else:
                    from_low = got[i, tile]
                    from_high = got[i, 4 + tile]
                rows = [edge[f, h, :, lanes] * entry("has_low", 1) for h in range(reach)]
                rows += [source[f, y, :, lanes] for y in range(CY)]
                rows += [edge[f, reach + h, :, lanes] * entry("has_high", 1) for h in range(reach)]
                for h in range(reach):
                    from_low += entry("near_low", reach, h) * rows[h] + entry("own_low", reach, h) * rows[reach + h]
                    from_high += (
                        entry("near_high", reach, h) * rows[reach + CY + h]
                        + entry("own_high", reach, h) * rows[CY + h]
                    )
                moves = {}
                for move, factor in stencil:
                    moves.setdefault(abs(move), {})[move] = factor
                values = []
                for y in range(CY):
                    at = reach + y
                    value = None
                    for move, factors in moves.items():
                        if move == 0:
                            term = np.float32(factors[0]) * rows[at]
                        elif factors[move] == factors[-move]:
                            term = np.float32(factors[move]) * (rows[at + move] + rows[at - move])
                        else:
                            term = np.float32(factors[move]) * (rows[at + move] - rows[at - move])
                        value = term if value is None else value + term
                    if y == 0:
                        value = value + from_low
                    if y == CY - 1:
                        value = value + from_high
                    if y > 0:
                        value = value - entry("lower", CY, y) * values[-1]
                    values.append(value)
                last = None
                for y in range(CY - 1, -1, -1):
                    value = values[y] if last is None else values[y] - np.float32(side) * last
                    last = value * entry("inverse", CY, y)
                    store(y, f, half, last)

    deriv = dict(
        name="d", source=v, phi=phi_d, col=col_d, gam=gam_d, got=got_d, edge=edge_d, reach=2, places=at_d,
        first=(d1_ss, d1_rs), second=(d2_ss, d2_rs), halo=(dh_ss, dh_rs),
        direct=(), planes=None, everyone=None,
    )
    smooth = dict(
        name="f", source=sb, phi=phi_f, col=col_f, gam=gam_f, got=got_f, edge=edge_f, reach=5, places=at_f,
        first=(f1_ss, f1_rs), second=(f2_ss, f2_rs), halo=(fh_ss, fh_rs),
        direct=DIRECT_FILTER, planes=planes_f, everyone=everyone_f,
    )

    def store_q(y, f, half, value):
        q[f, y, :, 128 * half : 128 * half + 128] = value

    def store_out(y, f, half, value):
        start = y * CZ + 128 * half
        result[0, f, :, start : start + 128] = value

    count = len(GROUPS)
    def q_lines(i):
        y_lines(deriv, i, DERIV_STENCIL, SIDE_DERIV, store_q)
        start_all("q", q, pq, q_ss, q_rs, *GROUPS[i], i)

    def send_u():
        for j in GX_ORDER:
            pltpu.make_async_remote_copy(
                u.at[:, along_gx(j)], pu.at[:, g], u_ss.at[0], u_rs.at[0],
                device_id={"gx": along_gx(j)}, device_id_type=MESH,
            ).start()

    batch(("u", 0), u.at[:, 1:NG], pu.at[:, 1:NG], u_ss.at[0], u_rs.at[0])
    pu[:, g] = u[:, g]

    @pl.when(jnp.logical_not(is_inlet))
    def _():
        send_u()

    before = len(leaving)
    for i in range(count):
        first_half(deriv, i)
    early = len(leaving)

    @pl.when(is_inlet)
    def _():
        inlet_rows[...] = jnp.zeros((2, 64, CZ), F32)
        inlet_copies().wait_recv()
        for y in range(CY):
            row = inlet[pl.ds(inflow[y], 1), :]
            for f in range(5):
                at = (y % 8) * 8 + f
                inlet_rows[y // 8, at : at + 1, :] = row[:, f * CZ : (f + 1) * CZ]
        total = None
        for b in range(2):
            lines = jnp.concatenate([inlet_rows[b], jnp.zeros((64, CZ), F32)], axis=0)
            for part in split(lines):
                term = dot(sel[b], part, ((1,), (1,)))
                total = term if total is None else total + term
        total = total.reshape(NG, 2, 16, 128)
        moved = pltpu.roll(total[:, 1].reshape(NG * 16, 128), 64, 1).reshape(NG, 16, 128)
        side = lax.broadcasted_iota(jnp.int32, (NG, 16, 128), 2) < 64
        patch_s[...] = jnp.where(side, total[:, 0], moved)

        @pl.loop(1, NG)
        def _(j):
            patch_copy(j).start()

        patch_r[...] = patch_s[0]

    @pl.when(is_inlet)
    def _():
        send_u()

    for i in range(count):
        second_half(deriv, i)
    def plane_copy(j):
        return pltpu.make_async_remote_copy(
            du.at[along_gx(j)], pdu.at[g], du_ss.at[0], du_rs.at[0],
            device_id={"gx": along_gx(j)}, device_id_type=MESH,
        )

    def plane_copies():
        return pltpu.make_async_remote_copy(
            du.at[1:NG], pdu.at[1:NG], du_ss.at[0], du_rs.at[0], device_id={"gx": along_gx(1)}, device_id_type=MESH,
        )

    @pl.when(sect == 1)
    def _():
        @pl.when(g > 0)
        def _():
            patch_copy(g).wait_recv()

        packed = patch_r[...]
        high, low = split(jnp.concatenate([packed, pltpu.roll(packed, 64, 1)], axis=0))
        for t in range(2):
            rows = place[t, 0:32, :]
            total = dot(high, rows, ((0,), (0,))) + dot(low, rows, ((0,), (0,)))
            hits = jnp.sum(counts[t], axis=0, keepdims=True)
            value = (total[:64] * (1.0 / jnp.maximum(hits, 1.0))).reshape(8, 8, CZ)
            du[8 * t : 8 * t + 8] = value

            @pl.when(g == 0)
            def _():
                taken = hits.reshape(1, 1, CZ) > 0
                du[8 * t : 8 * t + 8] = jnp.where(taken, value, inlet_rows[t].reshape(8, 8, CZ))

        row_of = lax.broadcasted_iota(jnp.int32, (8, CZ), 0)
        factors = []
        for h in range(5):
            factor = jnp.zeros((8, CZ), F32)
            for f in range(5):
                factor = jnp.where(row_of == f, mix(1, f, h), factor)
            factors.append(factor)
        for y in range(CY):
            value = factors[0] * du[y, 0:1, :]
            for h in range(1, 5):
                value += factors[h] * du[y, h : h + 1, :]
            dv[y] = value
        up = down = None
        for y in range(CY):
            a = table[at_d["send_up"] + k * CY + y] * dv[y]
            b = table[at_d["send_down"] + k * CY + y] * dv[y]
            up, down = (a, b) if up is None else (up + a, down + b)
        planes_x[0] = up
        planes_x[1] = down
        for j in range(1, NK):
            peer = along_yz(j)
            pltpu.make_async_remote_copy(
                planes_x.at[lax.div(k - peer + NK, NK)], everyone_x.at[k], x_ss.at[0], x_rs.at[0],
                device_id={"yz": peer}, device_id_type=MESH,
            ).start()
        pltpu.make_async_remote_copy(
            dv.at[CY - 2 : CY], edge_x.at[0:2], x_ss.at[1], x_rs.at[1],
            device_id={"yz": along_yz(1)}, device_id_type=MESH,
        ).start()
        pltpu.make_async_remote_copy(
            dv.at[0:2], edge_x.at[2:4], x_ss.at[1], x_rs.at[1],
            device_id={"yz": from_yz(1)}, device_id_type=MESH,
        ).start()

    def extra_copies():
        return [
            pltpu.make_async_remote_copy(
                whole, whole, x_ss.at[i], x_rs.at[i], device_id={"yz": along_yz(1)}, device_id_type=MESH,
            )
            for i, whole in enumerate((everyone_x.at[1:NK], edge_x))
        ]

    for wait in leaving[before:early]:
        wait()
    del leaving[before:early]

    for i in range(count):
        arrive(("d", "halo", i))
        arrive(("d2", i))

    @pl.when(sect == 1)
    def _():
        @pl.loop(1, NG)
        def _(j):
            plane_copy(j).start()

        pdu[g] = du[g]
        for y in range(CY):
            for f in range(5):
                v[f, y, 0:1, :] = v[f, y, 0:1, :] + dv[y, f : f + 1, :]
        for copy in extra_copies():
            copy.wait_recv()
        for f in range(5):
            for h in range(4):
                edge_d[f, h, 0:1, :] = edge_d[f, h, 0:1, :] + edge_x[h, f : f + 1, :]
        from_low = from_high = None
        for j in range(1, NK):
            block = along_yz(j)
            plane = everyone_x[block]
            a = table[at_d["take"] + k * NK + block] * plane
            b = table[at_d["take"] + NK * NK + k * NK + block] * plane
            from_low, from_high = (a, b) if from_low is None else (from_low + a, from_high + b)
        for i, (lo, hi) in enumerate(GROUPS):
            for f in range(lo, hi):
                for half in range(2):
                    tile = (f - lo) * 2 + half
                    lanes = slice(128 * half, 128 * half + 128)
                    got_d[i, tile, 0:1, :] = got_d[i, tile, 0:1, :] + from_low[f : f + 1, lanes]
                    got_d[i, 4 + tile, 0:1, :] = got_d[i, 4 + tile, 0:1, :] + from_high[f : f + 1, lanes]

    for i in range(count):
        q_lines(i)

    for load in loads[6:]:
        load.wait()
    arrive(("u", 0))

    @pl.when(sect == 1)
    def _():
        plane_copies().wait_recv()

        @pl.loop(0, NG)
        def _(r):
            for f in range(5):
                pu[f, r, 0:1, :] = pu[f, r, 0:1, :] + pdu[r, f : f + 1, :]

    for f in range(5):
        high, low = split(pu[f].reshape(NX, CZ))
        gx_[f] = dot(dx[sect, 0], high) + dot(dx[sect, 0], low) + dot(dx[sect, 1], high)
        gz_[f] = dot(high, dz[0]) + dot(low, dz[0]) + dot(high, dz[1])

    @pl.loop(0, 5)
    def _(f):
        value = pu[f].reshape(NX, CZ)
        for h in range(5):
            value += mix(0, f, h) * gx_[h]
            value += mix(2, f, h) * gz_[h]
        pp[f] = value

    for i in range(count):
        lo, hi = GROUPS[i]
        arrive(("q", i))
        for f in range(lo, hi):
            high, low = split(pp[f] + pq[f].reshape(NX, CZ))
            value = dot(high, fz[0]) + dot(low, fz[0]) + dot(high, fz[1])
            high, low = split(value)
            value = dot(fx[sect, 0], high) + dot(fx[sect, 0], low) + dot(fx[sect, 1], high)
            ps[f] = value.reshape(NG, CX, CZ)
        start_all("s", ps, sb, s_ss, s_rs, lo, hi, i)

    for i in range(count):
        arrive(("s", i))
        first_half(smooth, i)
        if i > 0:
            second_half(smooth, i - 1)
    for i in range(count):
        y_lines(smooth, i, FILTER_STENCIL, SIDE_FILTER, store_out)
        lo, hi = GROUPS[i]
        write = pltpu.make_async_copy(result.at[:, lo:hi], out.at[:, lo:hi], out_ss.at[i])
        write.start()
        leaving.append(write.wait)

    for wait in leaving:
        wait()

    @pl.when(sect == 1)
    def _():
        plane_copies().wait_send()
        for copy in extra_copies():
            copy.wait_send()

    @pl.when(is_outlet)
    def _():
        inflow_copy().wait_send()

    @pl.when(is_inlet)
    def _():
        inlet_copies().wait_send()

        @pl.loop(1, NG)
        def _(j):
            patch_copy(j).wait_send()


def per_device(fields, jacobians, inflow_map, donor_tiles, receptor_tiles):
    table_d, places_d = block_table(DERIV_STENCIL, SIDE_DERIV)
    table_f, places_f = block_table(FILTER_STENCIL, SIDE_FILTER)
    places_f = {name: start + table_d.size for name, start in places_f.items()}
    table = np.concatenate([table_d, table_f]).astype(np.float32)
    dx = np.stack([halves(line_matrix(NX, p, DERIV_STENCIL, SIDE_DERIV)) for p in (True, False)])
    fx = np.stack([halves(line_matrix(NX, p, FILTER_STENCIL, SIDE_FILTER)) for p in (True, False)])
    dz = halves(line_matrix(CZ, True, DERIV_STENCIL, SIDE_DERIV).T)
    fz = halves(line_matrix(CZ, True, FILTER_STENCIL, SIDE_FILTER).T)
    block = (5, CY, CX, CZ)
    count = len(GROUPS)

    def buffer(*shape, kind=F32):
        return pltpu.VMEM(shape, kind)

    def scalars(*shape, kind=jnp.int32):
        return pltpu.SMEM(shape, kind)

    def dma(length):
        return pltpu.SemaphoreType.DMA((length,))

    tiles = [buffer(count, NK, 8, 128)] * 4
    inputs = (
        fields, jnp.transpose(jacobians, (1, 0, 2)), inflow_map, jnp.transpose(donor_tiles, (0, 1, 4, 2, 3)),
        receptor_tiles.reshape(SLOTS), jnp.asarray(table), jnp.asarray(dx), jnp.asarray(fx), jnp.asarray(dz),
        jnp.asarray(fz),
    )
    return pl.pallas_call(
        functools.partial(kernel, places_d, places_f),
        out_shape=jax.ShapeDtypeStruct(fields.shape, F32),
        in_specs=[pl.BlockSpec(memory_space=HBM)] * len(inputs),
        out_specs=pl.BlockSpec(memory_space=HBM),
        scratch_shapes=[
            buffer(*fields.shape), scalars(5, 3, 5, kind=F32), scalars(16), scalars(1, 1, 3, 1, SLOTS), scalars(SLOTS),
            scalars(table.size, kind=F32),
            buffer(*dx.shape, kind=BF16), buffer(*fx.shape, kind=BF16),
            buffer(*dz.shape, kind=BF16), buffer(*fz.shape, kind=BF16), dma(10),
            buffer(CY, 5, CX, CZ),
            buffer(2, 512, CZ, kind=BF16), buffer(2, 512, CZ, kind=BF16),
            buffer(NG, 40, 256), buffer(NG, 40, 256),
            buffer(*block), buffer(*block), buffer(*block), buffer(*block), buffer(*block),
            buffer(5, NX, CZ), buffer(5, NX, CZ), buffer(5, NX, CZ),
            buffer(*block), buffer(*block),
            buffer(CY, 5 * CZ), buffer(NY, 5 * CZ), buffer(2, 64, CZ), buffer(NG, 16, 128), buffer(16, 128),
            *tiles, *tiles,
            buffer(5, 4, CX, CZ), buffer(5, 10, CX, CZ),
            buffer(2, 5, CX, CZ), buffer(NK, 5, CX, CZ),
            buffer(CY, 8, CZ), buffer(NG, 8, CZ), buffer(CY, 8, CZ), buffer(2, 8, CZ), buffer(NK, 8, CZ), buffer(4, 8, CZ),
            *([dma(1)] * 4), *([dma(count)] * 16), dma(2), dma(2), dma(NG), dma(1), dma(1), dma(1), dma(2), dma(2), buffer(*fields.shape), dma(count),
        ],
        compiler_params=pltpu.CompilerParams(
            collective_id=0, has_side_effects=True, vmem_limit_bytes=VMEM_MIB * 1024 * 1024
        ),
        name="segment",
    )(*inputs)


def solution(mesh):
    in_specs = (
        P("sect", None, "gx", "yz"),
        P(),
        P("yz"),
        P("sect", "gx", "yz", None, None),
        P("sect", "gx", "yz", None),
    )
    out_specs = P("sect", None, "gx", "yz")
    return jax.shard_map(
        per_device, mesh=mesh, in_specs=in_specs, out_specs=out_specs, check_vma=False
    )
```
